256 devices in a mesh: lat: 16 (over z, x_lo), lon: 16 (over x_hi, y, core).
Axes of the slice: x: 4 (x_hi: 2, x_lo: 2; x = x_hi * 2 + x_lo), y: 4, z: 8, core: 2. Of those that a mesh axis runs over, the one named last changes fastest.
Arguments:
- state: bfloat16 [64, 128, 64, 128], P('lat', 'lon'), may hold values from -6 to 6
- obs_row: int32 [64, 128, 128], P('lat', 'lon'), may hold values from 0 to 63
- obs_count: int32 [64, 128], P('lat', 'lon'), may hold values from 0 to 128
- obs_value: float32 [64, 128, 128], P('lat', 'lon'), may hold values from -6 to 6
- obs_weight: float32 [64, 128, 128], P('lat', 'lon'), may hold values from 0.5 to 2
- quadrant: int32 [64, 128, 64], P('lat', 'lon'), may hold values from 0 to 3
- frac_lat: float32 [64, 128, 64], P('lat', 'lon'), may hold values from 0 to 1
- frac_lon: float32 [64, 128, 64], P('lat', 'lon'), may hold values from 0 to 1
- land: int32 [64, 128, 64], P('lat', 'lon'), may hold values 0 or 1
Outputs:
- analysis: bfloat16 [64, 128, 64, 128], P('lat', 'lon')
The draws below stay inside these ranges and needn't reach their ends.
All inputs are finite; a program needn't handle non-finite values. No bound on the sum of `land` on one device may be relied on, other than what follows from the above.
Results may differ from the reference program's by a relative error of at most 0.0051.
Values may be sent and summed in bfloat16 or wider, within the bound.
No kernel may reach another device: no remote copies, remote signals or barrier semaphores. Data moves between devices by JAX's collectives and lax.ppermute only.
A program may use at most 64 MiB of HBM per device.

```python
import math
import jax
import jax.numpy as jnp
from jax import lax

M = 128
OBS = 128
RC = 64
ITERS = 6
NLAT = 64
NLON = 128


def touch_ends(values, own_key, low, largest):
    dims = values.shape
    place = [jax.random.randint(jax.random.fold_in(own_key, axis), (), 0, dims[axis]) for axis in range(len(dims))]
    values = values.at[tuple(place)].set(low)
    longest = dims.index(max(dims))
    place[longest] = (place[longest] + 1) % dims[longest]
    return values.at[tuple(place)].set(largest)


def block_levels(rng, extent, cuts, low, top_value):
    def one(position, shards_of):
        steps = jax.random.uniform(jax.random.fold_in(jax.random.fold_in(rng, 6), position), (shards_of,), jnp.float32, low / len(cuts), top_value / len(cuts))
        return jnp.repeat(jnp.exp(steps), extent[position] // shards_of).reshape((-1,) + (1,) * (len(extent) - position - 1))

    level = one(*cuts[0])
    for cut in cuts[1:]:
        level = level * one(*cut)
    return level


def gaussian(rng, shape, spread, bound, shards=(), kind=jnp.bfloat16):
    level = block_levels(rng, shape, shards, -0.22, 0.18) if shards else 1.0
    values = jax.random.normal(rng, shape, jnp.float32) * spread * level
    return jnp.minimum(jnp.maximum(values, -bound), bound).astype(kind)


def setup_inputs(seed: int = 0) -> dict:
    keys = jax.random.split(jax.random.key(seed), 10)
    return {
        "state": gaussian(keys[0], (NLAT, NLON, RC, M), 1.0, 6.0, ((0, 16), (1, 16))),
        "obs_row": touch_ends(jax.random.randint(keys[1], (NLAT, NLON, OBS), 0, RC), jax.random.fold_in(keys[1], 1), 0, RC - 1).astype(jnp.int32),
        "obs_count": touch_ends(jax.random.randint(keys[2], (NLAT, NLON), 0, OBS + 1), jax.random.fold_in(keys[2], 1), 0, OBS).astype(jnp.int32),
        "obs_value": gaussian(keys[3], (NLAT, NLON, OBS), 1.0, 6.0, ((0, 16), (1, 16)), jnp.float32),
        "obs_weight": jnp.clip(jnp.exp(math.log(2.0) - 1.3862944 * jax.random.uniform(keys[4], (NLAT, NLON, OBS), jnp.float32) ** block_levels(keys[4], (NLAT, NLON, OBS), ((0, 16), (1, 16)), -0.2, 0.2)), 0.5, 2.0),
        "quadrant": touch_ends(jax.random.randint(keys[5], (NLAT, NLON, RC), 0, 4), jax.random.fold_in(keys[5], 1), 0, 3).astype(jnp.int32),
        "frac_lat": jnp.clip(1.0 * jax.random.uniform(keys[6], (NLAT, NLON, RC), jnp.float32) ** block_levels(keys[6], (NLAT, NLON, RC), ((0, 16), (1, 16)), -0.2, 0.2), 0.0, 1.0),
        "frac_lon": jnp.clip(1.0 * jax.random.uniform(keys[7], (NLAT, NLON, RC), jnp.float32) ** block_levels(keys[7], (NLAT, NLON, RC), ((0, 16), (1, 16)), -0.2, 0.2), 0.0, 1.0),
        "land": touch_ends((jax.random.randint(keys[8], (NLAT, NLON, RC), 0, 4) < 3).astype(jnp.int32), jax.random.fold_in(keys[8], 1), 0, 1),
    }


HIGHEST = lax.Precision.HIGHEST
NEAR_WEIGHTS = (0.5, 1.0, 0.5)

def node_terms(cells, member_mean, obs_rows, counts, observed, weight):
    picked = jnp.take_along_axis(cells, obs_rows[..., None], axis=-2).astype(jnp.float32)
    centre = jnp.take_along_axis(member_mean, obs_rows, axis=-1)
    slot_ids = lax.broadcasted_iota(jnp.int32, obs_rows.shape, obs_rows.ndim - 1)
    live_weight = jnp.where(slot_ids < counts[..., None], weight, jnp.float32(0.0))
    blocks = ((picked - centre[..., None]) * live_weight[..., None]).astype(jnp.bfloat16)
    innovation = ((observed - centre) * live_weight).astype(jnp.bfloat16)
    return (blocks, innovation)

def gram_terms(blocks, innovation):
    wide_blocks = blocks.astype(jnp.float32)
    node_grams = jnp.einsum('...sm,...sn->...mn', wide_blocks, wide_blocks)
    node_sides = jnp.einsum('...sm,...s->...m', wide_blocks, innovation.astype(jnp.float32))
    return (node_grams, node_sides)

def transform_weights(gram_sum, side_sum, members):
    identity = jnp.eye(members, dtype=jnp.float32)
    frob_norm = jnp.sqrt(lax.optimization_barrier(jnp.sum(gram_sum * gram_sum, axis=(-2, -1))))
    iterate = gram_sum / frob_norm[..., None, None]
    inv_root = jnp.broadcast_to(identity, gram_sum.shape)
    for newton_step in range(ITERS):
        factor = 1.5 * identity - 0.5 * jnp.einsum('...ab,...bc->...ac', inv_root, iterate, precision=HIGHEST)
        iterate = jnp.einsum('...ab,...bc->...ac', iterate, factor, precision=HIGHEST)
        inv_root = jnp.einsum('...ab,...bc->...ac', factor, inv_root, precision=HIGHEST)
    inner_term = jnp.einsum('...ab,...b->...a', inv_root, side_sum, precision=HIGHEST)
    mean_weight = jnp.einsum('...ab,...b->...a', inv_root, inner_term, precision=HIGHEST) / frob_norm[..., None]
    spread_part = math.sqrt(members - 1) * inv_root / jnp.sqrt(frob_norm)[..., None, None]
    return (mean_weight[..., :, None] + spread_part).astype(jnp.bfloat16)

def reference(state, obs_row, obs_count, obs_value, obs_weight, quadrant, frac_lat, frac_lon, land):
    members = state.shape[3]
    row_ids = jnp.arange(NLAT, dtype=jnp.int32)

    def pick(array, row_index):
        return lax.dynamic_index_in_dim(array, row_index, 0, keepdims=False)

    def terms_row(row_index):
        cells = pick(state, row_index)
        member_mean = lax.optimization_barrier(jnp.mean(cells.astype(jnp.float32), axis=-1))
        return node_terms(cells, member_mean, pick(obs_row, row_index), pick(obs_count, row_index), pick(obs_value, row_index), pick(obs_weight, row_index))
    blocks, innovation = lax.map(terms_row, row_ids)
    padded_blocks = jnp.pad(blocks, ((1, 1), (0, 0), (0, 0), (0, 0)))
    padded_innov = jnp.pad(innovation, ((1, 1), (0, 0), (0, 0)))

    def weight_row(row_index):
        near_blocks = lax.dynamic_slice_in_dim(padded_blocks, row_index, 3, 0)
        near_innov = lax.dynamic_slice_in_dim(padded_innov, row_index, 3, 0)
        node_grams, node_sides = gram_terms(near_blocks, near_innov)
        identity = jnp.eye(members, dtype=jnp.float32)
        gram_sum = jnp.zeros((NLON, members, members), jnp.float32) + (members - 1) * identity
        side_sum = jnp.zeros((NLON, members), jnp.float32)
        for lat_off in range(3):
            for lon_off in range(3):
                factor = NEAR_WEIGHTS[lat_off] * NEAR_WEIGHTS[lon_off]
                gram_sum = gram_sum + factor * jnp.roll(node_grams[lat_off], 1 - lon_off, axis=0)
                side_sum = side_sum + factor * jnp.roll(node_sides[lat_off], 1 - lon_off, axis=0)
        return transform_weights(gram_sum, side_sum, members)
    weights = lax.map(weight_row, row_ids)
    padded_weights = jnp.pad(weights, ((1, 1), (0, 0), (0, 0), (0, 0)))

    def analysis_row(row_index):
        near_weights = lax.dynamic_slice_in_dim(padded_weights, row_index, 3, 0)
        cells = pick(state, row_index)
        values = cells.astype(jnp.float32)
        member_mean = lax.optimization_barrier(jnp.mean(values, axis=-1))
        perturb = (values - member_mean[..., None]).astype(jnp.bfloat16)
        corner_ids = pick(quadrant, row_index)
        lat_half = corner_ids // 2
        lon_half = corner_ids % 2
        lat_frac = pick(frac_lat, row_index)
        lon_frac = pick(frac_lon, row_index)
        accumulated = jnp.zeros(values.shape, jnp.float32)
        for lat_off in range(3):
            along_lat = jnp.where(lat_half == lat_off, 1.0 - lat_frac, 0.0) + jnp.where(lat_half + 1 == lat_off, lat_frac, 0.0)
            for lon_off in range(3):
                along_lon = jnp.where(lon_half == lon_off, 1.0 - lon_frac, 0.0) + jnp.where(lon_half + 1 == lon_off, lon_frac, 0.0)
                shifted = jnp.roll(near_weights[lat_off], 1 - lon_off, axis=0)
                product = jnp.einsum('jrm,jmn->jrn', perturb.astype(jnp.float32), shifted.astype(jnp.float32))
                accumulated = accumulated + (along_lat * along_lon)[..., None] * product
        land_row = pick(land, row_index)
        result = jnp.where(land_row[..., None] == 1, member_mean[..., None] + accumulated, values)
        return result.astype(jnp.bfloat16)
    return lax.map(analysis_row, row_ids)
```

```python
import math

import jax
import jax.numpy as jnp
from jax import lax
from jax.experimental import pallas as pl
from jax.experimental.pallas import tpu as pltpu
from jax.sharding import PartitionSpec as P

F32 = jnp.float32
BF16 = jnp.bfloat16
ITERS = 6
NEAR = (0.5, 1.0, 0.5)
PARAMS = pltpu.CompilerParams(vmem_limit_bytes=40 * 2**20)


def swap_pairs(count, phase):
    pairs = []
    for k in range(phase, count, 2):
        a, b = k, (k + 1) % count
        pairs += [(a, b), (b, a)]
    return pairs


def swap(x, axis, phase):
    return lax.ppermute(x, axis, swap_pairs(lax.axis_size(axis), phase))


def split(x):
    high = x.astype(BF16)
    return high, (x - high.astype(F32)).astype(BF16)


def stream(pair):
    return jnp.concatenate(pair, axis=1)


def held(pair):
    row = jnp.concatenate(pair, axis=1)
    return jnp.concatenate([row, row], axis=0)


def product(a, b):
    out = jnp.dot(stream(a), held(b), preferred_element_type=F32)
    half = out.shape[1] // 2
    return out[:, :half] + out[:, half:]


def weights_of(grams, sides):
    members = grams[0].shape[0]
    rows = lax.broadcasted_iota(jnp.int32, (members, members), 0)
    cols = lax.broadcasted_iota(jnp.int32, (members, members), 1)
    eye = jnp.where(rows == cols, F32(1.0), F32(0.0))
    inv_frob = []
    iterates = []
    for gram in grams:
        total = jnp.sum(jnp.sum(gram * gram, axis=0, keepdims=True), axis=1, keepdims=True)
        inverse = lax.rsqrt(total)
        inv_frob.append(inverse)
        iterates.append(gram * inverse)
    factors = [1.5 * eye - 0.5 * a for a in iterates]
    roots = factors
    root_parts = [split(t) for t in factors]
    iterates = [product(split(a), t) for a, t in zip(iterates, root_parts)]
    for step in range(1, ITERS):
        iterate_parts = [split(y) for y in iterates]
        factors = [
            1.5 * eye - 0.5 * product(z, y) for z, y in zip(root_parts, iterate_parts)
        ]
        factor_parts = [split(t) for t in factors]
        if step < ITERS - 1:
            iterates = [product(y, t) for y, t in zip(iterate_parts, factor_parts)]
        roots = [product(t, z) for t, z in zip(factor_parts, root_parts)]
        if step < ITERS - 1:
            root_parts = [split(z) for z in roots]
    out = []
    for root, side, inverse in zip(roots, sides, inv_frob):
        inner = jnp.sum(root * side, axis=1, keepdims=True)
        mean_weight = jnp.sum(root * inner, axis=0, keepdims=True) * inverse
        out.append((mean_weight + (math.sqrt(members - 1) * jnp.sqrt(inverse)) * root).astype(BF16))
    return out


def row_gram(cells):
    _, rows, members = cells.shape
    left = jnp.concatenate([cells[b] * BF16(NEAR[b]) for b in range(3)], axis=0)
    right = cells.reshape(3 * rows, members)
    return lax.dot_general(left, right, (((0,), (0,)), ((), ())), preferred_element_type=F32)


def identity(members):
    rows = lax.broadcasted_iota(jnp.int32, (members, members), 0)
    cols = lax.broadcasted_iota(jnp.int32, (members, members), 1)
    return jnp.where(rows == cols, F32(members - 1), F32(0.0))


def prepare(lat_size):
    def kernel(count_ref, state_ref, row_ref, value_ref, weight_ref, q_ref, side_ref, a_ref, b_ref):
        tile_lat, tile_lon, rows, members = state_ref.shape
        slots = row_ref.shape[2]
        lane = lax.broadcasted_iota(jnp.int32, (1, slots), 1)
        row_ids = lax.broadcasted_iota(jnp.int32, (rows, slots), 0)

        def body(i, carry):
            for j in range(tile_lon):
                x = state_ref[i, j].astype(F32)
                mean = jnp.sum(x, axis=1, keepdims=True) * (1.0 / members)
                centred = x - mean
                live = jnp.where(lane < count_ref[i, j], weight_ref[i, j : j + 1, :], 0.0)
                hit = row_ids == row_ref[i, j : j + 1, :]
                centre = jnp.sum(jnp.where(hit, mean, 0.0), axis=0, keepdims=True)
                innovation = ((value_ref[i, j : j + 1, :] - centre) * live).astype(BF16).astype(F32)
                square = jnp.sum(jnp.where(hit, live * live, 0.0), axis=1, keepdims=True)
                pull = jnp.sum(jnp.where(hit, live * innovation, 0.0), axis=1, keepdims=True)
                start = pl.multiple_of((i * tile_lon + j) * rows, rows)
                q_ref[pl.ds(start, rows), :] = (centred * jnp.sqrt(square)).astype(BF16)
                side_ref[pl.ds(i * tile_lon + j, 1), :] = jnp.sum(
                    centred * pull, axis=0, keepdims=True
                )
            return carry

        lax.fori_loop(0, tile_lat, body, 0)
        odd = lax.rem(lax.axis_index("lat"), 2)
        half = tile_lat // 2 * tile_lon
        for ref, first in ((a_ref, 1 - odd), (b_ref, odd)):
            ref[: half * rows, :] = q_ref[pl.ds(pl.multiple_of(first * half * rows, half * rows), half * rows), :]
            high, low = split(side_ref[pl.ds(pl.multiple_of(first * half, half), half), :])
            ref[half * rows : half * rows + half, :] = high
            ref[half * rows + half : half * rows + 2 * half, :] = low

    def call(state, obs_row, obs_count, obs_value, obs_weight):
        tile_lat, tile_lon, rows, members = state.shape
        cells = tile_lat * tile_lon
        payload = cells // 2 * rows + cells
        vmem = pl.BlockSpec(memory_space=pltpu.VMEM)
        return pl.pallas_call(
            kernel,
            in_specs=[pl.BlockSpec(memory_space=pltpu.SMEM)] + [vmem] * 4,
            out_specs=[vmem] * 4,
            out_shape=[
                jax.ShapeDtypeStruct((cells * rows, members), BF16),
                jax.ShapeDtypeStruct((cells, members), F32),
                jax.ShapeDtypeStruct((payload, members), BF16),
                jax.ShapeDtypeStruct((payload, members), BF16),
            ],
            compiler_params=PARAMS,
            cost_estimate=pl.CostEstimate(flops=10**8, bytes_accessed=2 * 10**6, transcendentals=0),
            name="prepare",
        )(obs_count, state, obs_row, obs_value, obs_weight)

    return call


def interior(q, side):
    tile_lat, tile_lon, rows, members = q.shape

    def kernel(q_ref, side_ref, out_ref, gram_ref):
        def grams(i, carry):
            for j in range(tile_lon - 2):
                gram_ref[i, j] = row_gram(q_ref[i, j : j + 3])
            return carry

        lax.fori_loop(0, tile_lat, grams, 0)
        base = identity(members)

        def body(i, carry):
            gram_sums, sides = [], []
            for j in range(tile_lon - 2):
                gram_sums.append(
                    base + 0.5 * (gram_ref[i, j] + gram_ref[i + 2, j]) + gram_ref[i + 1, j]
                )
                total = 0.0
                for a in range(3):
                    for b in range(3):
                        total = total + NEAR[a] * NEAR[b] * side_ref[i + a, j + b : j + b + 1, :]
                sides.append(total)
            for j, w in enumerate(weights_of(gram_sums, sides)):
                out_ref[i, j] = w
            return carry

        lax.fori_loop(0, tile_lat - 2, body, 0)

    vmem = pl.BlockSpec(memory_space=pltpu.VMEM)
    return pl.pallas_call(
        kernel,
        in_specs=[vmem] * 2,
        out_specs=vmem,
        out_shape=jax.ShapeDtypeStruct((tile_lat - 2, tile_lon - 2, members, members), BF16),
        scratch_shapes=[pltpu.VMEM((tile_lat, tile_lon - 2, members, members), F32)],
        compiler_params=PARAMS,
        cost_estimate=pl.CostEstimate(flops=5 * 10**9, bytes_accessed=2 * 10**6, transcendentals=0),
        name="interior",
    )(q, side)


def widen(q, side, got_a, got_b):
    tile_lat, tile_lon, rows, members = q.shape
    half = 2 * tile_lon
    wide = tile_lat + 4
    count = 2 * wide
    payload = count * rows + 2 * count

    def kernel(q_ref, side_ref, a_ref, b_ref, wide_ref, wide_side_ref, to_a_ref, to_b_ref):
        lat = lax.axis_index("lat")
        lon = lax.axis_index("lon")
        lat_odd = lax.rem(lat, 2)
        lon_odd = lax.rem(lon, 2)
        wide_ref[2 : 2 + tile_lat] = q_ref[...]
        wide_side_ref[2 : 2 + tile_lat] = side_ref[...]
        last = lax.axis_size("lat") - 1
        a_valid = jnp.where(lat_odd == 0, lat < last, lat > 0)
        b_valid = jnp.where(lat_odd == 0, lat > 0, lat < last)
        for ref, first, valid in (
            (a_ref, (1 - lat_odd) * (tile_lat + 2), a_valid),
            (b_ref, lat_odd * (tile_lat + 2), b_valid),
        ):
            for i in range(2):
                for j in range(tile_lon):
                    k = (i * tile_lon + j) * rows
                    piece = ref[k : k + rows, :]
                    wide_ref[first + i, j] = jnp.where(valid, piece, jnp.zeros_like(piece))
            base = half * rows
            total = ref[base : base + half, :].astype(F32) + ref[base + half : base + 2 * half, :].astype(F32)
            total = jnp.where(valid, total, 0.0)
            wide_side_ref[first] = total[:tile_lon]
            wide_side_ref[first + 1] = total[tile_lon:]
        for ref, first in ((to_a_ref, (1 - lon_odd) * (tile_lon - 2)), (to_b_ref, lon_odd * (tile_lon - 2))):
            collected = []
            for i in range(wide):
                for j in range(2):
                    k = (i * 2 + j) * rows
                    ref[k : k + rows, :] = wide_ref[i, first + j]
                    collected.append(wide_side_ref[i, pl.ds(first + j, 1), :])
            high, low = split(jnp.concatenate(collected, axis=0))
            base = count * rows
            ref[base : base + count, :] = high
            ref[base + count : base + 2 * count, :] = low

    vmem = pl.BlockSpec(memory_space=pltpu.VMEM)
    return pl.pallas_call(
        kernel,
        in_specs=[vmem] * 4,
        out_specs=[vmem] * 4,
        out_shape=[
            jax.ShapeDtypeStruct((wide, tile_lon, rows, members), BF16),
            jax.ShapeDtypeStruct((wide, tile_lon, members), F32),
            jax.ShapeDtypeStruct((payload, members), BF16),
            jax.ShapeDtypeStruct((payload, members), BF16),
        ],
        compiler_params=PARAMS,
        cost_estimate=pl.CostEstimate(flops=10**6, bytes_accessed=3 * 10**6, transcendentals=0),
        name="widen",
    )(q, side, got_a, got_b)


def node_valid(row):
    lat = lax.axis_index("lat")
    return lat, row


def middle(wide_q, wide_side):
    wide, tile_lon, rows, members = wide_q.shape
    tile_lat = wide - 4

    def kernel(q_ref, side_ref, out_ref, gram_ref):
        def grams(i, carry):
            for j in range(tile_lon - 2):
                gram_ref[i, j] = row_gram(q_ref[i, j : j + 3])
            return carry

        lax.fori_loop(0, wide, grams, 0)
        base = identity(members)
        lat = lax.axis_index("lat")
        last = lax.axis_size("lat") - 1

        def body(g, carry):
            i = jnp.where(g < 2, g, g + tile_lat - 2)
            outside = jnp.logical_or(
                jnp.logical_and(i == 0, lat == 0), jnp.logical_and(i == tile_lat + 1, lat == last)
            )
            gram_sums, sides = [], []
            for j in range(tile_lon - 2):
                gram_sums.append(
                    base + 0.5 * (gram_ref[i, j] + gram_ref[i + 2, j]) + gram_ref[i + 1, j]
                )
                total = 0.0
                for a in range(3):
                    for b in range(3):
                        total = total + NEAR[a] * NEAR[b] * side_ref[i + a, j + b : j + b + 1, :]
                sides.append(total)
            for j, w in enumerate(weights_of(gram_sums, sides)):
                out_ref[g, j] = jnp.where(outside, jnp.zeros_like(w), w)
            return carry

        lax.fori_loop(0, 4, body, 0)

    vmem = pl.BlockSpec(memory_space=pltpu.VMEM)
    return pl.pallas_call(
        kernel,
        in_specs=[vmem] * 2,
        out_specs=vmem,
        out_shape=jax.ShapeDtypeStruct((4, tile_lon - 2, members, members), BF16),
        scratch_shapes=[pltpu.VMEM((wide, tile_lon - 2, members, members), F32)],
        compiler_params=PARAMS,
        cost_estimate=pl.CostEstimate(flops=10**10, bytes_accessed=3 * 10**6, transcendentals=0),
        name="middle",
    )(wide_q, wide_side)


def finish(state, wide_q, wide_side, got_a, got_b, inner_w, middle_w, quadrant, frac_lat, frac_lon, land):
    tile_lat, tile_lon, rows, members = state.shape
    wide = tile_lat + 4
    count = 2 * wide

    def kernel(
        state_ref, q_ref, side_ref, a_ref, b_ref, inner_ref, middle_ref, quad_ref, flat_ref, flon_ref, land_ref,
        out_ref, edge_ref, edge_side_ref, gram_ref, w_ref, coef_ref,
    ):
        lat = lax.axis_index("lat")
        last = lax.axis_size("lat") - 1
        lon_odd = lax.rem(lax.axis_index("lon"), 2)
        for s in range(2):
            own = 0 if s == 0 else tile_lon - 2
            at = 2 if s == 0 else 0
            edge_ref[s, :, at : at + 2] = q_ref[:, own : own + 2]
            edge_side_ref[s, :, at : at + 2, :] = side_ref[:, own : own + 2, :]
        for ref, s in ((a_ref, 1 - lon_odd), (b_ref, lon_odd)):
            at = (1 - s) * 0 + s * 2
            base = count * rows
            total = ref[base : base + count, :].astype(F32) + ref[base + count : base + 2 * count, :].astype(F32)
            for i in range(wide):
                for j in range(2):
                    k = (i * 2 + j) * rows
                    edge_ref[s, i, at + j] = ref[k : k + rows, :]
                    edge_side_ref[s, i, pl.ds(at + j, 1), :] = total[2 * i + j : 2 * i + j + 1, :]

        def grams(i, carry):
            for s in range(2):
                for j in range(2):
                    gram_ref[i, s * 2 + j] = row_gram(edge_ref[s, i, j : j + 3])
            return carry

        lax.fori_loop(0, wide, grams, 0)
        base_gram = identity(members)
        for i in range(tile_lat + 2):
            if i < 2:
                source, k = middle_ref, i
            elif i < tile_lat:
                source, k = inner_ref, i - 2
            else:
                source, k = middle_ref, i - tile_lat + 2
            w_ref[i, 2 : tile_lon] = source[k]

        def body(g, carry):
            gram_sums, sides = [], []
            for r in range(2):
                i = g * 2 + r
                for c in range(4):
                    s, j = c // 2, c % 2
                    gram_sums.append(
                        base_gram + 0.5 * (gram_ref[i, c] + gram_ref[i + 2, c]) + gram_ref[i + 1, c]
                    )
                    total = 0.0
                    for a in range(3):
                        for b in range(3):
                            total = total + NEAR[a] * NEAR[b] * edge_side_ref[s, i + a, j + b : j + b + 1, :]
                    sides.append(total)
            out = weights_of(gram_sums, sides)
            for r in range(2):
                i = g * 2 + r
                outside = jnp.logical_or(
                    jnp.logical_and(i == 0, lat == 0), jnp.logical_and(i == tile_lat + 1, lat == last)
                )
                for c in range(4):
                    s, j = c // 2, c % 2
                    w = out[r * 4 + c]
                    w_ref[i, s * tile_lon + j] = jnp.where(outside, jnp.zeros_like(w), w)
            return carry

        lax.fori_loop(0, (tile_lat + 2) // 2, body, 0)

        def analyse(i, carry):
            quad = quad_ref[i]
            fa, fo = flat_ref[i], flon_ref[i]
            dry = jnp.where(land_ref[i] == 1, F32(1.0), F32(0.0))
            north, west = quad < 2, lax.rem(quad, 2) == 0
            zero = jnp.zeros_like(fa)
            along_lat = [
                jnp.where(north, 1.0 - fa, zero) * dry,
                jnp.where(north, fa, 1.0 - fa) * dry,
                jnp.where(north, zero, fa) * dry,
            ]
            along_lon = [
                jnp.where(west, 1.0 - fo, zero),
                jnp.where(west, fo, 1.0 - fo),
                jnp.where(west, zero, fo),
            ]
            for a in range(3):
                for b in range(3):
                    k = (a * 3 + b) * tile_lon
                    coef_ref[k : k + tile_lon, :rows] = along_lat[a] * along_lon[b]
            coef_ref[9 * tile_lon : 10 * tile_lon, :rows] = dry
            columns = coef_ref[...].T
            for j in range(tile_lon):
                x = state_ref[i, j].astype(F32)
                mean = jnp.sum(x, axis=1, keepdims=True) * (1.0 / members)
                centred = x - mean
                perturb = centred.astype(BF16)
                k = 9 * tile_lon + j
                total = x - columns[:rows, k : k + 1] * centred
                for a in range(3):
                    near = w_ref[i + a, j : j + 3].reshape(3 * members, members)
                    out = lax.dot_general(perturb, near, (((1,), (1,)), ((), ())), preferred_element_type=F32)
                    for b in range(3):
                        k = (a * 3 + b) * tile_lon + j
                        total = total + columns[:rows, k : k + 1] * out[:, b * members : (b + 1) * members]
                out_ref[i, j] = total.astype(BF16)
            return carry

        coef_ref[...] = jnp.zeros_like(coef_ref)
        lax.fori_loop(0, tile_lat, analyse, 0)

    vmem = pl.BlockSpec(memory_space=pltpu.VMEM)
    return pl.pallas_call(
        kernel,
        in_specs=[vmem] * 11,
        out_specs=vmem,
        out_shape=jax.ShapeDtypeStruct(state.shape, BF16),
        scratch_shapes=[
            pltpu.VMEM((2, wide, 4, rows, members), BF16),
            pltpu.VMEM((2, wide, 4, members), F32),
            pltpu.VMEM((wide, 4, members, members), F32),
            pltpu.VMEM((tile_lat + 2, tile_lon + 2, members, members), BF16),
            pltpu.VMEM((128, 128), F32),
        ],
        compiler_params=PARAMS,
        cost_estimate=pl.CostEstimate(flops=10**10, bytes_accessed=3 * 10**6, transcendentals=0),
        name="finish",
    )(state, wide_q, wide_side, got_a, got_b, inner_w, middle_w, quadrant, frac_lat, frac_lon, land)


def body(state, obs_row, obs_count, obs_value, obs_weight, quadrant, frac_lat, frac_lon, land):
    tile_lat, tile_lon, rows, members = state.shape
    flat_q, flat_side, send_a, send_b = prepare(lax.axis_size("lat"))(
        state, obs_row, obs_count, obs_value, obs_weight
    )
    got_a = swap(send_a, "lat", 0)
    got_b = swap(send_b, "lat", 1)
    q = flat_q.reshape(tile_lat, tile_lon, rows, members)
    side = flat_side.reshape(tile_lat, tile_lon, members)
    inner_w = interior(q, side)
    wide_q, wide_side, to_a, to_b = widen(q, side, got_a, got_b)
    lon_a = swap(to_a, "lon", 0)
    lon_b = swap(to_b, "lon", 1)
    middle_w = middle(wide_q, wide_side)
    return finish(
        state, wide_q, wide_side, lon_a, lon_b, inner_w, middle_w, quadrant, frac_lat, frac_lon, land
    )


def solution(mesh):
    cell = P("lat", "lon", None)
    return jax.shard_map(
        body,
        mesh=mesh,
        in_specs=(
            P("lat", "lon", None, None), cell, P("lat", "lon"), cell, cell, cell, cell, cell, cell,
        ),
        out_specs=P("lat", "lon", None, None),
        check_vma=False,
    )
```

```python
import math

import jax
import jax.numpy as jnp
from jax import lax
from jax.experimental import pallas as pl
from jax.experimental.pallas import tpu as pltpu
from jax.sharding import PartitionSpec as P

F32 = jnp.float32
BF16 = jnp.bfloat16
ITERS = 6
NEAR = (0.5, 1.0, 0.5)
PARAMS = pltpu.CompilerParams(vmem_limit_bytes=40 * 2**20)


def swap_pairs(count, phase):
    pairs = []
    for k in range(phase, count, 2):
        a, b = k, (k + 1) % count
        pairs += [(a, b), (b, a)]
    return pairs


def swap(x, axis, phase):
    return lax.ppermute(x, axis, swap_pairs(lax.axis_size(axis), phase))


def split(x):
    high = x.astype(BF16)
    return high, (x - high.astype(F32)).astype(BF16)


def stream(pair):
    return jnp.concatenate(pair, axis=1)


def held(pair):
    row = jnp.concatenate(pair, axis=1)
    return jnp.concatenate([row, row], axis=0)


def product(a, b):
    out = jnp.dot(stream(a), held(b), preferred_element_type=F32)
    half = out.shape[1] // 2
    return out[:, :half] + out[:, half:]


def weights_of(grams, sides):
    members = grams[0].shape[0]
    rows = lax.broadcasted_iota(jnp.int32, (members, members), 0)
    cols = lax.broadcasted_iota(jnp.int32, (members, members), 1)
    eye = jnp.where(rows == cols, F32(1.0), F32(0.0))
    inv_frob = []
    iterates = []
    for gram in grams:
        total = jnp.sum(jnp.sum(gram * gram, axis=0, keepdims=True), axis=1, keepdims=True)
        inverse = lax.rsqrt(total)
        inv_frob.append(inverse)
        iterates.append(gram * inverse)
    factors = [1.5 * eye - 0.5 * a for a in iterates]
    roots = factors
    root_parts = [split(t) for t in factors]
    iterates = [product(split(a), t) for a, t in zip(iterates, root_parts)]
    for step in range(1, ITERS):
        iterate_parts = [split(y) for y in iterates]
        factors = [
            1.5 * eye - 0.5 * product(z, y) for z, y in zip(root_parts, iterate_parts)
        ]
        factor_parts = [split(t) for t in factors]
        if step < ITERS - 1:
            iterates = [product(y, t) for y, t in zip(iterate_parts, factor_parts)]
        roots = [product(t, z) for t, z in zip(factor_parts, root_parts)]
        if step < ITERS - 1:
            root_parts = [split(z) for z in roots]
    out = []
    for root, side, inverse in zip(roots, sides, inv_frob):
        inner = jnp.sum(root * side, axis=1, keepdims=True)
        mean_weight = jnp.sum(root * inner, axis=0, keepdims=True) * inverse
        out.append((mean_weight + (math.sqrt(members - 1) * jnp.sqrt(inverse)) * root).astype(BF16))
    return out


def row_grams(pairs):
    turned = [pair.T for pair in pairs]
    rows = pairs[0].shape[0] // 2
    half = BF16(0.5)
    out = []
    for p in range(len(pairs) - 1):
        first, second = pairs[p], pairs[p + 1]
        zero = jnp.zeros((rows, first.shape[1]), BF16)
        left = jnp.concatenate([first[:rows] * half, first[rows:], second[:rows] * half, zero], axis=0)
        right = jnp.concatenate([zero, first[rows:] * half, second[:rows], second[rows:] * half], axis=0)
        both = jnp.dot(
            jnp.concatenate(turned[p : p + 2], axis=1),
            jnp.concatenate([left, right], axis=1),
            preferred_element_type=F32,
        )
        members = both.shape[0]
        out += [both[:, :members], both[:, members:]]
    return out


def pair_of(ref, i, j):
    pair = ref[i, j : j + 2]
    return pair.reshape(2 * pair.shape[1], pair.shape[2])


def node_sum(base, gram_ref, i, j):
    return base + 0.5 * (gram_ref[i, j] + gram_ref[i + 2, j]) + gram_ref[i + 1, j]


def near_side(side_ref, i, j):
    total = 0.0
    for a in range(3):
        for b in range(3):
            total = total + NEAR[a] * NEAR[b] * side_ref[i + a, j + b : j + b + 1, :]
    return total


def identity(members):
    rows = lax.broadcasted_iota(jnp.int32, (members, members), 0)
    cols = lax.broadcasted_iota(jnp.int32, (members, members), 1)
    return jnp.where(rows == cols, F32(members - 1), F32(0.0))


def prepare(state, obs_row, obs_count, obs_value, obs_weight):
    tile_lat, tile_lon, rows, members = state.shape
    slots = obs_row.shape[2]
    cells = tile_lat * tile_lon
    payload = cells // 2 * rows + cells

    def kernel(
        count_hbm, state_hbm, row_hbm, value_hbm, weight_hbm, q_ref, side_ref, a_ref, b_ref,
        count_ref, state_ref, row_ref, value_ref, weight_ref, sems,
    ):
        copies = [
            pltpu.make_async_copy(source, target, sems.at[k])
            for k, (source, target) in enumerate(
                (
                    (count_hbm, count_ref),
                    (row_hbm, row_ref),
                    (value_hbm, value_ref),
                    (weight_hbm, weight_ref),
                    (state_hbm, state_ref),
                )
            )
        ]
        for copy in copies:
            copy.start()
        lane = lax.broadcasted_iota(jnp.int32, (1, slots), 1)
        row_ids = lax.broadcasted_iota(jnp.int32, (rows, slots), 0)
        for copy in copies:
            copy.wait()

        def body(i, carry):
            for j in range(tile_lon):
                x = state_ref[i, j].astype(F32)
                mean = jnp.sum(x, axis=1, keepdims=True) * (1.0 / members)
                centred = x - mean
                live = jnp.where(lane < count_ref[i, j], weight_ref[i, j : j + 1, :], 0.0)
                hit = row_ids == row_ref[i, j : j + 1, :]
                centre = jnp.sum(jnp.where(hit, mean, 0.0), axis=0, keepdims=True)
                innovation = ((value_ref[i, j : j + 1, :] - centre) * live).astype(BF16).astype(F32)
                square = jnp.sum(jnp.where(hit, live * live, 0.0), axis=1, keepdims=True)
                pull = jnp.sum(jnp.where(hit, live * innovation, 0.0), axis=1, keepdims=True)
                start = pl.multiple_of((i * tile_lon + j) * rows, rows)
                q_ref[pl.ds(start, rows), :] = (centred * jnp.sqrt(square)).astype(BF16)
                side_ref[pl.ds(i * tile_lon + j, 1), :] = jnp.sum(
                    centred * pull, axis=0, keepdims=True
                )
            return carry

        lax.fori_loop(0, tile_lat, body, 0)
        odd = lax.rem(lax.axis_index("lat"), 2)
        half = tile_lat // 2 * tile_lon
        for ref, first in ((a_ref, 1 - odd), (b_ref, odd)):
            start = pl.multiple_of(first * half * rows, half * rows)
            ref[: half * rows, :] = q_ref[pl.ds(start, half * rows), :]
            high, low = split(side_ref[pl.ds(pl.multiple_of(first * half, half), half), :])
            ref[half * rows : half * rows + half, :] = high
            ref[half * rows + half : half * rows + 2 * half, :] = low

    vmem = pl.BlockSpec(memory_space=pltpu.VMEM)
    hbm = pl.BlockSpec(memory_space=pltpu.HBM)
    return pl.pallas_call(
        kernel,
        in_specs=[hbm] * 5,
        out_specs=[vmem] * 4,
        out_shape=[
            jax.ShapeDtypeStruct((cells * rows, members), BF16),
            jax.ShapeDtypeStruct((cells, members), F32),
            jax.ShapeDtypeStruct((payload, members), BF16),
            jax.ShapeDtypeStruct((payload, members), BF16),
        ],
        scratch_shapes=[
            pltpu.SMEM(obs_count.shape, obs_count.dtype),
            pltpu.VMEM(state.shape, state.dtype),
            pltpu.VMEM(obs_row.shape, obs_row.dtype),
            pltpu.VMEM(obs_value.shape, obs_value.dtype),
            pltpu.VMEM(obs_weight.shape, obs_weight.dtype),
            pltpu.SemaphoreType.DMA((5,)),
        ],
        compiler_params=PARAMS,
        cost_estimate=pl.CostEstimate(flops=10**8, bytes_accessed=2 * 10**6, transcendentals=0),
        name="prepare",
    )(*[
        pltpu.with_memory_space_constraint(x, pltpu.HBM)
        for x in (obs_count, state, obs_row, obs_value, obs_weight)
    ])


def interior(q, side, quadrant, frac_lat, frac_lon, land):
    tile_lat, tile_lon, rows, members = q.shape

    def kernel(q_ref, side_ref, quad_ref, flat_ref, flon_ref, land_ref, out_ref, columns_ref, gram_ref, coef_ref):
        def grams(i, carry):
            pairs = [pair_of(q_ref, i, j) for j in range(0, tile_lon, 2)]
            for j, gram in enumerate(row_grams(pairs)):
                gram_ref[i, j] = gram
            return carry

        lax.fori_loop(0, tile_lat, grams, 0, unroll=True)
        base = identity(members)
        nodes = [(i, j) for i in range(tile_lat - 2) for j in range(tile_lon - 2)]
        sums = [node_sum(base, gram_ref, i, j) for i, j in nodes]
        sides = [near_side(side_ref, i, j) for i, j in nodes]
        for (i, j), w in zip(nodes, weights_of(sums, sides)):
            out_ref[i, j] = w

        coef_ref[...] = jnp.zeros_like(coef_ref)

        def columns(i, carry):
            quad = quad_ref[i]
            fa, fo = flat_ref[i], flon_ref[i]
            dry = jnp.where(land_ref[i] == 1, F32(1.0), F32(0.0))
            north, west = quad < 2, lax.rem(quad, 2) == 0
            zero = jnp.zeros_like(fa)
            coefs = (
                jnp.where(north, 1.0 - fa, zero) * dry,
                jnp.where(north, fa, 1.0 - fa) * dry,
                jnp.where(north, zero, fa) * dry,
                jnp.where(west, 1.0 - fo, zero),
                jnp.where(west, fo, 1.0 - fo),
                jnp.where(west, zero, fo),
                dry,
            )
            for k, coef in enumerate(coefs):
                coef_ref[k * tile_lon : (k + 1) * tile_lon, :rows] = coef
            turned = coef_ref[...].T
            for k in range(len(coefs)):
                for j in range(tile_lon):
                    at = k * tile_lon + j
                    columns_ref[i, k, j * rows : (j + 1) * rows, :] = jnp.broadcast_to(
                        turned[:rows, at : at + 1], (rows, members)
                    )
            return carry

        lax.fori_loop(0, tile_lat, columns, 0)

    vmem = pl.BlockSpec(memory_space=pltpu.VMEM)
    return pl.pallas_call(
        kernel,
        in_specs=[vmem] * 6,
        out_specs=[vmem] * 2,
        out_shape=[
            jax.ShapeDtypeStruct((tile_lat - 2, tile_lon - 2, members, members), BF16),
            jax.ShapeDtypeStruct((tile_lat, 7, tile_lon * rows, members), F32),
        ],
        scratch_shapes=[
            pltpu.VMEM((tile_lat, tile_lon - 2, members, members), F32),
            pltpu.VMEM((128, 128), F32),
        ],
        compiler_params=PARAMS,
        cost_estimate=pl.CostEstimate(flops=5 * 10**9, bytes_accessed=2 * 10**6, transcendentals=0),
        name="interior",
    )(q, side, quadrant, frac_lat, frac_lon, land)


def widen(q, side, got_a, got_b):
    tile_lat, tile_lon, rows, members = q.shape
    half = 2 * tile_lon
    wide = tile_lat + 4
    count = 2 * wide
    payload = count * rows + 2 * count

    def kernel(q_ref, side_ref, a_ref, b_ref, wide_ref, wide_side_ref, to_a_ref, to_b_ref):
        lat = lax.axis_index("lat")
        lon = lax.axis_index("lon")
        lat_odd = lax.rem(lat, 2)
        lon_odd = lax.rem(lon, 2)
        wide_ref[2 : 2 + tile_lat] = q_ref[...]
        wide_side_ref[2 : 2 + tile_lat] = side_ref[...]
        last = lax.axis_size("lat") - 1
        a_valid = jnp.where(lat_odd == 0, lat < last, lat > 0)
        b_valid = jnp.where(lat_odd == 0, lat > 0, lat < last)
        for ref, first, valid in (
            (a_ref, (1 - lat_odd) * (tile_lat + 2), a_valid),
            (b_ref, lat_odd * (tile_lat + 2), b_valid),
        ):
            for i in range(2):
                for j in range(tile_lon):
                    k = (i * tile_lon + j) * rows
                    piece = ref[k : k + rows, :]
                    wide_ref[first + i, j] = jnp.where(valid, piece, jnp.zeros_like(piece))
            base = half * rows
            total = ref[base : base + half, :].astype(F32) + ref[base + half : base + 2 * half, :].astype(F32)
            total = jnp.where(valid, total, 0.0)
            wide_side_ref[first] = total[:tile_lon]
            wide_side_ref[first + 1] = total[tile_lon:]
        for ref, first in ((to_a_ref, (1 - lon_odd) * (tile_lon - 2)), (to_b_ref, lon_odd * (tile_lon - 2))):
            collected = []
            for i in range(wide):
                for j in range(2):
                    k = (i * 2 + j) * rows
                    ref[k : k + rows, :] = wide_ref[i, first + j]
                    collected.append(wide_side_ref[i, pl.ds(first + j, 1), :])
            high, low = split(jnp.concatenate(collected, axis=0))
            base = count * rows
            ref[base : base + count, :] = high
            ref[base + count : base + 2 * count, :] = low

    vmem = pl.BlockSpec(memory_space=pltpu.VMEM)
    return pl.pallas_call(
        kernel,
        in_specs=[vmem] * 4,
        out_specs=[vmem] * 4,
        out_shape=[
            jax.ShapeDtypeStruct((wide, tile_lon, rows, members), BF16),
            jax.ShapeDtypeStruct((wide, tile_lon, members), F32),
            jax.ShapeDtypeStruct((payload, members), BF16),
            jax.ShapeDtypeStruct((payload, members), BF16),
        ],
        compiler_params=PARAMS,
        cost_estimate=pl.CostEstimate(flops=10**6, bytes_accessed=3 * 10**6, transcendentals=0),
        name="widen",
    )(q, side, got_a, got_b)


def middle(wide_q, wide_side):
    wide, tile_lon, rows, members = wide_q.shape
    tile_lat = wide - 4

    def kernel(q_ref, side_ref, out_ref, gram_ref):
        def grams(i, carry):
            pairs = [pair_of(q_ref, i, j) for j in range(0, tile_lon, 2)]
            for j, gram in enumerate(row_grams(pairs)):
                gram_ref[i, j] = gram
            return carry

        lax.fori_loop(0, wide, grams, 0, unroll=True)
        base = identity(members)
        lat = lax.axis_index("lat")
        last = lax.axis_size("lat") - 1

        def body(g, carry):
            first = g * tile_lat
            outside = (
                jnp.logical_and(g == 0, lat == 0),
                jnp.logical_and(g == 1, lat == last),
            )
            nodes = [(r, j) for r in range(2) for j in range(tile_lon - 2)]
            sums = [node_sum(base, gram_ref, first + r, j) for r, j in nodes]
            sides = [near_side(side_ref, first + r, j) for r, j in nodes]
            for (r, j), w in zip(nodes, weights_of(sums, sides)):
                out_ref[2 * g + r, j] = jnp.where(outside[r], jnp.zeros_like(w), w)
            return carry

        lax.fori_loop(0, 2, body, 0)

    vmem = pl.BlockSpec(memory_space=pltpu.VMEM)
    return pl.pallas_call(
        kernel,
        in_specs=[vmem] * 2,
        out_specs=vmem,
        out_shape=jax.ShapeDtypeStruct((4, tile_lon - 2, members, members), BF16),
        scratch_shapes=[pltpu.VMEM((wide, tile_lon - 2, members, members), F32)],
        compiler_params=PARAMS,
        cost_estimate=pl.CostEstimate(flops=10**10, bytes_accessed=3 * 10**6, transcendentals=0),
        name="middle",
    )(wide_q, wide_side)


def finish(state, wide_q, wide_side, got_a, got_b, inner_w, middle_w, columns):
    tile_lat, tile_lon, rows, members = state.shape
    wide = tile_lat + 4
    count = 2 * wide

    def kernel(
        state_ref, q_ref, side_ref, a_ref, b_ref, inner_ref, middle_ref, columns_ref,
        out_ref, edge_ref, edge_side_ref, gram_ref, w_ref, perturb_ref,
    ):
        lat = lax.axis_index("lat")
        last = lax.axis_size("lat") - 1
        lon_odd = lax.rem(lax.axis_index("lon"), 2)
        for s in range(2):
            own = 0 if s == 0 else tile_lon - 2
            at = 2 if s == 0 else 0
            edge_ref[s, :, at : at + 2] = q_ref[:, own : own + 2]
            edge_side_ref[s, :, at : at + 2, :] = side_ref[:, own : own + 2, :]
        for ref, s in ((a_ref, 1 - lon_odd), (b_ref, lon_odd)):
            at = s * 2
            base = count * rows
            total = ref[base : base + count, :].astype(F32) + ref[base + count : base + 2 * count, :].astype(F32)
            for i in range(wide):
                for j in range(2):
                    k = (i * 2 + j) * rows
                    edge_ref[s, i, at + j] = ref[k : k + rows, :]
                    edge_side_ref[s, i, pl.ds(at + j, 1), :] = total[2 * i + j : 2 * i + j + 1, :]

        def grams(i, carry):
            for s in range(2):
                pairs = [pair_of(edge_ref.at[s], i, j) for j in (0, 2)]
                for j, gram in enumerate(row_grams(pairs)):
                    gram_ref[i, s * 2 + j] = gram
            return carry

        lax.fori_loop(0, wide, grams, 0, unroll=True)
        base_gram = identity(members)
        for i in range(tile_lat + 2):
            if i < 2:
                source, k = middle_ref, i
            elif i < tile_lat:
                source, k = inner_ref, i - 2
            else:
                source, k = middle_ref, i - tile_lat + 2
            w_ref[i, 2 : tile_lon] = source[k]
        group = (tile_lat + 2) // 2

        def body(g, carry):
            nodes = [(g * group + r, c) for r in range(group) for c in range(4)]
            sums = [node_sum(base_gram, gram_ref, i, c) for i, c in nodes]
            sides = [near_side(edge_side_ref.at[c // 2], i, c % 2) for i, c in nodes]
            for (i, c), w in zip(nodes, weights_of(sums, sides)):
                outside = jnp.logical_or(
                    jnp.logical_and(i == 0, lat == 0), jnp.logical_and(i == tile_lat + 1, lat == last)
                )
                w_ref[i, (c // 2) * tile_lon + c % 2] = jnp.where(outside, jnp.zeros_like(w), w)
            return carry

        lax.fori_loop(0, 2, body, 0)

        def analyse(i, carry):
            totals = []
            for j in range(tile_lon):
                x = state_ref[i, j].astype(F32)
                mean = jnp.sum(x, axis=1, keepdims=True) * (1.0 / members)
                centred = x - mean
                perturb_ref[j * rows : (j + 1) * rows, :] = centred.astype(BF16)
                totals.append(x - columns_ref[i, 6, j * rows : (j + 1) * rows, :] * centred)
            for n in range(tile_lon + 2):
                low, high = max(n - 2, 0), min(n, tile_lon - 1)
                near = jnp.concatenate([w_ref[i + a, n] for a in range(3)], axis=0)
                out = lax.dot_general(
                    perturb_ref[low * rows : (high + 1) * rows, :],
                    near,
                    (((1,), (1,)), ((), ())),
                    preferred_element_type=F32,
                )
                for j in range(low, high + 1):
                    here = out[(j - low) * rows : (j - low + 1) * rows]
                    span = slice(j * rows, (j + 1) * rows)
                    mixed = 0.0
                    for a in range(3):
                        mixed = mixed + columns_ref[i, a, span, :] * here[:, a * members : (a + 1) * members]
                    totals[j] = totals[j] + columns_ref[i, 3 + n - j, span, :] * mixed
                    if n == j + 2:
                        out_ref[i, j] = totals[j].astype(BF16)
            return carry

        lax.fori_loop(0, tile_lat, analyse, 0)

    vmem = pl.BlockSpec(memory_space=pltpu.VMEM)
    return pl.pallas_call(
        kernel,
        in_specs=[vmem] * 8,
        out_specs=vmem,
        out_shape=jax.ShapeDtypeStruct(state.shape, BF16),
        scratch_shapes=[
            pltpu.VMEM((2, wide, 4, rows, members), BF16),
            pltpu.VMEM((2, wide, 4, members), F32),
            pltpu.VMEM((wide, 4, members, members), F32),
            pltpu.VMEM((tile_lat + 2, tile_lon + 2, members, members), BF16),
            pltpu.VMEM((tile_lon * rows, members), BF16),
        ],
        compiler_params=PARAMS,
        cost_estimate=pl.CostEstimate(flops=10**10, bytes_accessed=3 * 10**6, transcendentals=0),
        name="finish",
    )(state, wide_q, wide_side, got_a, got_b, inner_w, middle_w, columns)


def body(state, obs_row, obs_count, obs_value, obs_weight, quadrant, frac_lat, frac_lon, land):
    tile_lat, tile_lon, rows, members = state.shape
    flat_q, flat_side, send_a, send_b = prepare(state, obs_row, obs_count, obs_value, obs_weight)
    got_a = swap(send_a, "lat", 0)
    got_b = swap(send_b, "lat", 1)
    q = flat_q.reshape(tile_lat, tile_lon, rows, members)
    side = flat_side.reshape(tile_lat, tile_lon, members)
    inner_w, columns = interior(q, side, quadrant, frac_lat, frac_lon, land)
    wide_q, wide_side, to_a, to_b = widen(q, side, got_a, got_b)
    lon_a = swap(to_a, "lon", 0)
    lon_b = swap(to_b, "lon", 1)
    middle_w = middle(wide_q, wide_side)
    return finish(state, wide_q, wide_side, lon_a, lon_b, inner_w, middle_w, columns)


def solution(mesh):
    cell = P("lat", "lon", None)
    return jax.shard_map(
        body,
        mesh=mesh,
        in_specs=(
            P("lat", "lon", None, None), cell, P("lat", "lon"), cell, cell, cell, cell, cell, cell,
        ),
        out_specs=P("lat", "lon", None, None),
        check_vma=False,
    )
```

```python
import math

import jax
import jax.numpy as jnp
from jax import lax
from jax.experimental import pallas as pl
from jax.experimental.pallas import tpu as pltpu
from jax.sharding import PartitionSpec as P

F32 = jnp.float32
BF16 = jnp.bfloat16
ITERS = 6
NEAR = (0.5, 1.0, 0.5)
PARAMS = pltpu.CompilerParams(vmem_limit_bytes=40 * 2**20)


def swap(x, axis, phase, closed):
    count = lax.axis_size(axis)
    pairs = []
    for k in range(phase, count, 2):
        a, b = k, (k + 1) % count
        pairs += [(a, b), (b, a)] if closed or a < b else [(a, a), (b, b)]
    return lax.ppermute(x, axis, pairs)


def split(x):
    high = x.astype(BF16)
    return high, (x - high.astype(F32)).astype(BF16)


def stream(pair):
    return jnp.concatenate(pair, axis=1)


def held(pair):
    row = jnp.concatenate(pair, axis=1)
    return jnp.concatenate([row, row], axis=0)


def product(a, b):
    out = jnp.dot(stream(a), held(b), preferred_element_type=F32)
    half = out.shape[1] // 2
    return out[:, :half] + out[:, half:]


def weights_of(grams, sides):
    members = grams[0].shape[0]
    rows = lax.broadcasted_iota(jnp.int32, (members, members), 0)
    cols = lax.broadcasted_iota(jnp.int32, (members, members), 1)
    eye = jnp.where(rows == cols, F32(1.0), F32(0.0))
    inv_frob = []
    iterates = []
    for gram in grams:
        total = jnp.sum(jnp.sum(gram * gram, axis=0, keepdims=True), axis=1, keepdims=True)
        inverse = lax.rsqrt(total)
        inv_frob.append(inverse)
        iterates.append(gram * inverse)
    first = [split(a) for a in iterates]
    squares, square_parts = iterates, first
    for step in range(0, ITERS, 2):
        inner = [
            product(part, part) + (3.375 * eye - 4.5 * x)
            for part, x in zip(square_parts, squares)
        ]
        inner_parts = [split(x) for x in inner]
        factors = [
            0.0625 * product(part, part) + ((24.609375 / 16) * eye - (8.625 / 16) * x)
            for part, x in zip(inner_parts, squares)
        ]
        factor_parts = [split(x) for x in factors]
        if step == 0:
            roots, root_parts = factors, factor_parts
        else:
            roots = [product(z, x) for z, x in zip(root_parts, factor_parts)]
        if step < ITERS - 2:
            if step > 0:
                root_parts = [split(z) for z in roots]
            half = [split(product(a, z)) for a, z in zip(first, root_parts)]
            squares = [product(x, z) for x, z in zip(half, root_parts)]
            square_parts = [split(x) for x in squares]
    out = []
    for root, side, inverse in zip(roots, sides, inv_frob):
        inner = jnp.sum(root * side, axis=1, keepdims=True)
        mean_weight = jnp.sum(root * inner, axis=0, keepdims=True) * inverse
        out.append((mean_weight + (math.sqrt(members - 1) * jnp.sqrt(inverse)) * root).astype(BF16))
    return out


def row_grams(pairs):
    turned = [pair.T for pair in pairs]
    rows = pairs[0].shape[0] // 2
    half = BF16(0.5)
    out = []
    for p in range(len(pairs) - 1):
        first, second = pairs[p], pairs[p + 1]
        zero = jnp.zeros((rows, first.shape[1]), BF16)
        left = jnp.concatenate([first[:rows] * half, first[rows:], second[:rows] * half, zero], axis=0)
        right = jnp.concatenate([zero, first[rows:] * half, second[:rows], second[rows:] * half], axis=0)
        both = jnp.dot(
            jnp.concatenate(turned[p : p + 2], axis=1),
            jnp.concatenate([left, right], axis=1),
            preferred_element_type=F32,
        )
        members = both.shape[0]
        out += [both[:, :members], both[:, members:]]
    return out


def pair_of(ref, i, j):
    pair = ref[i, j : j + 2]
    return pair.reshape(2 * pair.shape[1], pair.shape[2])


def node_sum(base, gram_ref, i, j):
    return base + 0.5 * (gram_ref[i, j] + gram_ref[i + 2, j]) + gram_ref[i + 1, j]


def near_side(side_ref, i, j):
    total = 0.0
    for a in range(3):
        for b in range(3):
            total = total + NEAR[a] * NEAR[b] * side_ref[i + a, j + b : j + b + 1, :]
    return total


def identity(members):
    rows = lax.broadcasted_iota(jnp.int32, (members, members), 0)
    cols = lax.broadcasted_iota(jnp.int32, (members, members), 1)
    return jnp.where(rows == cols, F32(members - 1), F32(0.0))


def prepare(state, obs_row, obs_count, obs_value, obs_weight):
    tile_lat, tile_lon, rows, members = state.shape
    slots = obs_row.shape[2]
    cells = tile_lat * tile_lon
    payload = cells // 2 * rows + cells

    def kernel(
        count_hbm, state_hbm, row_hbm, value_hbm, weight_hbm, q_ref, side_ref, a_ref, b_ref,
        count_ref, state_ref, row_ref, value_ref, weight_ref, sems,
    ):
        copies = [
            pltpu.make_async_copy(source, target, sems.at[k])
            for k, (source, target) in enumerate(
                (
                    (count_hbm, count_ref),
                    (row_hbm, row_ref),
                    (value_hbm, value_ref),
                    (weight_hbm, weight_ref),
                )
            )
        ]
        row_copies = [
            pltpu.make_async_copy(state_hbm.at[i], state_ref.at[i], sems.at[4 + i]) for i in range(tile_lat)
        ]
        for copy in copies + row_copies:
            copy.start()
        lane = lax.broadcasted_iota(jnp.int32, (1, slots), 1)
        row_ids = lax.broadcasted_iota(jnp.int32, (rows, slots), 0)
        for copy in copies:
            copy.wait()

        for i in range(tile_lat):
            row_copies[i].wait()
            for j in range(tile_lon):
                x = state_ref[i, j].astype(F32)
                mean = jnp.sum(x, axis=1, keepdims=True) * (1.0 / members)
                centred = x - mean
                live = jnp.where(lane < count_ref[i, j], weight_ref[i, j : j + 1, :], 0.0)
                hit = row_ids == row_ref[i, j : j + 1, :]
                centre = jnp.sum(jnp.where(hit, mean, 0.0), axis=0, keepdims=True)
                innovation = ((value_ref[i, j : j + 1, :] - centre) * live).astype(BF16).astype(F32)
                square = jnp.sum(jnp.where(hit, live * live, 0.0), axis=1, keepdims=True)
                pull = jnp.sum(jnp.where(hit, live * innovation, 0.0), axis=1, keepdims=True)
                start = (i * tile_lon + j) * rows
                q_ref[start : start + rows, :] = (centred * jnp.sqrt(square)).astype(BF16)
                side_ref[i * tile_lon + j : i * tile_lon + j + 1, :] = jnp.sum(
                    centred * pull, axis=0, keepdims=True
                )
        odd = lax.rem(lax.axis_index("lat"), 2)
        half = tile_lat // 2 * tile_lon
        for ref, first in ((a_ref, 1 - odd), (b_ref, odd)):
            start = pl.multiple_of(first * half * rows, half * rows)
            ref[: half * rows, :] = q_ref[pl.ds(start, half * rows), :]
            high, low = split(side_ref[pl.ds(pl.multiple_of(first * half, half), half), :])
            ref[half * rows : half * rows + half, :] = high
            ref[half * rows + half : half * rows + 2 * half, :] = low

    vmem = pl.BlockSpec(memory_space=pltpu.VMEM)
    hbm = pl.BlockSpec(memory_space=pltpu.HBM)
    return pl.pallas_call(
        kernel,
        in_specs=[hbm] * 5,
        out_specs=[vmem] * 4,
        out_shape=[
            jax.ShapeDtypeStruct((cells * rows, members), BF16),
            jax.ShapeDtypeStruct((cells, members), F32),
            jax.ShapeDtypeStruct((payload, members), BF16),
            jax.ShapeDtypeStruct((payload, members), BF16),
        ],
        scratch_shapes=[
            pltpu.SMEM(obs_count.shape, obs_count.dtype),
            pltpu.VMEM(state.shape, state.dtype),
            pltpu.VMEM(obs_row.shape, obs_row.dtype),
            pltpu.VMEM(obs_value.shape, obs_value.dtype),
            pltpu.VMEM(obs_weight.shape, obs_weight.dtype),
            pltpu.SemaphoreType.DMA((4 + tile_lat,)),
        ],
        compiler_params=PARAMS,
        cost_estimate=pl.CostEstimate(flops=10**8, bytes_accessed=2 * 10**6, transcendentals=0),
        name="prepare",
    )(*[
        pltpu.with_memory_space_constraint(x, pltpu.HBM)
        for x in (obs_count, state, obs_row, obs_value, obs_weight)
    ])


def interior(q, side, quadrant, frac_lat, frac_lon, land):
    tile_lat, tile_lon, rows, members = q.shape

    def kernel(
        q_ref, side_ref, quad_hbm, flat_hbm, flon_hbm, land_hbm, out_ref, columns_ref, gram_ref,
        coef_ref, quad_ref, flat_ref, flon_ref, land_ref, sems,
    ):
        copies = [
            pltpu.make_async_copy(source, target, sems.at[k])
            for k, (source, target) in enumerate(
                ((quad_hbm, quad_ref), (flat_hbm, flat_ref), (flon_hbm, flon_ref), (land_hbm, land_ref))
            )
        ]
        for copy in copies:
            copy.start()

        def grams(i, carry):
            pairs = [pair_of(q_ref, i, j) for j in range(0, tile_lon, 2)]
            for j, gram in enumerate(row_grams(pairs)):
                gram_ref[i, j] = gram
            return carry

        lax.fori_loop(0, tile_lat, grams, 0, unroll=True)
        base = identity(members)
        nodes = [(i, j) for i in range(tile_lat - 2) for j in range(tile_lon - 2)]
        sums = [node_sum(base, gram_ref, i, j) for i, j in nodes]
        sides = [near_side(side_ref, i, j) for i, j in nodes]
        for (i, j), w in zip(nodes, weights_of(sums, sides)):
            out_ref[i, j] = w

        coef_ref[...] = jnp.zeros_like(coef_ref)
        for copy in copies:
            copy.wait()

        def columns(i, carry):
            quad = quad_ref[i]
            fa, fo = flat_ref[i], flon_ref[i]
            dry = jnp.where(land_ref[i] == 1, F32(1.0), F32(0.0))
            north, west = quad < 2, lax.rem(quad, 2) == 0
            zero = jnp.zeros_like(fa)
            coefs = (
                jnp.where(north, 1.0 - fa, zero) * dry,
                jnp.where(north, fa, 1.0 - fa) * dry,
                jnp.where(north, zero, fa) * dry,
                jnp.where(west, 1.0 - fo, zero),
                jnp.where(west, fo, 1.0 - fo),
                jnp.where(west, zero, fo),
                dry,
            )
            for k, coef in enumerate(coefs):
                coef_ref[k * tile_lon : (k + 1) * tile_lon, :rows] = coef
            turned = coef_ref[...].T
            for k in range(len(coefs)):
                for j in range(tile_lon):
                    at = k * tile_lon + j
                    columns_ref[i, k, j * rows : (j + 1) * rows, :] = jnp.broadcast_to(
                        turned[:rows, at : at + 1], (rows, members)
                    )
            return carry

        lax.fori_loop(0, tile_lat, columns, 0)

    vmem = pl.BlockSpec(memory_space=pltpu.VMEM)
    return pl.pallas_call(
        kernel,
        in_specs=[vmem] * 2 + [pl.BlockSpec(memory_space=pltpu.HBM)] * 4,
        out_specs=[vmem] * 3,
        out_shape=[
            jax.ShapeDtypeStruct((tile_lat - 2, tile_lon - 2, members, members), BF16),
            jax.ShapeDtypeStruct((tile_lat, 7, tile_lon * rows, members), F32),
            jax.ShapeDtypeStruct((tile_lat, tile_lon - 2, members, members), F32),
        ],
        scratch_shapes=[pltpu.VMEM((128, 128), F32)]
        + [pltpu.VMEM(x.shape, x.dtype) for x in (quadrant, frac_lat, frac_lon, land)]
        + [pltpu.SemaphoreType.DMA((4,))],
        compiler_params=PARAMS,
        cost_estimate=pl.CostEstimate(flops=5 * 10**9, bytes_accessed=2 * 10**6, transcendentals=0),
        name="interior",
    )(
        q, side,
        *[pltpu.with_memory_space_constraint(x, pltpu.HBM) for x in (quadrant, frac_lat, frac_lon, land)],
    )


def widen(q, side, got_a, got_b):
    tile_lat, tile_lon, rows, members = q.shape
    half = 2 * tile_lon
    wide = tile_lat + 4
    count = 2 * wide
    payload = count * rows + 2 * count

    def kernel(q_ref, side_ref, a_ref, b_ref, wide_ref, wide_side_ref, to_a_ref, to_b_ref):
        lat = lax.axis_index("lat")
        lon = lax.axis_index("lon")
        lat_odd = lax.rem(lat, 2)
        lon_odd = lax.rem(lon, 2)
        wide_ref[2 : 2 + tile_lat] = q_ref[...]
        wide_side_ref[2 : 2 + tile_lat] = side_ref[...]
        last = lax.axis_size("lat") - 1
        a_valid = jnp.where(lat_odd == 0, lat < last, lat > 0)
        b_valid = jnp.where(lat_odd == 0, lat > 0, lat < last)
        for ref, first, valid in (
            (a_ref, (1 - lat_odd) * (tile_lat + 2), a_valid),
            (b_ref, lat_odd * (tile_lat + 2), b_valid),
        ):
            for i in range(2):
                for j in range(tile_lon):
                    k = (i * tile_lon + j) * rows
                    piece = ref[k : k + rows, :]
                    wide_ref[first + i, j] = jnp.where(valid, piece, jnp.zeros_like(piece))
            base = half * rows
            total = ref[base : base + half, :].astype(F32) + ref[base + half : base + 2 * half, :].astype(F32)
            total = jnp.where(valid, total, 0.0)
            wide_side_ref[first] = total[:tile_lon]
            wide_side_ref[first + 1] = total[tile_lon:]
        for ref, first in ((to_a_ref, (1 - lon_odd) * (tile_lon - 2)), (to_b_ref, lon_odd * (tile_lon - 2))):
            collected = []
            for i in range(wide):
                for j in range(2):
                    k = (i * 2 + j) * rows
                    ref[k : k + rows, :] = wide_ref[i, first + j]
                    collected.append(wide_side_ref[i, pl.ds(first + j, 1), :])
            high, low = split(jnp.concatenate(collected, axis=0))
            base = count * rows
            ref[base : base + count, :] = high
            ref[base + count : base + 2 * count, :] = low

    vmem = pl.BlockSpec(memory_space=pltpu.VMEM)
    return pl.pallas_call(
        kernel,
        in_specs=[vmem] * 4,
        out_specs=[vmem] * 4,
        out_shape=[
            jax.ShapeDtypeStruct((wide, tile_lon, rows, members), BF16),
            jax.ShapeDtypeStruct((wide, tile_lon, members), F32),
            jax.ShapeDtypeStruct((payload, members), BF16),
            jax.ShapeDtypeStruct((payload, members), BF16),
        ],
        compiler_params=PARAMS,
        cost_estimate=pl.CostEstimate(flops=10**6, bytes_accessed=3 * 10**6, transcendentals=0),
        name="widen",
    )(q, side, got_a, got_b)


def middle(wide_q, wide_side, own_grams):
    wide, tile_lon, rows, members = wide_q.shape
    tile_lat = wide - 4

    def kernel(q_ref, side_ref, own_ref, out_ref, gram_ref):
        for k in range(8):
            i = k if k < 4 else k + tile_lat - 4
            if 2 <= i < 2 + tile_lat:
                gram_ref[k] = own_ref[i - 2]
            else:
                pairs = [pair_of(q_ref, i, j) for j in range(0, tile_lon, 2)]
                for j, gram in enumerate(row_grams(pairs)):
                    gram_ref[k, j] = gram
        base = identity(members)
        lat = lax.axis_index("lat")
        last = lax.axis_size("lat") - 1

        def body(g, carry):
            first = g * tile_lat
            outside = (
                jnp.logical_and(g == 0, lat == 0),
                jnp.logical_and(g == 1, lat == last),
            )
            nodes = [(r, j) for r in range(2) for j in range(tile_lon - 2)]
            sums = [node_sum(base, gram_ref, 4 * g + r, j) for r, j in nodes]
            sides = [near_side(side_ref, first + r, j) for r, j in nodes]
            for (r, j), w in zip(nodes, weights_of(sums, sides)):
                out_ref[2 * g + r, j] = jnp.where(outside[r], jnp.zeros_like(w), w)
            return carry

        lax.fori_loop(0, 2, body, 0)

    vmem = pl.BlockSpec(memory_space=pltpu.VMEM)
    return pl.pallas_call(
        kernel,
        in_specs=[vmem] * 3,
        out_specs=vmem,
        out_shape=jax.ShapeDtypeStruct((4, tile_lon - 2, members, members), BF16),
        scratch_shapes=[pltpu.VMEM((8, tile_lon - 2, members, members), F32)],
        compiler_params=PARAMS,
        cost_estimate=pl.CostEstimate(flops=10**10, bytes_accessed=3 * 10**6, transcendentals=0),
        name="middle",
    )(wide_q, wide_side, own_grams)


def finish(state, wide_q, wide_side, got_a, got_b, inner_w, middle_w, columns):
    tile_lat, tile_lon, rows, members = state.shape
    wide = tile_lat + 4
    count = 2 * wide

    def kernel(
        state_ref, q_ref, side_ref, a_ref, b_ref, inner_ref, middle_ref, columns_ref,
        out_hbm, edge_ref, edge_side_ref, gram_ref, w_ref, perturb_ref, out_ref, sems,
    ):
        lat = lax.axis_index("lat")
        last = lax.axis_size("lat") - 1
        lon_odd = lax.rem(lax.axis_index("lon"), 2)
        for s in range(2):
            own = 0 if s == 0 else tile_lon - 2
            at = 2 if s == 0 else 0
            edge_ref[s, :, at : at + 2] = q_ref[:, own : own + 2]
            edge_side_ref[s, :, at : at + 2, :] = side_ref[:, own : own + 2, :]
        for ref, s in ((a_ref, 1 - lon_odd), (b_ref, lon_odd)):
            at = s * 2
            base = count * rows
            total = ref[base : base + count, :].astype(F32) + ref[base + count : base + 2 * count, :].astype(F32)
            for i in range(wide):
                for j in range(2):
                    k = (i * 2 + j) * rows
                    edge_ref[s, i, at + j] = ref[k : k + rows, :]
                    edge_side_ref[s, i, pl.ds(at + j, 1), :] = total[2 * i + j : 2 * i + j + 1, :]

        def grams(i, carry):
            for s in range(2):
                pairs = [pair_of(edge_ref.at[s], i, j) for j in (0, 2)]
                for j, gram in enumerate(row_grams(pairs)):
                    gram_ref[i, s * 2 + j] = gram
            return carry

        lax.fori_loop(0, wide, grams, 0, unroll=True)
        base_gram = identity(members)
        for i in range(tile_lat + 2):
            if i < 2:
                source, k = middle_ref, i
            elif i < tile_lat:
                source, k = inner_ref, i - 2
            else:
                source, k = middle_ref, i - tile_lat + 2
            w_ref[i, 2 : tile_lon] = source[k]
        group = (tile_lat + 2) // 2

        def body(g, carry):
            nodes = [(g * group + r, c) for r in range(group) for c in range(4)]
            sums = [node_sum(base_gram, gram_ref, i, c) for i, c in nodes]
            sides = [near_side(edge_side_ref.at[c // 2], i, c % 2) for i, c in nodes]
            for (i, c), w in zip(nodes, weights_of(sums, sides)):
                outside = jnp.logical_or(
                    jnp.logical_and(i == 0, lat == 0), jnp.logical_and(i == tile_lat + 1, lat == last)
                )
                w_ref[i, (c // 2) * tile_lon + c % 2] = jnp.where(outside, jnp.zeros_like(w), w)
            return carry

        lax.fori_loop(0, 2, body, 0)

        def analyse(i, carry):
            totals = []
            for j in range(tile_lon):
                x = state_ref[i, j].astype(F32)
                mean = jnp.sum(x, axis=1, keepdims=True) * (1.0 / members)
                centred = x - mean
                perturb_ref[j * rows : (j + 1) * rows, :] = centred.astype(BF16)
                totals.append(x - columns_ref[i, 6, j * rows : (j + 1) * rows, :] * centred)
            for n in range(tile_lon + 2):
                low, high = max(n - 2, 0), min(n, tile_lon - 1)
                near = jnp.concatenate([w_ref[i + a, n] for a in range(3)], axis=0)
                out = lax.dot_general(
                    perturb_ref[low * rows : (high + 1) * rows, :],
                    near,
                    (((1,), (1,)), ((), ())),
                    preferred_element_type=F32,
                )
                for j in range(low, high + 1):
                    here = out[(j - low) * rows : (j - low + 1) * rows]
                    span = slice(j * rows, (j + 1) * rows)
                    mixed = 0.0
                    for a in range(3):
                        mixed = mixed + columns_ref[i, a, span, :] * here[:, a * members : (a + 1) * members]
                    totals[j] = totals[j] + columns_ref[i, 3 + n - j, span, :] * mixed
                    if n == j + 2:
                        out_ref[i, j] = totals[j].astype(BF16)
            pltpu.make_async_copy(out_ref.at[i], out_hbm.at[i], sems.at[i]).start()
            return carry

        lax.fori_loop(0, tile_lat, analyse, 0)
        for i in range(tile_lat):
            pltpu.make_async_copy(out_ref.at[i], out_hbm.at[i], sems.at[i]).wait()

    vmem = pl.BlockSpec(memory_space=pltpu.VMEM)
    return pl.pallas_call(
        kernel,
        in_specs=[vmem] * 8,
        out_specs=pl.BlockSpec(memory_space=pltpu.HBM),
        out_shape=jax.ShapeDtypeStruct(state.shape, BF16),
        scratch_shapes=[
            pltpu.VMEM((2, wide, 4, rows, members), BF16),
            pltpu.VMEM((2, wide, 4, members), F32),
            pltpu.VMEM((wide, 4, members, members), F32),
            pltpu.VMEM((tile_lat + 2, tile_lon + 2, members, members), BF16),
            pltpu.VMEM((tile_lon * rows, members), BF16),
            pltpu.VMEM(state.shape, BF16),
            pltpu.SemaphoreType.DMA((tile_lat,)),
        ],
        compiler_params=PARAMS,
        cost_estimate=pl.CostEstimate(flops=10**10, bytes_accessed=3 * 10**6, transcendentals=0),
        name="finish",
    )(state, wide_q, wide_side, got_a, got_b, inner_w, middle_w, columns)


def body(state, obs_row, obs_count, obs_value, obs_weight, quadrant, frac_lat, frac_lon, land):
    tile_lat, tile_lon, rows, members = state.shape
    flat_q, flat_side, send_a, send_b = prepare(state, obs_row, obs_count, obs_value, obs_weight)
    got_a = swap(send_a, "lat", 0, False)
    got_b = swap(send_b, "lat", 1, False)
    q = flat_q.reshape(tile_lat, tile_lon, rows, members)
    side = flat_side.reshape(tile_lat, tile_lon, members)
    inner_w, columns, own_grams = interior(q, side, quadrant, frac_lat, frac_lon, land)
    wide_q, wide_side, to_a, to_b = widen(q, side, got_a, got_b)
    lon_b = swap(to_b, "lon", 1, True)
    lon_a = swap(to_a, "lon", 0, True)
    middle_w = middle(wide_q, wide_side, own_grams)
    return finish(state, wide_q, wide_side, lon_a, lon_b, inner_w, middle_w, columns)


def solution(mesh):
    cell = P("lat", "lon", None)
    return jax.shard_map(
        body,
        mesh=mesh,
        in_specs=(
            P("lat", "lon", None, None), cell, P("lat", "lon"), cell, cell, cell, cell, cell, cell,
        ),
        out_specs=P("lat", "lon", None, None),
        check_vma=False,
    )
```

```python
import math

import jax
import jax.numpy as jnp
from jax import lax
from jax.experimental import pallas as pl
from jax.experimental.pallas import tpu as pltpu
from jax.sharding import PartitionSpec as P

F32 = jnp.float32
BF16 = jnp.bfloat16
ITERS = 6
NEAR = (0.5, 1.0, 0.5)
PARAMS = pltpu.CompilerParams(vmem_limit_bytes=40 * 2**20)


def swap(x, axis, phase, closed):
    count = lax.axis_size(axis)
    pairs = []
    for k in range(phase, count, 2):
        a, b = k, (k + 1) % count
        pairs += [(a, b), (b, a)] if closed or a < b else [(a, a), (b, b)]
    return lax.ppermute(x, axis, pairs)


def split(x):
    high = x.astype(BF16)
    return high, (x - high.astype(F32)).astype(BF16)


def stream(pair):
    return jnp.concatenate(pair, axis=1)


def held(pair):
    row = jnp.concatenate(pair, axis=1)
    return jnp.concatenate([row, row], axis=0)


def product(a, b):
    out = jnp.dot(stream(a), held(b), preferred_element_type=F32)
    half = out.shape[1] // 2
    return out[:, :half] + out[:, half:]


def weights_of(grams, sides):
    members = grams[0].shape[0]
    rows = lax.broadcasted_iota(jnp.int32, (members, members), 0)
    cols = lax.broadcasted_iota(jnp.int32, (members, members), 1)
    eye = jnp.where(rows == cols, F32(1.0), F32(0.0))
    inv_frob = []
    iterates = []
    for gram in grams:
        total = jnp.sum(jnp.sum(gram * gram, axis=0, keepdims=True), axis=1, keepdims=True)
        inverse = lax.rsqrt(total)
        inv_frob.append(inverse)
        iterates.append(gram * inverse)
    first = [split(a) for a in iterates]
    squares, square_parts = iterates, first
    for step in range(0, ITERS, 2):
        inner = [
            product(part, part) + (3.375 * eye - 4.5 * x)
            for part, x in zip(square_parts, squares)
        ]
        inner_parts = [split(x) for x in inner]
        factors = [
            0.0625 * product(part, part) + ((24.609375 / 16) * eye - (8.625 / 16) * x)
            for part, x in zip(inner_parts, squares)
        ]
        factor_parts = [split(x) for x in factors]
        if step == 0:
            roots, root_parts = factors, factor_parts
        else:
            roots = [product(z, x) for z, x in zip(root_parts, factor_parts)]
        if step < ITERS - 2:
            if step > 0:
                root_parts = [split(z) for z in roots]
            half = [split(product(a, z)) for a, z in zip(first, root_parts)]
            squares = [product(x, z) for x, z in zip(half, root_parts)]
            square_parts = [split(x) for x in squares]
    out = []
    for root, side, inverse in zip(roots, sides, inv_frob):
        inner = jnp.sum(root * side, axis=1, keepdims=True)
        mean_weight = jnp.sum(root * inner, axis=0, keepdims=True) * inverse
        out.append((mean_weight + (math.sqrt(members - 1) * jnp.sqrt(inverse)) * root).astype(BF16))
    return out


def row_grams(pairs):
    turned = [pair.T for pair in pairs]
    rows = pairs[0].shape[0] // 2
    half = BF16(0.5)
    out = []
    for p in range(len(pairs) - 1):
        first, second = pairs[p], pairs[p + 1]
        zero = jnp.zeros((rows, first.shape[1]), BF16)
        left = jnp.concatenate([first[:rows] * half, first[rows:], second[:rows] * half, zero], axis=0)
        right = jnp.concatenate([zero, first[rows:] * half, second[:rows], second[rows:] * half], axis=0)
        both = jnp.dot(
            jnp.concatenate(turned[p : p + 2], axis=1),
            jnp.concatenate([left, right], axis=1),
            preferred_element_type=F32,
        )
        members = both.shape[0]
        out += [both[:, :members], both[:, members:]]
    return out


def pair_of(ref, i, j):
    pair = ref[i, j : j + 2]
    return pair.reshape(2 * pair.shape[1], pair.shape[2])


def node_sum(base, gram_ref, i, j):
    return base + 0.5 * (gram_ref[i, j] + gram_ref[i + 2, j]) + gram_ref[i + 1, j]


def near_side(side_ref, i, j):
    total = 0.0
    for a in range(3):
        for b in range(3):
            total = total + NEAR[a] * NEAR[b] * side_ref[i + a, j + b : j + b + 1, :]
    return total


def identity(members):
    rows = lax.broadcasted_iota(jnp.int32, (members, members), 0)
    cols = lax.broadcasted_iota(jnp.int32, (members, members), 1)
    return jnp.where(rows == cols, F32(members - 1), F32(0.0))


def pack_side(ref, at, side):
    high = side.astype(BF16).astype(F32)
    ref[at : at + 2 * side.shape[0], :] = jnp.concatenate([high, side - high], axis=0).astype(BF16)


def unpack_side(ref, at, count):
    both = ref[at : at + 2 * count, :].astype(F32)
    return both[:count] + both[count:]


def prepare(state, obs_row, obs_count, obs_value, obs_weight):
    tile_lat, tile_lon, rows, members = state.shape
    slots = obs_row.shape[2]
    cells = tile_lat * tile_lon
    payload = tile_lon * rows + 2 * tile_lon

    def kernel(
        count_hbm, state_hbm, row_hbm, value_hbm, weight_hbm,
        q_ref, side_ref, a_in_ref, b_in_ref, a_out_ref, b_out_ref,
        count_ref, state_ref, row_ref, value_ref, weight_ref, sems,
    ):
        copies = [
            pltpu.make_async_copy(source, target, sems.at[k])
            for k, (source, target) in enumerate(
                (
                    (count_hbm, count_ref),
                    (row_hbm, row_ref),
                    (value_hbm, value_ref),
                    (weight_hbm, weight_ref),
                )
            )
        ]
        row_copies = [
            pltpu.make_async_copy(state_hbm.at[i], state_ref.at[i], sems.at[4 + i]) for i in range(tile_lat)
        ]
        for copy in copies + row_copies:
            copy.start()
        lane = lax.broadcasted_iota(jnp.int32, (1, slots), 1)
        row_ids = lax.broadcasted_iota(jnp.int32, (rows, slots), 0)
        for copy in copies:
            copy.wait()

        for i in range(tile_lat):
            row_copies[i].wait()
            for j in range(tile_lon):
                x = state_ref[i, j].astype(F32)
                mean = jnp.sum(x, axis=1, keepdims=True) * (1.0 / members)
                centred = x - mean
                live = jnp.where(lane < count_ref[i, j], weight_ref[i, j : j + 1, :], 0.0)
                hit = row_ids == row_ref[i, j : j + 1, :]
                centre = jnp.sum(jnp.where(hit, mean, 0.0), axis=0, keepdims=True)
                innovation = ((value_ref[i, j : j + 1, :] - centre) * live).astype(BF16).astype(F32)
                square = jnp.sum(jnp.where(hit, live * live, 0.0), axis=1, keepdims=True)
                pull = jnp.sum(jnp.where(hit, live * innovation, 0.0), axis=1, keepdims=True)
                start = (i * tile_lon + j) * rows
                q_ref[start : start + rows, :] = (centred * jnp.sqrt(square)).astype(BF16)
                side_ref[i * tile_lon + j : i * tile_lon + j + 1, :] = jnp.sum(
                    centred * pull, axis=0, keepdims=True
                )
        odd = lax.rem(lax.axis_index("lat"), 2)
        for ref, row in (
            (a_in_ref, (1 - odd) * (tile_lat - 1)),
            (b_in_ref, odd * (tile_lat - 1)),
            (a_out_ref, 1 + (1 - odd) * (tile_lat - 3)),
            (b_out_ref, 1 + odd * (tile_lat - 3)),
        ):
            start = pl.multiple_of(row * tile_lon * rows, tile_lon * rows)
            ref[: tile_lon * rows, :] = q_ref[pl.ds(start, tile_lon * rows), :]
            start = pl.multiple_of(row * tile_lon, tile_lon)
            pack_side(ref, tile_lon * rows, side_ref[pl.ds(start, tile_lon), :])

    vmem = pl.BlockSpec(memory_space=pltpu.VMEM)
    hbm = pl.BlockSpec(memory_space=pltpu.HBM)
    return pl.pallas_call(
        kernel,
        in_specs=[hbm] * 5,
        out_specs=[vmem] * 6,
        out_shape=[
            jax.ShapeDtypeStruct((cells * rows, members), BF16),
            jax.ShapeDtypeStruct((cells, members), F32),
        ]
        + [jax.ShapeDtypeStruct((payload, members), BF16)] * 4,
        scratch_shapes=[
            pltpu.SMEM(obs_count.shape, obs_count.dtype),
            pltpu.VMEM(state.shape, state.dtype),
            pltpu.VMEM(obs_row.shape, obs_row.dtype),
            pltpu.VMEM(obs_value.shape, obs_value.dtype),
            pltpu.VMEM(obs_weight.shape, obs_weight.dtype),
            pltpu.SemaphoreType.DMA((4 + tile_lat,)),
        ],
        compiler_params=PARAMS,
        cost_estimate=pl.CostEstimate(flops=10**8, bytes_accessed=2 * 10**6, transcendentals=0),
        name="prepare",
    )(*[
        pltpu.with_memory_space_constraint(x, pltpu.HBM)
        for x in (obs_count, state, obs_row, obs_value, obs_weight)
    ])


def interior(q, side, quadrant, frac_lat, frac_lon, land):
    tile_lat, tile_lon, rows, members = q.shape

    def kernel(
        q_ref, side_ref, quad_hbm, flat_hbm, flon_hbm, land_hbm, out_ref, columns_ref, gram_ref,
        coef_ref, quad_ref, flat_ref, flon_ref, land_ref, sems,
    ):
        copies = [
            pltpu.make_async_copy(source, target, sems.at[k])
            for k, (source, target) in enumerate(
                ((quad_hbm, quad_ref), (flat_hbm, flat_ref), (flon_hbm, flon_ref), (land_hbm, land_ref))
            )
        ]
        for copy in copies:
            copy.start()

        def grams(i, carry):
            pairs = [pair_of(q_ref, i, j) for j in range(0, tile_lon, 2)]
            for j, gram in enumerate(row_grams(pairs)):
                gram_ref[i, j] = gram
            return carry

        lax.fori_loop(0, tile_lat, grams, 0, unroll=True)
        base = identity(members)
        nodes = [(i, j) for i in range(tile_lat - 2) for j in range(tile_lon - 2)]
        sums = [node_sum(base, gram_ref, i, j) for i, j in nodes]
        sides = [near_side(side_ref, i, j) for i, j in nodes]
        for (i, j), w in zip(nodes, weights_of(sums, sides)):
            out_ref[i, j] = w

        coef_ref[...] = jnp.zeros_like(coef_ref)
        for copy in copies:
            copy.wait()

        def columns(i, carry):
            quad = quad_ref[i]
            fa, fo = flat_ref[i], flon_ref[i]
            dry = jnp.where(land_ref[i] == 1, F32(1.0), F32(0.0))
            north, west = quad < 2, lax.rem(quad, 2) == 0
            zero = jnp.zeros_like(fa)
            coefs = (
                jnp.where(north, 1.0 - fa, zero) * dry,
                jnp.where(north, fa, 1.0 - fa) * dry,
                jnp.where(north, zero, fa) * dry,
                jnp.where(west, 1.0 - fo, zero),
                jnp.where(west, fo, 1.0 - fo),
                jnp.where(west, zero, fo),
                dry,
            )
            for k, coef in enumerate(coefs):
                coef_ref[k * tile_lon : (k + 1) * tile_lon, :rows] = coef
            turned = coef_ref[...].T
            for k in range(len(coefs)):
                for j in range(tile_lon):
                    at = k * tile_lon + j
                    columns_ref[i, k, j * rows : (j + 1) * rows, :] = jnp.broadcast_to(
                        turned[:rows, at : at + 1], (rows, members)
                    )
            return carry

        lax.fori_loop(0, tile_lat, columns, 0)

    vmem = pl.BlockSpec(memory_space=pltpu.VMEM)
    return pl.pallas_call(
        kernel,
        in_specs=[vmem] * 2 + [pl.BlockSpec(memory_space=pltpu.HBM)] * 4,
        out_specs=[vmem] * 3,
        out_shape=[
            jax.ShapeDtypeStruct((tile_lat - 2, tile_lon - 2, members, members), BF16),
            jax.ShapeDtypeStruct((tile_lat, 7, tile_lon * rows, members), F32),
            jax.ShapeDtypeStruct((tile_lat, tile_lon - 2, members, members), F32),
        ],
        scratch_shapes=[pltpu.VMEM((128, 128), F32)]
        + [pltpu.VMEM(x.shape, x.dtype) for x in (quadrant, frac_lat, frac_lon, land)]
        + [pltpu.SemaphoreType.DMA((4,))],
        compiler_params=PARAMS,
        cost_estimate=pl.CostEstimate(flops=5 * 10**9, bytes_accessed=2 * 10**6, transcendentals=0),
        name="interior",
    )(
        q, side,
        *[pltpu.with_memory_space_constraint(x, pltpu.HBM) for x in (quadrant, frac_lat, frac_lon, land)],
    )


def rim(q, side, own_grams, got_a, got_b):
    tile_lat, tile_lon, rows, members = q.shape
    inner = tile_lon - 2

    def kernel(side_ref, own_ref, a_ref, b_ref, out_ref, gram_ref, near_ref):
        lat = lax.axis_index("lat")
        odd = lax.rem(lat, 2) == 1
        last = lax.axis_size("lat") - 1
        near_ref[1 : 1 + tile_lat] = side_ref[...]
        a_side = unpack_side(a_ref, tile_lon * rows, tile_lon)
        b_side = unpack_side(b_ref, tile_lon * rows, tile_lon)
        for k, from_a, valid in ((0, odd, lat > 0), (1, jnp.logical_not(odd), lat < last)):
            near_ref[k * (tile_lat + 1)] = jnp.where(valid, jnp.where(from_a, a_side, b_side), 0.0)
            pairs = []
            for j in range(0, tile_lon, 2):
                span = slice(j * rows, (j + 2) * rows)
                pair = jnp.where(from_a, a_ref[span, :], b_ref[span, :])
                pairs.append(jnp.where(valid, pair, jnp.zeros_like(pair)))
            for j, gram in enumerate(row_grams(pairs)):
                gram_ref[k, j] = gram
        base = identity(members)
        nodes = [(k, j) for k in range(2) for j in range(inner)]
        sums = []
        for k, j in nodes:
            i, beside = (0, 1) if k == 0 else (tile_lat - 1, tile_lat - 2)
            sums.append(base + 0.5 * (gram_ref[k, j] + own_ref[beside, j]) + own_ref[i, j])
        sides = [near_side(near_ref, k * (tile_lat - 1), j) for k, j in nodes]
        for (k, j), w in zip(nodes, weights_of(sums, sides)):
            out_ref[k, j] = w

    vmem = pl.BlockSpec(memory_space=pltpu.VMEM)
    return pl.pallas_call(
        kernel,
        in_specs=[vmem] * 4,
        out_specs=[vmem] * 2,
        out_shape=[
            jax.ShapeDtypeStruct((2, inner, members, members), BF16),
            jax.ShapeDtypeStruct((2, inner, members, members), F32),
        ],
        scratch_shapes=[pltpu.VMEM((tile_lat + 2, tile_lon, members), F32)],
        compiler_params=PARAMS,
        cost_estimate=pl.CostEstimate(flops=5 * 10**9, bytes_accessed=2 * 10**6, transcendentals=0),
        name="rim",
    )(side, own_grams, got_a, got_b)


def widen(q, side, got, after):
    tile_lat, tile_lon, rows, members = q.shape
    wide = tile_lat + 4
    count = 2 * wide
    payload = count * rows + 2 * count

    def kernel(
        q_ref, side_ref, a_in_ref, b_in_ref, a_out_ref, b_out_ref, after_ref,
        wide_ref, wide_side_ref, to_a_ref, to_b_ref,
    ):
        lat = lax.axis_index("lat")
        lon = lax.axis_index("lon")
        lat_odd = lax.rem(lat, 2)
        lon_odd = lax.rem(lon, 2)
        wide_ref[2 : 2 + tile_lat] = q_ref[...]
        wide_side_ref[2 : 2 + tile_lat] = side_ref[...]
        last = lax.axis_size("lat") - 1
        a_valid = jnp.where(lat_odd == 0, lat < last, lat > 0)
        b_valid = jnp.where(lat_odd == 0, lat > 0, lat < last)
        for ref, row, valid in (
            (a_in_ref, 1 + (1 - lat_odd) * (tile_lat + 1), a_valid),
            (b_in_ref, 1 + lat_odd * (tile_lat + 1), b_valid),
            (a_out_ref, (1 - lat_odd) * (tile_lat + 3), a_valid),
            (b_out_ref, lat_odd * (tile_lat + 3), b_valid),
        ):
            for j in range(tile_lon):
                piece = ref[j * rows : (j + 1) * rows, :]
                wide_ref[row, j] = jnp.where(valid, piece, jnp.zeros_like(piece))
            wide_side_ref[row] = jnp.where(valid, unpack_side(ref, tile_lon * rows, tile_lon), 0.0)
        for ref, first in ((to_a_ref, (1 - lon_odd) * (tile_lon - 2)), (to_b_ref, lon_odd * (tile_lon - 2))):
            collected = []
            for i in range(wide):
                for j in range(2):
                    k = (i * 2 + j) * rows
                    ref[k : k + rows, :] = wide_ref[i, first + j]
                    collected.append(wide_side_ref[i, pl.ds(first + j, 1), :])
            pack_side(ref, count * rows, jnp.concatenate(collected, axis=0))

    vmem = pl.BlockSpec(memory_space=pltpu.VMEM)
    return pl.pallas_call(
        kernel,
        in_specs=[vmem] * 6 + [pl.BlockSpec(memory_space=pl.ANY)],
        out_specs=[vmem] * 4,
        out_shape=[
            jax.ShapeDtypeStruct((wide, tile_lon, rows, members), BF16),
            jax.ShapeDtypeStruct((wide, tile_lon, members), F32),
            jax.ShapeDtypeStruct((payload, members), BF16),
            jax.ShapeDtypeStruct((payload, members), BF16),
        ],
        compiler_params=PARAMS,
        cost_estimate=pl.CostEstimate(flops=10**6, bytes_accessed=3 * 10**6, transcendentals=0),
        name="widen",
    )(q, side, *got, after)


def beyond(wide_q, wide_side, own_grams, rim_grams):
    wide, tile_lon, rows, members = wide_q.shape
    tile_lat = wide - 4
    inner = tile_lon - 2

    def kernel(q_ref, side_ref, own_ref, rim_ref, out_ref):
        lat = lax.axis_index("lat")
        last = lax.axis_size("lat") - 1
        base = identity(members)
        sums, sides, outside = [], [], []
        for k, far, own, absent in ((0, 0, 0, lat == 0), (1, wide - 1, tile_lat - 1, lat == last)):
            pairs = [pair_of(q_ref, far, j) for j in range(0, tile_lon, 2)]
            for j, gram in enumerate(row_grams(pairs)):
                sums.append(base + 0.5 * (gram + own_ref[own, j]) + rim_ref[k, j])
                sides.append(near_side(side_ref, k * (tile_lat + 1), j))
                outside.append(absent)
        for n, w in enumerate(weights_of(sums, sides)):
            out_ref[n // inner, n % inner] = jnp.where(outside[n], jnp.zeros_like(w), w)

    vmem = pl.BlockSpec(memory_space=pltpu.VMEM)
    return pl.pallas_call(
        kernel,
        in_specs=[vmem] * 4,
        out_specs=vmem,
        out_shape=jax.ShapeDtypeStruct((2, inner, members, members), BF16),
        compiler_params=PARAMS,
        cost_estimate=pl.CostEstimate(flops=5 * 10**9, bytes_accessed=3 * 10**6, transcendentals=0),
        name="beyond",
    )(wide_q, wide_side, own_grams, rim_grams)


def edge_weights(q_ref, side_ref, got_ref, edge, edge_ref, edge_side_ref, store):
    wide, tile_lon, rows, members = q_ref.shape
    tile_lat = wide - 4
    lat = lax.axis_index("lat")
    last = lax.axis_size("lat") - 1
    own, at = edge * (tile_lon - 2), edge * 2
    got_side = unpack_side(got_ref, 2 * wide * rows, 2 * wide)
    for i in range(wide):
        for j in range(2):
            k = (i * 2 + j) * rows
            edge_ref[i, at + j] = got_ref[k : k + rows, :]
            edge_ref[i, 2 - at + j] = q_ref[i, own + j]
        got_part = got_side[2 * i : 2 * i + 2]
        own_part = jnp.where(edge == 0, side_ref[i, :2, :], side_ref[i, tile_lon - 2 :, :])
        edge_side_ref[i, :2, :] = jnp.where(edge == 0, got_part, own_part)
        edge_side_ref[i, 2:, :] = jnp.where(edge == 0, own_part, got_part)
    grams = [row_grams([pair_of(edge_ref, i, 0), pair_of(edge_ref, i, 2)]) for i in range(wide)]
    base = identity(members)
    nodes = [(i, j) for i in range(tile_lat + 2) for j in range(2)]
    sums = [base + 0.5 * (grams[i][j] + grams[i + 2][j]) + grams[i + 1][j] for i, j in nodes]
    sides = [near_side(edge_side_ref, i, j) for i, j in nodes]
    for (i, j), w in zip(nodes, weights_of(sums, sides)):
        if i == 0:
            w = jnp.where(lat == 0, jnp.zeros_like(w), w)
        if i == tile_lat + 1:
            w = jnp.where(lat == last, jnp.zeros_like(w), w)
        store(i, j, w)


def edge_scratch(wide, rows, members):
    return [pltpu.VMEM((wide, 4, rows, members), BF16), pltpu.VMEM((wide, 4, members), F32)]


def near_edge(wide_q, wide_side, got_a):
    wide, tile_lon, rows, members = wide_q.shape

    def kernel(q_ref, side_ref, a_ref, out_ref, edge_ref, edge_side_ref):
        def store(i, j, w):
            out_ref[i, j] = w

        edge = 1 - lax.rem(lax.axis_index("lon"), 2)
        edge_weights(q_ref, side_ref, a_ref, edge, edge_ref, edge_side_ref, store)

    vmem = pl.BlockSpec(memory_space=pltpu.VMEM)
    return pl.pallas_call(
        kernel,
        in_specs=[vmem] * 3,
        out_specs=vmem,
        out_shape=jax.ShapeDtypeStruct((wide - 2, 2, members, members), BF16),
        scratch_shapes=edge_scratch(wide, rows, members),
        compiler_params=PARAMS,
        cost_estimate=pl.CostEstimate(flops=5 * 10**9, bytes_accessed=3 * 10**6, transcendentals=0),
        name="near_edge",
    )(wide_q, wide_side, got_a)


def finish(state, wide_q, wide_side, got_b, inner_w, rim_w, beyond_w, near_w, columns):
    tile_lat, tile_lon, rows, members = state.shape
    wide = tile_lat + 4

    def kernel(
        state_ref, q_ref, side_ref, b_ref, inner_ref, rim_ref, beyond_ref, near_ref, columns_ref,
        out_hbm, edge_ref, edge_side_ref, w_ref, perturb_ref, out_ref, sems,
    ):
        edge = lax.rem(lax.axis_index("lon"), 2)

        def store(i, j, w):
            w_ref[i, edge * tile_lon + j] = w

        edge_weights(q_ref, side_ref, b_ref, edge, edge_ref, edge_side_ref, store)
        for i in range(tile_lat + 2):
            if i in (0, tile_lat + 1):
                source, k = beyond_ref, min(i, 1)
            elif i in (1, tile_lat):
                source, k = rim_ref, min(i - 1, 1)
            else:
                source, k = inner_ref, i - 2
            w_ref[i, 2:tile_lon] = source[k]
            for j in range(2):
                w_ref[i, (1 - edge) * tile_lon + j] = near_ref[i, j]

        def analyse(i, carry):
            totals = []
            for j in range(tile_lon):
                x = state_ref[i, j].astype(F32)
                mean = jnp.sum(x, axis=1, keepdims=True) * (1.0 / members)
                centred = x - mean
                perturb_ref[j * rows : (j + 1) * rows, :] = centred.astype(BF16)
                totals.append(x - columns_ref[i, 6, j * rows : (j + 1) * rows, :] * centred)
            for n in range(tile_lon + 2):
                low, high = max(n - 2, 0), min(n, tile_lon - 1)
                near = jnp.concatenate([w_ref[i + a, n] for a in range(3)], axis=0)
                out = lax.dot_general(
                    perturb_ref[low * rows : (high + 1) * rows, :],
                    near,
                    (((1,), (1,)), ((), ())),
                    preferred_element_type=F32,
                )
                for j in range(low, high + 1):
                    here = out[(j - low) * rows : (j - low + 1) * rows]
                    span = slice(j * rows, (j + 1) * rows)
                    mixed = 0.0
                    for a in range(3):
                        mixed = mixed + columns_ref[i, a, span, :] * here[:, a * members : (a + 1) * members]
                    totals[j] = totals[j] + columns_ref[i, 3 + n - j, span, :] * mixed
                    if n == j + 2:
                        out_ref[i, j] = totals[j].astype(BF16)
            pltpu.make_async_copy(out_ref.at[i], out_hbm.at[i], sems.at[i]).start()
            return carry

        lax.fori_loop(0, tile_lat, analyse, 0)
        for i in range(tile_lat):
            pltpu.make_async_copy(out_ref.at[i], out_hbm.at[i], sems.at[i]).wait()

    vmem = pl.BlockSpec(memory_space=pltpu.VMEM)
    return pl.pallas_call(
        kernel,
        in_specs=[vmem] * 9,
        out_specs=pl.BlockSpec(memory_space=pltpu.HBM),
        out_shape=jax.ShapeDtypeStruct(state.shape, BF16),
        scratch_shapes=edge_scratch(wide, rows, members)
        + [
            pltpu.VMEM((tile_lat + 2, tile_lon + 2, members, members), BF16),
            pltpu.VMEM((tile_lon * rows, members), BF16),
            pltpu.VMEM(state.shape, BF16),
            pltpu.SemaphoreType.DMA((tile_lat,)),
        ],
        compiler_params=PARAMS,
        cost_estimate=pl.CostEstimate(flops=10**10, bytes_accessed=3 * 10**6, transcendentals=0),
        name="finish",
    )(state, wide_q, wide_side, got_b, inner_w, rim_w, beyond_w, near_w, columns)


def body(state, obs_row, obs_count, obs_value, obs_weight, quadrant, frac_lat, frac_lon, land):
    tile_lat, tile_lon, rows, members = state.shape
    flat_q, flat_side, a_in, b_in, a_out, b_out = prepare(
        state, obs_row, obs_count, obs_value, obs_weight
    )
    a_in = swap(a_in, "lat", 0, False)
    b_in = swap(b_in, "lat", 1, False)
    a_out = swap(a_out, "lat", 0, False)
    b_out = swap(b_out, "lat", 1, False)
    q = flat_q.reshape(tile_lat, tile_lon, rows, members)
    side = flat_side.reshape(tile_lat, tile_lon, members)
    inner_w, columns, own_grams = interior(q, side, quadrant, frac_lat, frac_lon, land)
    rim_w, rim_grams = rim(q, side, own_grams, a_in, b_in)
    wide_q, wide_side, to_a, to_b = widen(q, side, (a_in, b_in, a_out, b_out), rim_grams)
    lon_b = swap(to_b, "lon", 1, True)
    lon_a = swap(to_a, "lon", 0, True)
    beyond_w = beyond(wide_q, wide_side, own_grams, rim_grams)
    near_w = near_edge(wide_q, wide_side, lon_a)
    return finish(state, wide_q, wide_side, lon_b, inner_w, rim_w, beyond_w, near_w, columns)


def solution(mesh):
    cell = P("lat", "lon", None)
    return jax.shard_map(
        body,
        mesh=mesh,
        in_specs=(
            P("lat", "lon", None, None), cell, P("lat", "lon"), cell, cell, cell, cell, cell, cell,
        ),
        out_specs=P("lat", "lon", None, None),
        check_vma=False,
    )
```

```python
import math

import jax
import jax.numpy as jnp
from jax import lax
from jax.experimental import pallas as pl
from jax.experimental.pallas import tpu as pltpu
from jax.sharding import PartitionSpec as P

F32 = jnp.float32
BF16 = jnp.bfloat16
ITERS = 6
NEAR = (0.5, 1.0, 0.5)
PARAMS = pltpu.CompilerParams(vmem_limit_bytes=40 * 2**20)


def swap(x, axis, phase):
    count = lax.axis_size(axis)
    pairs = []
    for k in range(phase, count, 2):
        a, b = k, (k + 1) % count
        pairs += [(a, b), (b, a)]
    return lax.ppermute(x, axis, pairs)


def swap_inner_lat(x):
    lats, lons = lax.axis_size("lat"), lax.axis_size("lon")
    pairs = []
    for j in range(lons):
        for k in range(1, lats - 1, 2):
            a, b = k * lons + j, (k + 1) * lons + j
            pairs += [(a, b), (b, a)]
        for k in (0, lats - 1):
            pairs.append((k * lons + j, k * lons + (j ^ 1)))
    return lax.ppermute(x, ("lat", "lon"), pairs)


def split(x):
    high = x.astype(BF16)
    return high, (x - high.astype(F32)).astype(BF16)


def stream(pair):
    return jnp.concatenate(pair, axis=1)


def held(pair):
    row = jnp.concatenate(pair, axis=1)
    return jnp.concatenate([row, row], axis=0)


def product(a, b):
    out = jnp.dot(stream(a), held(b), preferred_element_type=F32)
    half = out.shape[1] // 2
    return out[:, :half] + out[:, half:]


def weights_of(grams, sides):
    members = grams[0].shape[0]
    rows = lax.broadcasted_iota(jnp.int32, (members, members), 0)
    cols = lax.broadcasted_iota(jnp.int32, (members, members), 1)
    eye = jnp.where(rows == cols, F32(1.0), F32(0.0))
    inv_frob = []
    iterates = []
    for gram in grams:
        total = jnp.sum(jnp.sum(gram * gram, axis=0, keepdims=True), axis=1, keepdims=True)
        inverse = lax.rsqrt(total)
        inv_frob.append(inverse)
        iterates.append(gram * inverse)
    first = [split(a) for a in iterates]
    squares, square_parts = iterates, first
    for step in range(0, ITERS, 2):
        inner = [
            product(part, part) + (3.375 * eye - 4.5 * x)
            for part, x in zip(square_parts, squares)
        ]
        inner_parts = [split(x) for x in inner]
        factors = [
            0.0625 * product(part, part) + ((24.609375 / 16) * eye - (8.625 / 16) * x)
            for part, x in zip(inner_parts, squares)
        ]
        factor_parts = [split(x) for x in factors]
        if step == 0:
            roots, root_parts = factors, factor_parts
        else:
            roots = [product(z, x) for z, x in zip(root_parts, factor_parts)]
        if step < ITERS - 2:
            if step > 0:
                root_parts = [split(z) for z in roots]
            half = [split(product(a, z)) for a, z in zip(first, root_parts)]
            squares = [product(x, z) for x, z in zip(half, root_parts)]
            square_parts = [split(x) for x in squares]
    out = []
    for root, side, inverse in zip(roots, sides, inv_frob):
        inner = jnp.sum(root * side, axis=1, keepdims=True)
        mean_weight = jnp.sum(root * inner, axis=0, keepdims=True) * inverse
        out.append((mean_weight + (math.sqrt(members - 1) * jnp.sqrt(inverse)) * root).astype(BF16))
    return out


def row_grams(pairs):
    turned = [pair.T for pair in pairs]
    rows = pairs[0].shape[0] // 2
    half = BF16(0.5)
    out = []
    for p in range(len(pairs) - 1):
        first, second = pairs[p], pairs[p + 1]
        zero = jnp.zeros((rows, first.shape[1]), BF16)
        left = jnp.concatenate([first[:rows] * half, first[rows:], second[:rows] * half, zero], axis=0)
        right = jnp.concatenate([zero, first[rows:] * half, second[:rows], second[rows:] * half], axis=0)
        both = jnp.dot(
            jnp.concatenate(turned[p : p + 2], axis=1),
            jnp.concatenate([left, right], axis=1),
            preferred_element_type=F32,
        )
        members = both.shape[0]
        out += [both[:, :members], both[:, members:]]
    return out


def pair_of(ref, i, j):
    pair = ref[i, j : j + 2]
    return pair.reshape(2 * pair.shape[1], pair.shape[2])


def node_sum(base, gram_ref, i, j):
    return base + 0.5 * (gram_ref[i, j] + gram_ref[i + 2, j]) + gram_ref[i + 1, j]


def near_side(side_ref, i, j):
    total = 0.0
    for a in range(3):
        for b in range(3):
            total = total + NEAR[a] * NEAR[b] * side_ref[i + a, j + b : j + b + 1, :]
    return total


def identity(members):
    rows = lax.broadcasted_iota(jnp.int32, (members, members), 0)
    cols = lax.broadcasted_iota(jnp.int32, (members, members), 1)
    return jnp.where(rows == cols, F32(members - 1), F32(0.0))


def pack_side(ref, at, side):
    high = side.astype(BF16).astype(F32)
    ref[at : at + 2 * side.shape[0], :] = jnp.concatenate([high, side - high], axis=0).astype(BF16)


def unpack_side(ref, at, count):
    both = ref[at : at + 2 * count, :].astype(F32)
    return both[:count] + both[count:]


def prepare(state, obs_row, obs_count, obs_value, obs_weight):
    tile_lat, tile_lon, rows, members = state.shape
    slots = obs_row.shape[2]
    cells = tile_lat * tile_lon
    half = tile_lat // 2 * tile_lon
    payload = half * rows + 2 * half

    def kernel(
        count_hbm, state_hbm, row_hbm, value_hbm, weight_hbm,
        q_ref, side_ref, a_ref, b_ref,
        count_ref, state_ref, row_ref, value_ref, weight_ref, sems,
    ):
        copies = [
            pltpu.make_async_copy(source, target, sems.at[k])
            for k, (source, target) in enumerate(
                (
                    (count_hbm, count_ref),
                    (row_hbm, row_ref),
                    (value_hbm, value_ref),
                    (weight_hbm, weight_ref),
                )
            )
        ]
        row_copies = [
            pltpu.make_async_copy(state_hbm.at[i], state_ref.at[i], sems.at[4 + i]) for i in range(tile_lat)
        ]
        for copy in copies + row_copies:
            copy.start()
        lane = lax.broadcasted_iota(jnp.int32, (1, slots), 1)
        row_ids = lax.broadcasted_iota(jnp.int32, (rows, slots), 0)
        for copy in copies:
            copy.wait()

        for i in range(tile_lat):
            row_copies[i].wait()
            for j in range(tile_lon):
                x = state_ref[i, j].astype(F32)
                mean = jnp.sum(x, axis=1, keepdims=True) * (1.0 / members)
                centred = x - mean
                live = jnp.where(lane < count_ref[i, j], weight_ref[i, j : j + 1, :], 0.0)
                hit = row_ids == row_ref[i, j : j + 1, :]
                centre = jnp.sum(jnp.where(hit, mean, 0.0), axis=0, keepdims=True)
                innovation = ((value_ref[i, j : j + 1, :] - centre) * live).astype(BF16).astype(F32)
                square = jnp.sum(jnp.where(hit, live * live, 0.0), axis=1, keepdims=True)
                pull = jnp.sum(jnp.where(hit, live * innovation, 0.0), axis=1, keepdims=True)
                start = (i * tile_lon + j) * rows
                q_ref[start : start + rows, :] = (centred * jnp.sqrt(square)).astype(BF16)
                side_ref[i * tile_lon + j : i * tile_lon + j + 1, :] = jnp.sum(
                    centred * pull, axis=0, keepdims=True
                )
        odd = lax.rem(lax.axis_index("lat"), 2)
        for ref, first in ((a_ref, 1 - odd), (b_ref, odd)):
            start = pl.multiple_of(first * half * rows, half * rows)
            ref[: half * rows, :] = q_ref[pl.ds(start, half * rows), :]
            start = pl.multiple_of(first * half, half)
            pack_side(ref, half * rows, side_ref[pl.ds(start, half), :])

    vmem = pl.BlockSpec(memory_space=pltpu.VMEM)
    hbm = pl.BlockSpec(memory_space=pltpu.HBM)
    return pl.pallas_call(
        kernel,
        in_specs=[hbm] * 5,
        out_specs=[vmem] * 4,
        out_shape=[
            jax.ShapeDtypeStruct((cells * rows, members), BF16),
            jax.ShapeDtypeStruct((cells, members), F32),
        ]
        + [jax.ShapeDtypeStruct((payload, members), BF16)] * 2,
        scratch_shapes=[
            pltpu.SMEM(obs_count.shape, obs_count.dtype),
            pltpu.VMEM(state.shape, state.dtype),
            pltpu.VMEM(obs_row.shape, obs_row.dtype),
            pltpu.VMEM(obs_value.shape, obs_value.dtype),
            pltpu.VMEM(obs_weight.shape, obs_weight.dtype),
            pltpu.SemaphoreType.DMA((4 + tile_lat,)),
        ],
        compiler_params=PARAMS,
        cost_estimate=pl.CostEstimate(flops=10**8, bytes_accessed=2 * 10**6, transcendentals=0),
        name="prepare",
    )(*[
        pltpu.with_memory_space_constraint(x, pltpu.HBM)
        for x in (obs_count, state, obs_row, obs_value, obs_weight)
    ])


def interior(q, side, quadrant, frac_lat, frac_lon, land):
    tile_lat, tile_lon, rows, members = q.shape

    def kernel(
        q_ref, side_ref, quad_hbm, flat_hbm, flon_hbm, land_hbm, out_ref, columns_ref, gram_ref,
        coef_ref, quad_ref, flat_ref, flon_ref, land_ref, sems,
    ):
        copies = [
            pltpu.make_async_copy(source, target, sems.at[k])
            for k, (source, target) in enumerate(
                ((quad_hbm, quad_ref), (flat_hbm, flat_ref), (flon_hbm, flon_ref), (land_hbm, land_ref))
            )
        ]
        for copy in copies:
            copy.start()

        def grams(i, carry):
            pairs = [pair_of(q_ref, i, j) for j in range(0, tile_lon, 2)]
            for j, gram in enumerate(row_grams(pairs)):
                gram_ref[i, j] = gram
            return carry

        lax.fori_loop(0, tile_lat, grams, 0, unroll=True)
        base = identity(members)
        nodes = [(i, j) for i in range(tile_lat - 2) for j in range(tile_lon - 2)]
        sums = [node_sum(base, gram_ref, i, j) for i, j in nodes]
        sides = [near_side(side_ref, i, j) for i, j in nodes]
        for (i, j), w in zip(nodes, weights_of(sums, sides)):
            out_ref[i, j] = w

        coef_ref[...] = jnp.zeros_like(coef_ref)
        for copy in copies:
            copy.wait()

        def columns(i, carry):
            quad = quad_ref[i]
            fa, fo = flat_ref[i], flon_ref[i]
            dry = jnp.where(land_ref[i] == 1, F32(1.0), F32(0.0))
            north, west = quad < 2, lax.rem(quad, 2) == 0
            zero = jnp.zeros_like(fa)
            coefs = (
                jnp.where(north, 1.0 - fa, zero) * dry,
                jnp.where(north, fa, 1.0 - fa) * dry,
                jnp.where(north, zero, fa) * dry,
                jnp.where(west, 1.0 - fo, zero),
                jnp.where(west, fo, 1.0 - fo),
                jnp.where(west, zero, fo),
                dry,
            )
            for k, coef in enumerate(coefs):
                coef_ref[k * tile_lon : (k + 1) * tile_lon, :rows] = coef
            turned = coef_ref[...].T
            for k in range(len(coefs)):
                for j in range(tile_lon):
                    at = k * tile_lon + j
                    columns_ref[i, k, j * rows : (j + 1) * rows, :] = jnp.broadcast_to(
                        turned[:rows, at : at + 1], (rows, members)
                    )
            return carry

        lax.fori_loop(0, tile_lat, columns, 0)

    vmem = pl.BlockSpec(memory_space=pltpu.VMEM)
    return pl.pallas_call(
        kernel,
        in_specs=[vmem] * 2 + [pl.BlockSpec(memory_space=pltpu.HBM)] * 4,
        out_specs=[vmem] * 3,
        out_shape=[
            jax.ShapeDtypeStruct((tile_lat - 2, tile_lon - 2, members, members), BF16),
            jax.ShapeDtypeStruct((tile_lat, 7, tile_lon * rows, members), F32),
            jax.ShapeDtypeStruct((tile_lat, tile_lon - 2, members, members), F32),
        ],
        scratch_shapes=[pltpu.VMEM((128, 128), F32)]
        + [pltpu.VMEM(x.shape, x.dtype) for x in (quadrant, frac_lat, frac_lon, land)]
        + [pltpu.SemaphoreType.DMA((4,))],
        compiler_params=PARAMS,
        cost_estimate=pl.CostEstimate(flops=5 * 10**9, bytes_accessed=2 * 10**6, transcendentals=0),
        name="interior",
    )(
        q, side,
        *[pltpu.with_memory_space_constraint(x, pltpu.HBM) for x in (quadrant, frac_lat, frac_lon, land)],
    )


def lat_edge(phase, side, own_grams, got):
    tile_lat, tile_lon, members = side.shape
    inner = tile_lon - 2
    count = 2 * tile_lon
    rows = got.shape[0] // count - 2

    def kernel(side_ref, own_ref, got_ref, out_ref, near_ref):
        lat = lax.axis_index("lat")
        south = (lax.rem(lat, 2) + phase + 1) % 2
        valid = jnp.where(south == 1, lat < lax.axis_size("lat") - 1, lat > 0)
        got_side = jnp.where(valid, unpack_side(got_ref, count * rows, count), 0.0)
        north_side, south_side = got_side[:tile_lon], got_side[tile_lon:]
        own, behind = south * (tile_lat - 1), 1 + south * (tile_lat - 3)
        near_ref[0] = jnp.where(south == 1, south_side, north_side)
        near_ref[1] = jnp.where(south == 1, north_side, south_side)
        near_ref[2] = side_ref[own]
        near_ref[3] = side_ref[behind]
        grams = []
        for first in (south, 1 - south):
            pairs = []
            for j in range(0, tile_lon, 2):
                start = pl.multiple_of((first * tile_lon + j) * rows, 2 * rows)
                pair = got_ref[pl.ds(start, 2 * rows), :]
                pairs.append(jnp.where(valid, pair, jnp.zeros_like(pair)))
            grams.append(row_grams(pairs))
        far, near = grams
        base = identity(members)
        sums = [base + 0.5 * (far[j] + own_ref[own, j]) + near[j] for j in range(inner)]
        sums += [base + 0.5 * (near[j] + own_ref[behind, j]) + own_ref[own, j] for j in range(inner)]
        sides = [near_side(near_ref, k, j) for k in range(2) for j in range(inner)]
        for n, w in enumerate(weights_of(sums, sides)):
            if n < inner:
                w = jnp.where(valid, w, jnp.zeros_like(w))
            out_ref[n // inner, n % inner] = w

    vmem = pl.BlockSpec(memory_space=pltpu.VMEM)
    return pl.pallas_call(
        kernel,
        in_specs=[vmem] * 3,
        out_specs=vmem,
        out_shape=jax.ShapeDtypeStruct((2, inner, members, members), BF16),
        scratch_shapes=[pltpu.VMEM((4, tile_lon, members), F32)],
        compiler_params=PARAMS,
        cost_estimate=pl.CostEstimate(flops=5 * 10**9, bytes_accessed=2 * 10**6, transcendentals=0),
        name="lat_edge",
    )(side, own_grams, got)


def widen(q, side, got_a, got_b, after):
    tile_lat, tile_lon, rows, members = q.shape
    half = 2 * tile_lon
    wide = tile_lat + 4
    count = 2 * wide
    payload = count * rows + 2 * count

    def kernel(
        q_ref, side_ref, a_ref, b_ref, after_ref, wide_ref, wide_side_ref, to_a_ref, to_b_ref,
    ):
        lat = lax.axis_index("lat")
        lon = lax.axis_index("lon")
        lat_odd = lax.rem(lat, 2)
        lon_odd = lax.rem(lon, 2)
        wide_ref[2 : 2 + tile_lat] = q_ref[...]
        wide_side_ref[2 : 2 + tile_lat] = side_ref[...]
        last = lax.axis_size("lat") - 1
        a_valid = jnp.where(lat_odd == 0, lat < last, lat > 0)
        b_valid = jnp.where(lat_odd == 0, lat > 0, lat < last)
        for ref, first, valid in (
            (a_ref, (1 - lat_odd) * (tile_lat + 2), a_valid),
            (b_ref, lat_odd * (tile_lat + 2), b_valid),
        ):
            total = jnp.where(valid, unpack_side(ref, half * rows, half), 0.0)
            for i in range(2):
                wide_side_ref[first + i] = total[i * tile_lon : (i + 1) * tile_lon]
                for j in range(tile_lon):
                    k = (i * tile_lon + j) * rows
                    piece = ref[k : k + rows, :]
                    wide_ref[first + i, j] = jnp.where(valid, piece, jnp.zeros_like(piece))
        for ref, first in ((to_a_ref, (1 - lon_odd) * (tile_lon - 2)), (to_b_ref, lon_odd * (tile_lon - 2))):
            collected = []
            for i in range(wide):
                for j in range(2):
                    k = (i * 2 + j) * rows
                    ref[k : k + rows, :] = wide_ref[i, first + j]
                    collected.append(wide_side_ref[i, pl.ds(first + j, 1), :])
            pack_side(ref, count * rows, jnp.concatenate(collected, axis=0))

    vmem = pl.BlockSpec(memory_space=pltpu.VMEM)
    return pl.pallas_call(
        kernel,
        in_specs=[vmem] * 4 + [pl.BlockSpec(memory_space=pl.ANY)],
        out_specs=[vmem] * 4,
        out_shape=[
            jax.ShapeDtypeStruct((wide, tile_lon, rows, members), BF16),
            jax.ShapeDtypeStruct((wide, tile_lon, members), F32),
            jax.ShapeDtypeStruct((payload, members), BF16),
            jax.ShapeDtypeStruct((payload, members), BF16),
        ],
        compiler_params=PARAMS,
        cost_estimate=pl.CostEstimate(flops=10**6, bytes_accessed=3 * 10**6, transcendentals=0),
        name="widen",
    )(q, side, got_a, got_b, after)


def edge_weights(q_ref, side_ref, got_ref, edge, edge_ref, edge_side_ref, store):
    wide, tile_lon, rows, members = q_ref.shape
    tile_lat = wide - 4
    lat = lax.axis_index("lat")
    last = lax.axis_size("lat") - 1
    own, at = edge * (tile_lon - 2), edge * 2
    got_side = unpack_side(got_ref, 2 * wide * rows, 2 * wide)
    for i in range(wide):
        for j in range(2):
            k = (i * 2 + j) * rows
            edge_ref[i, at + j] = got_ref[k : k + rows, :]
            edge_ref[i, 2 - at + j] = q_ref[i, own + j]
        got_part = got_side[2 * i : 2 * i + 2]
        own_part = jnp.where(edge == 0, side_ref[i, :2, :], side_ref[i, tile_lon - 2 :, :])
        edge_side_ref[i, :2, :] = jnp.where(edge == 0, got_part, own_part)
        edge_side_ref[i, 2:, :] = jnp.where(edge == 0, own_part, got_part)
    grams = [row_grams([pair_of(edge_ref, i, 0), pair_of(edge_ref, i, 2)]) for i in range(wide)]
    base = identity(members)
    nodes = [(i, j) for i in range(tile_lat + 2) for j in range(2)]
    sums = [base + 0.5 * (grams[i][j] + grams[i + 2][j]) + grams[i + 1][j] for i, j in nodes]
    sides = [near_side(edge_side_ref, i, j) for i, j in nodes]
    for (i, j), w in zip(nodes, weights_of(sums, sides)):
        if i == 0:
            w = jnp.where(lat == 0, jnp.zeros_like(w), w)
        if i == tile_lat + 1:
            w = jnp.where(lat == last, jnp.zeros_like(w), w)
        store(i, j, w)


def edge_scratch(wide, rows, members):
    return [pltpu.VMEM((wide, 4, rows, members), BF16), pltpu.VMEM((wide, 4, members), F32)]


def near_edge(wide_q, wide_side, got_a):
    wide, tile_lon, rows, members = wide_q.shape

    def kernel(q_ref, side_ref, a_ref, out_ref, edge_ref, edge_side_ref):
        def store(i, j, w):
            out_ref[i, j] = w

        edge = 1 - lax.rem(lax.axis_index("lon"), 2)
        edge_weights(q_ref, side_ref, a_ref, edge, edge_ref, edge_side_ref, store)

    vmem = pl.BlockSpec(memory_space=pltpu.VMEM)
    return pl.pallas_call(
        kernel,
        in_specs=[vmem] * 3,
        out_specs=vmem,
        out_shape=jax.ShapeDtypeStruct((wide - 2, 2, members, members), BF16),
        scratch_shapes=edge_scratch(wide, rows, members),
        compiler_params=PARAMS,
        cost_estimate=pl.CostEstimate(flops=5 * 10**9, bytes_accessed=3 * 10**6, transcendentals=0),
        name="near_edge",
    )(wide_q, wide_side, got_a)


def finish(state, wide_q, wide_side, got_b, inner_w, lat_a_w, lat_b_w, near_w, columns):
    tile_lat, tile_lon, rows, members = state.shape
    wide = tile_lat + 4

    def kernel(
        state_ref, q_ref, side_ref, b_ref, inner_ref, lat_a_ref, lat_b_ref, near_ref, columns_ref,
        out_hbm, edge_ref, edge_side_ref, w_ref, perturb_ref, out_ref, sems,
    ):
        edge = lax.rem(lax.axis_index("lon"), 2)

        def store(i, j, w):
            w_ref[i, edge * tile_lon + j] = w

        edge_weights(q_ref, side_ref, b_ref, edge, edge_ref, edge_side_ref, store)
        for i in range(tile_lat - 2):
            w_ref[2 + i, 2:tile_lon] = inner_ref[i]
        odd = lax.rem(lax.axis_index("lat"), 2)
        for ref, south in ((lat_a_ref, 1 - odd), (lat_b_ref, odd)):
            w_ref[south * (tile_lat + 1), 2:tile_lon] = ref[0]
            w_ref[1 + south * (tile_lat - 1), 2:tile_lon] = ref[1]
        for i in range(tile_lat + 2):
            for j in range(2):
                w_ref[i, (1 - edge) * tile_lon + j] = near_ref[i, j]

        def analyse(i, carry):
            totals = []
            for j in range(tile_lon):
                x = state_ref[i, j].astype(F32)
                mean = jnp.sum(x, axis=1, keepdims=True) * (1.0 / members)
                centred = x - mean
                perturb_ref[j * rows : (j + 1) * rows, :] = centred.astype(BF16)
                totals.append(x - columns_ref[i, 6, j * rows : (j + 1) * rows, :] * centred)
            for n in range(tile_lon + 2):
                low, high = max(n - 2, 0), min(n, tile_lon - 1)
                near = jnp.concatenate([w_ref[i + a, n] for a in range(3)], axis=0)
                out = lax.dot_general(
                    perturb_ref[low * rows : (high + 1) * rows, :],
                    near,
                    (((1,), (1,)), ((), ())),
                    preferred_element_type=F32,
                )
                for j in range(low, high + 1):
                    here = out[(j - low) * rows : (j - low + 1) * rows]
                    span = slice(j * rows, (j + 1) * rows)
                    mixed = 0.0
                    for a in range(3):
                        mixed = mixed + columns_ref[i, a, span, :] * here[:, a * members : (a + 1) * members]
                    totals[j] = totals[j] + columns_ref[i, 3 + n - j, span, :] * mixed
                    if n == j + 2:
                        out_ref[i, j] = totals[j].astype(BF16)
            pltpu.make_async_copy(out_ref.at[i], out_hbm.at[i], sems.at[i]).start()
            return carry

        lax.fori_loop(0, tile_lat, analyse, 0)
        for i in range(tile_lat):
            pltpu.make_async_copy(out_ref.at[i], out_hbm.at[i], sems.at[i]).wait()

    vmem = pl.BlockSpec(memory_space=pltpu.VMEM)
    return pl.pallas_call(
        kernel,
        in_specs=[vmem] * 9,
        out_specs=pl.BlockSpec(memory_space=pltpu.HBM),
        out_shape=jax.ShapeDtypeStruct(state.shape, BF16),
        scratch_shapes=edge_scratch(wide, rows, members)
        + [
            pltpu.VMEM((tile_lat + 2, tile_lon + 2, members, members), BF16),
            pltpu.VMEM((tile_lon * rows, members), BF16),
            pltpu.VMEM(state.shape, BF16),
            pltpu.SemaphoreType.DMA((tile_lat,)),
        ],
        compiler_params=PARAMS,
        cost_estimate=pl.CostEstimate(flops=10**10, bytes_accessed=3 * 10**6, transcendentals=0),
        name="finish",
    )(state, wide_q, wide_side, got_b, inner_w, lat_a_w, lat_b_w, near_w, columns)


def body(state, obs_row, obs_count, obs_value, obs_weight, quadrant, frac_lat, frac_lon, land):
    tile_lat, tile_lon, rows, members = state.shape
    flat_q, flat_side, send_a, send_b = prepare(state, obs_row, obs_count, obs_value, obs_weight)
    got_a = swap(send_a, "lat", 0)
    got_b = swap_inner_lat(send_b)
    q = flat_q.reshape(tile_lat, tile_lon, rows, members)
    side = flat_side.reshape(tile_lat, tile_lon, members)
    inner_w, columns, own_grams = interior(q, side, quadrant, frac_lat, frac_lon, land)
    lat_a_w = lat_edge(0, side, own_grams, got_a)
    wide_q, wide_side, to_a, to_b = widen(q, side, got_a, got_b, lat_a_w)
    lon_b = swap(to_b, "lon", 1)
    lon_a = swap(to_a, "lon", 0)
    lat_b_w = lat_edge(1, side, own_grams, got_b)
    near_w = near_edge(wide_q, wide_side, lon_a)
    return finish(state, wide_q, wide_side, lon_b, inner_w, lat_a_w, lat_b_w, near_w, columns)


def solution(mesh):
    cell = P("lat", "lon", None)
    return jax.shard_map(
        body,
        mesh=mesh,
        in_specs=(
            P("lat", "lon", None, None), cell, P("lat", "lon"), cell, cell, cell, cell, cell, cell,
        ),
        out_specs=P("lat", "lon", None, None),
        check_vma=False,
    )
```

```python
import math

import jax
import jax.numpy as jnp
from jax import lax
from jax.experimental import pallas as pl
from jax.experimental.pallas import tpu as pltpu
from jax.sharding import PartitionSpec as P

F32 = jnp.float32
BF16 = jnp.bfloat16
ITERS = 6
NEAR = (0.5, 1.0, 0.5)
PARAMS = pltpu.CompilerParams(vmem_limit_bytes=40 * 2**20)


def swap(x, axis, phase):
    count = lax.axis_size(axis)
    pairs = []
    for k in range(phase, count, 2):
        a, b = k, (k + 1) % count
        pairs += [(a, b), (b, a)]
    return lax.ppermute(x, axis, pairs)


def swap_inner_lat(x):
    lats, lons = lax.axis_size("lat"), lax.axis_size("lon")
    pairs = []
    for j in range(lons):
        for k in range(1, lats - 1, 2):
            a, b = k * lons + j, (k + 1) * lons + j
            pairs += [(a, b), (b, a)]
        for k in (0, lats - 1):
            pairs.append((k * lons + j, k * lons + (j ^ 1)))
    return lax.ppermute(x, ("lat", "lon"), pairs)


def split(x):
    high = x.astype(BF16)
    return high, (x - high.astype(F32)).astype(BF16)


def stream(pair):
    return jnp.concatenate(pair, axis=1)


def held(pair):
    row = jnp.concatenate(pair, axis=1)
    return jnp.concatenate([row, row], axis=0)


def product(a, b):
    out = jnp.dot(stream(a), held(b), preferred_element_type=F32)
    half = out.shape[1] // 2
    return out[:, :half] + out[:, half:]


def weights_of(grams, sides):
    members = grams[0].shape[0]
    rows = lax.broadcasted_iota(jnp.int32, (members, members), 0)
    cols = lax.broadcasted_iota(jnp.int32, (members, members), 1)
    eye = jnp.where(rows == cols, F32(1.0), F32(0.0))
    inv_frob = []
    iterates = []
    for gram in grams:
        total = jnp.sum(jnp.sum(gram * gram, axis=0, keepdims=True), axis=1, keepdims=True)
        inverse = lax.rsqrt(total)
        inv_frob.append(inverse)
        iterates.append(gram * inverse)
    first = [split(a) for a in iterates]
    squares, square_parts = iterates, first
    for step in range(0, ITERS, 2):
        inner = [
            product(part, part) + (3.375 * eye - 4.5 * x)
            for part, x in zip(square_parts, squares)
        ]
        inner_parts = [split(x) for x in inner]
        factors = [
            0.0625 * product(part, part) + ((24.609375 / 16) * eye - (8.625 / 16) * x)
            for part, x in zip(inner_parts, squares)
        ]
        factor_parts = [split(x) for x in factors]
        if step == 0:
            roots, root_parts = factors, factor_parts
        else:
            roots = [product(z, x) for z, x in zip(root_parts, factor_parts)]
        if step < ITERS - 2:
            if step > 0:
                root_parts = [split(z) for z in roots]
            half = [split(product(a, z)) for a, z in zip(first, root_parts)]
            squares = [product(x, z) for x, z in zip(half, root_parts)]
            square_parts = [split(x) for x in squares]
    out = []
    for root, side, inverse in zip(roots, sides, inv_frob):
        inner = jnp.sum(root * side, axis=1, keepdims=True)
        mean_weight = jnp.sum(root * inner, axis=0, keepdims=True) * inverse
        out.append((mean_weight + (math.sqrt(members - 1) * jnp.sqrt(inverse)) * root).astype(BF16))
    return out


def row_grams(pairs):
    turned = [pair.T for pair in pairs]
    rows = pairs[0].shape[0] // 2
    half = BF16(0.5)
    out = []
    for p in range(len(pairs) - 1):
        first, second = pairs[p], pairs[p + 1]
        zero = jnp.zeros((rows, first.shape[1]), BF16)
        left = jnp.concatenate([first[:rows] * half, first[rows:], second[:rows] * half, zero], axis=0)
        right = jnp.concatenate([zero, first[rows:] * half, second[:rows], second[rows:] * half], axis=0)
        both = jnp.dot(
            jnp.concatenate(turned[p : p + 2], axis=1),
            jnp.concatenate([left, right], axis=1),
            preferred_element_type=F32,
        )
        members = both.shape[0]
        out += [both[:, :members], both[:, members:]]
    return out


def pair_of(ref, i, j):
    pair = ref[i, j : j + 2]
    return pair.reshape(2 * pair.shape[1], pair.shape[2])


def node_sum(base, gram_ref, i, j):
    return base + 0.5 * (gram_ref[i, j] + gram_ref[i + 2, j]) + gram_ref[i + 1, j]


def near_side(side_ref, i, j):
    total = 0.0
    for a in range(3):
        for b in range(3):
            total = total + NEAR[a] * NEAR[b] * side_ref[i + a, j + b : j + b + 1, :]
    return total


def identity(members):
    rows = lax.broadcasted_iota(jnp.int32, (members, members), 0)
    cols = lax.broadcasted_iota(jnp.int32, (members, members), 1)
    return jnp.where(rows == cols, F32(members - 1), F32(0.0))


def pack_side(ref, at, side):
    high = side.astype(BF16).astype(F32)
    ref[at : at + 2 * side.shape[0], :] = jnp.concatenate([high, side - high], axis=0).astype(BF16)


def unpack_side(ref, at, count):
    both = ref[at : at + 2 * count, :].astype(F32)
    return both[:count] + both[count:]


def cell_copies(first, hbm_refs, refs, sems):
    copies = [pltpu.make_async_copy(hbm_refs[0], refs[0], sems.at[0])]
    for k in range(1, 5):
        source = hbm_refs[k].at[pl.ds(first, 2)]
        copies.append(pltpu.make_async_copy(source, refs[k], sems.at[k]))
    return copies


def cell_scratch(count, state, *rest):
    shapes = [pltpu.SMEM(count.shape, count.dtype)]
    for x in (state, *rest):
        shapes.append(pltpu.VMEM((2, *x.shape[1:]), x.dtype))
    return shapes + [pltpu.SemaphoreType.DMA((5,))]


def cell_rows(first, refs, payload_ref, side_ref):
    count_ref, state_ref, row_ref, value_ref, weight_ref = refs
    _, tile_lon, rows, members = state_ref.shape
    slots = row_ref.shape[2]
    lane = lax.broadcasted_iota(jnp.int32, (1, slots), 1)
    row_ids = lax.broadcasted_iota(jnp.int32, (rows, slots), 0)
    for i in range(2):
        for j in range(tile_lon):
            x = state_ref[i, j].astype(F32)
            mean = jnp.sum(x, axis=1, keepdims=True) * (1.0 / members)
            centred = x - mean
            live = jnp.where(lane < count_ref[first + i, j], weight_ref[i, j : j + 1, :], 0.0)
            hit = row_ids == row_ref[i, j : j + 1, :]
            centre = jnp.sum(jnp.where(hit, mean, 0.0), axis=0, keepdims=True)
            innovation = ((value_ref[i, j : j + 1, :] - centre) * live).astype(BF16).astype(F32)
            square = jnp.sum(jnp.where(hit, live * live, 0.0), axis=1, keepdims=True)
            pull = jnp.sum(jnp.where(hit, live * innovation, 0.0), axis=1, keepdims=True)
            k = i * tile_lon + j
            payload_ref[k * rows : (k + 1) * rows, :] = (centred * jnp.sqrt(square)).astype(BF16)
            side_ref[k : k + 1, :] = jnp.sum(centred * pull, axis=0, keepdims=True)
    pack_side(payload_ref, 2 * tile_lon * rows, side_ref[...])


def in_hbm(arrays):
    return [pltpu.with_memory_space_constraint(x, pltpu.HBM) for x in arrays]


def prepare(state, obs_row, obs_count, obs_value, obs_weight):
    tile_lat, tile_lon, rows, members = state.shape
    half = 2 * tile_lon
    arrays = (obs_count, state, obs_row, obs_value, obs_weight)

    def kernel(*refs):
        hbm_refs, (payload_ref, side_ref), cells, sems = refs[:5], refs[5:7], refs[7:12], refs[12]
        first = (1 - lax.rem(lax.axis_index("lat"), 2)) * (tile_lat - 2)
        copies = cell_copies(first, hbm_refs, cells, sems)
        for copy in copies:
            copy.start()
        for copy in copies:
            copy.wait()
        cell_rows(first, cells, payload_ref, side_ref)

    vmem = pl.BlockSpec(memory_space=pltpu.VMEM)
    return pl.pallas_call(
        kernel,
        in_specs=[pl.BlockSpec(memory_space=pltpu.HBM)] * 5,
        out_specs=[vmem] * 2,
        out_shape=[
            jax.ShapeDtypeStruct((half * rows + 2 * half, members), BF16),
            jax.ShapeDtypeStruct((half, members), F32),
        ],
        scratch_shapes=cell_scratch(*arrays),
        compiler_params=PARAMS,
        cost_estimate=pl.CostEstimate(flops=10**8, bytes_accessed=10**6, transcendentals=0),
        name="prepare",
    )(*in_hbm(arrays))


def complete(state, obs_row, obs_count, obs_value, obs_weight, first_rows, first_side, quadrant, frac_lat, frac_lon, land):
    tile_lat, tile_lon, rows, members = state.shape
    half = 2 * tile_lon
    arrays = (obs_count, state, obs_row, obs_value, obs_weight)
    placing = (quadrant, frac_lat, frac_lon, land)

    def kernel(*refs):
        hbm_refs, placing_hbm, (a_ref, a_side_ref) = refs[:5], refs[5:9], refs[9:11]
        b_ref, q_ref, side_ref, columns_ref, gram_ref = refs[11:16]
        cells, sems = refs[16:21], refs[21]
        b_side_ref, coef_ref = refs[22:24]
        placing_refs, placing_sems = refs[24:28], refs[28]
        quad_ref, flat_ref, flon_ref, land_ref = placing_refs
        odd = lax.rem(lax.axis_index("lat"), 2)
        a_first, b_first = (1 - odd) * (tile_lat - 2), odd * (tile_lat - 2)
        copies = cell_copies(b_first, hbm_refs, cells, sems)
        placing_copies = [
            pltpu.make_async_copy(source, target, placing_sems.at[k])
            for k, (source, target) in enumerate(zip(placing_hbm, placing_refs))
        ]
        for copy in copies + placing_copies:
            copy.start()

        def place(ref, part_ref, first):
            for i in range(2):
                side_ref[first + i] = part_ref[i * tile_lon : (i + 1) * tile_lon]
                pairs = []
                for j in range(0, tile_lon, 2):
                    k = (i * tile_lon + j) * rows
                    q_ref[first + i, j] = ref[k : k + rows, :]
                    q_ref[first + i, j + 1] = ref[k + rows : k + 2 * rows, :]
                    pairs.append(ref[k : k + 2 * rows, :])
                for j, gram in enumerate(row_grams(pairs)):
                    gram_ref[first + i, j] = gram

        place(a_ref, a_side_ref, a_first)
        for copy in copies:
            copy.wait()
        cell_rows(b_first, cells, b_ref, b_side_ref)
        place(b_ref, b_side_ref, b_first)
        coef_ref[...] = jnp.zeros_like(coef_ref)
        for copy in placing_copies:
            copy.wait()

        def columns(i, carry):
            quad = quad_ref[i]
            fa, fo = flat_ref[i], flon_ref[i]
            dry = jnp.where(land_ref[i] == 1, F32(1.0), F32(0.0))
            north, west = quad < 2, lax.rem(quad, 2) == 0
            zero = jnp.zeros_like(fa)
            coefs = (
                jnp.where(north, 1.0 - fa, zero) * dry,
                jnp.where(north, fa, 1.0 - fa) * dry,
                jnp.where(north, zero, fa) * dry,
                jnp.where(west, 1.0 - fo, zero),
                jnp.where(west, fo, 1.0 - fo),
                jnp.where(west, zero, fo),
                dry,
            )
            for k, coef in enumerate(coefs):
                coef_ref[k * tile_lon : (k + 1) * tile_lon, :rows] = coef
            turned = coef_ref[...].T
            for k in range(len(coefs)):
                for j in range(tile_lon):
                    at = k * tile_lon + j
                    columns_ref[i, k, j * rows : (j + 1) * rows, :] = jnp.broadcast_to(
                        turned[:rows, at : at + 1], (rows, members)
                    )
            return carry

        lax.fori_loop(0, tile_lat, columns, 0)

    vmem = pl.BlockSpec(memory_space=pltpu.VMEM)
    return pl.pallas_call(
        kernel,
        in_specs=[pl.BlockSpec(memory_space=pltpu.HBM)] * 9 + [vmem] * 2,
        out_specs=[vmem] * 5,
        out_shape=[
            jax.ShapeDtypeStruct(first_rows.shape, BF16),
            jax.ShapeDtypeStruct(state.shape, BF16),
            jax.ShapeDtypeStruct((tile_lat, tile_lon, members), F32),
            jax.ShapeDtypeStruct((tile_lat, 7, tile_lon * rows, members), F32),
            jax.ShapeDtypeStruct((tile_lat, tile_lon - 2, members, members), F32),
        ],
        scratch_shapes=cell_scratch(*arrays)
        + [pltpu.VMEM((half, members), F32), pltpu.VMEM((128, 128), F32)]
        + [pltpu.VMEM(x.shape, x.dtype) for x in placing]
        + [pltpu.SemaphoreType.DMA((4,))],
        compiler_params=PARAMS,
        cost_estimate=pl.CostEstimate(flops=10**9, bytes_accessed=10**6, transcendentals=0),
        name="complete",
    )(*in_hbm(arrays), *in_hbm(placing), first_rows, first_side)


def interior(side, own_grams):
    tile_lat, tile_lon, members = side.shape

    def kernel(side_ref, gram_ref, out_ref):
        base = identity(members)
        nodes = [(i, j) for i in range(tile_lat - 2) for j in range(tile_lon - 2)]
        sums = [node_sum(base, gram_ref, i, j) for i, j in nodes]
        sides = [near_side(side_ref, i, j) for i, j in nodes]
        for (i, j), w in zip(nodes, weights_of(sums, sides)):
            out_ref[i, j] = w

    vmem = pl.BlockSpec(memory_space=pltpu.VMEM)
    return pl.pallas_call(
        kernel,
        in_specs=[vmem] * 2,
        out_specs=vmem,
        out_shape=jax.ShapeDtypeStruct((tile_lat - 2, tile_lon - 2, members, members), BF16),
        compiler_params=PARAMS,
        cost_estimate=pl.CostEstimate(flops=5 * 10**9, bytes_accessed=2 * 10**6, transcendentals=0),
        name="interior",
    )(side, own_grams)


def lat_edge(phase, side, own_grams, got):
    tile_lat, tile_lon, members = side.shape
    inner = tile_lon - 2
    count = 2 * tile_lon
    rows = got.shape[0] // count - 2

    def kernel(side_ref, own_ref, got_ref, out_ref, near_ref):
        lat = lax.axis_index("lat")
        south = (lax.rem(lat, 2) + phase + 1) % 2
        valid = jnp.where(south == 1, lat < lax.axis_size("lat") - 1, lat > 0)
        got_side = jnp.where(valid, unpack_side(got_ref, count * rows, count), 0.0)
        north_side, south_side = got_side[:tile_lon], got_side[tile_lon:]
        own, behind = south * (tile_lat - 1), 1 + south * (tile_lat - 3)
        near_ref[0] = jnp.where(south == 1, south_side, north_side)
        near_ref[1] = jnp.where(south == 1, north_side, south_side)
        near_ref[2] = side_ref[own]
        near_ref[3] = side_ref[behind]
        grams = []
        for first in (south, 1 - south):
            pairs = []
            for j in range(0, tile_lon, 2):
                start = pl.multiple_of((first * tile_lon + j) * rows, 2 * rows)
                pair = got_ref[pl.ds(start, 2 * rows), :]
                pairs.append(jnp.where(valid, pair, jnp.zeros_like(pair)))
            grams.append(row_grams(pairs))
        far, near = grams
        base = identity(members)
        sums = [base + 0.5 * (far[j] + own_ref[own, j]) + near[j] for j in range(inner)]
        sums += [base + 0.5 * (near[j] + own_ref[behind, j]) + own_ref[own, j] for j in range(inner)]
        sides = [near_side(near_ref, k, j) for k in range(2) for j in range(inner)]
        for n, w in enumerate(weights_of(sums, sides)):
            if n < inner:
                w = jnp.where(valid, w, jnp.zeros_like(w))
            out_ref[n // inner, n % inner] = w

    vmem = pl.BlockSpec(memory_space=pltpu.VMEM)
    return pl.pallas_call(
        kernel,
        in_specs=[vmem] * 3,
        out_specs=vmem,
        out_shape=jax.ShapeDtypeStruct((2, inner, members, members), BF16),
        scratch_shapes=[pltpu.VMEM((4, tile_lon, members), F32)],
        compiler_params=PARAMS,
        cost_estimate=pl.CostEstimate(flops=5 * 10**9, bytes_accessed=2 * 10**6, transcendentals=0),
        name="lat_edge",
    )(side, own_grams, got)


def widen(q, side, got_a, got_b, after):
    tile_lat, tile_lon, rows, members = q.shape
    half = 2 * tile_lon
    wide = tile_lat + 4
    count = 2 * wide
    payload = count * rows + 2 * count

    def kernel(
        q_ref, side_ref, a_ref, b_ref, after_ref, wide_ref, wide_side_ref, to_a_ref, to_b_ref,
    ):
        lat = lax.axis_index("lat")
        lon = lax.axis_index("lon")
        lat_odd = lax.rem(lat, 2)
        lon_odd = lax.rem(lon, 2)
        wide_ref[2 : 2 + tile_lat] = q_ref[...]
        wide_side_ref[2 : 2 + tile_lat] = side_ref[...]
        last = lax.axis_size("lat") - 1
        a_valid = jnp.where(lat_odd == 0, lat < last, lat > 0)
        b_valid = jnp.where(lat_odd == 0, lat > 0, lat < last)
        for ref, first, valid in (
            (a_ref, (1 - lat_odd) * (tile_lat + 2), a_valid),
            (b_ref, lat_odd * (tile_lat + 2), b_valid),
        ):
            total = jnp.where(valid, unpack_side(ref, half * rows, half), 0.0)
            for i in range(2):
                wide_side_ref[first + i] = total[i * tile_lon : (i + 1) * tile_lon]
                for j in range(tile_lon):
                    k = (i * tile_lon + j) * rows
                    piece = ref[k : k + rows, :]
                    wide_ref[first + i, j] = jnp.where(valid, piece, jnp.zeros_like(piece))
        for ref, first in ((to_a_ref, (1 - lon_odd) * (tile_lon - 2)), (to_b_ref, lon_odd * (tile_lon - 2))):
            collected = []
            for i in range(wide):
                for j in range(2):
                    k = (i * 2 + j) * rows
                    ref[k : k + rows, :] = wide_ref[i, first + j]
                    collected.append(wide_side_ref[i, pl.ds(first + j, 1), :])
            pack_side(ref, count * rows, jnp.concatenate(collected, axis=0))

    vmem = pl.BlockSpec(memory_space=pltpu.VMEM)
    return pl.pallas_call(
        kernel,
        in_specs=[vmem] * 4 + [pl.BlockSpec(memory_space=pl.ANY)],
        out_specs=[vmem] * 4,
        out_shape=[
            jax.ShapeDtypeStruct((wide, tile_lon, rows, members), BF16),
            jax.ShapeDtypeStruct((wide, tile_lon, members), F32),
            jax.ShapeDtypeStruct((payload, members), BF16),
            jax.ShapeDtypeStruct((payload, members), BF16),
        ],
        compiler_params=PARAMS,
        cost_estimate=pl.CostEstimate(flops=10**6, bytes_accessed=3 * 10**6, transcendentals=0),
        name="widen",
    )(q, side, got_a, got_b, after)


def edge_weights(q_ref, side_ref, got_ref, edge, edge_ref, edge_side_ref, store):
    wide, tile_lon, rows, members = q_ref.shape
    tile_lat = wide - 4
    lat = lax.axis_index("lat")
    last = lax.axis_size("lat") - 1
    own, at = edge * (tile_lon - 2), edge * 2
    got_side = unpack_side(got_ref, 2 * wide * rows, 2 * wide)
    for i in range(wide):
        for j in range(2):
            k = (i * 2 + j) * rows
            edge_ref[i, at + j] = got_ref[k : k + rows, :]
            edge_ref[i, 2 - at + j] = q_ref[i, own + j]
        got_part = got_side[2 * i : 2 * i + 2]
        own_part = jnp.where(edge == 0, side_ref[i, :2, :], side_ref[i, tile_lon - 2 :, :])
        edge_side_ref[i, :2, :] = jnp.where(edge == 0, got_part, own_part)
        edge_side_ref[i, 2:, :] = jnp.where(edge == 0, own_part, got_part)
    grams = [row_grams([pair_of(edge_ref, i, 0), pair_of(edge_ref, i, 2)]) for i in range(wide)]
    base = identity(members)
    nodes = [(i, j) for i in range(tile_lat + 2) for j in range(2)]
    sums = [base + 0.5 * (grams[i][j] + grams[i + 2][j]) + grams[i + 1][j] for i, j in nodes]
    sides = [near_side(edge_side_ref, i, j) for i, j in nodes]
    for (i, j), w in zip(nodes, weights_of(sums, sides)):
        if i == 0:
            w = jnp.where(lat == 0, jnp.zeros_like(w), w)
        if i == tile_lat + 1:
            w = jnp.where(lat == last, jnp.zeros_like(w), w)
        store(i, j, w)


def edge_scratch(wide, rows, members):
    return [pltpu.VMEM((wide, 4, rows, members), BF16), pltpu.VMEM((wide, 4, members), F32)]


def near_edge(wide_q, wide_side, got_a):
    wide, tile_lon, rows, members = wide_q.shape

    def kernel(q_ref, side_ref, a_ref, out_ref, edge_ref, edge_side_ref):
        def store(i, j, w):
            out_ref[i, j] = w

        edge = 1 - lax.rem(lax.axis_index("lon"), 2)
        edge_weights(q_ref, side_ref, a_ref, edge, edge_ref, edge_side_ref, store)

    vmem = pl.BlockSpec(memory_space=pltpu.VMEM)
    return pl.pallas_call(
        kernel,
        in_specs=[vmem] * 3,
        out_specs=vmem,
        out_shape=jax.ShapeDtypeStruct((wide - 2, 2, members, members), BF16),
        scratch_shapes=edge_scratch(wide, rows, members),
        compiler_params=PARAMS,
        cost_estimate=pl.CostEstimate(flops=5 * 10**9, bytes_accessed=3 * 10**6, transcendentals=0),
        name="near_edge",
    )(wide_q, wide_side, got_a)


def finish(state, wide_q, wide_side, got_b, inner_w, lat_a_w, lat_b_w, near_w, columns):
    tile_lat, tile_lon, rows, members = state.shape
    wide = tile_lat + 4

    def kernel(
        state_ref, q_ref, side_ref, b_ref, inner_ref, lat_a_ref, lat_b_ref, near_ref, columns_ref,
        out_hbm, edge_ref, edge_side_ref, w_ref, perturb_ref, out_ref, sems,
    ):
        edge = lax.rem(lax.axis_index("lon"), 2)

        def store(i, j, w):
            w_ref[i, edge * tile_lon + j] = w

        edge_weights(q_ref, side_ref, b_ref, edge, edge_ref, edge_side_ref, store)
        for i in range(tile_lat - 2):
            w_ref[2 + i, 2:tile_lon] = inner_ref[i]
        odd = lax.rem(lax.axis_index("lat"), 2)
        for ref, south in ((lat_a_ref, 1 - odd), (lat_b_ref, odd)):
            w_ref[south * (tile_lat + 1), 2:tile_lon] = ref[0]
            w_ref[1 + south * (tile_lat - 1), 2:tile_lon] = ref[1]
        for i in range(tile_lat + 2):
            for j in range(2):
                w_ref[i, (1 - edge) * tile_lon + j] = near_ref[i, j]

        def analyse(i, carry):
            totals = []
            for j in range(tile_lon):
                x = state_ref[i, j].astype(F32)
                mean = jnp.sum(x, axis=1, keepdims=True) * (1.0 / members)
                centred = x - mean
                perturb_ref[j * rows : (j + 1) * rows, :] = centred.astype(BF16)
                totals.append(x - columns_ref[i, 6, j * rows : (j + 1) * rows, :] * centred)
            for n in range(tile_lon + 2):
                low, high = max(n - 2, 0), min(n, tile_lon - 1)
                near = jnp.concatenate([w_ref[i + a, n] for a in range(3)], axis=0)
                out = lax.dot_general(
                    perturb_ref[low * rows : (high + 1) * rows, :],
                    near,
                    (((1,), (1,)), ((), ())),
                    preferred_element_type=F32,
                )
                for j in range(low, high + 1):
                    here = out[(j - low) * rows : (j - low + 1) * rows]
                    span = slice(j * rows, (j + 1) * rows)
                    mixed = 0.0
                    for a in range(3):
                        mixed = mixed + columns_ref[i, a, span, :] * here[:, a * members : (a + 1) * members]
                    totals[j] = totals[j] + columns_ref[i, 3 + n - j, span, :] * mixed
                    if n == j + 2:
                        out_ref[i, j] = totals[j].astype(BF16)
            pltpu.make_async_copy(out_ref.at[i], out_hbm.at[i], sems.at[i]).start()
            return carry

        lax.fori_loop(0, tile_lat, analyse, 0)
        for i in range(tile_lat):
            pltpu.make_async_copy(out_ref.at[i], out_hbm.at[i], sems.at[i]).wait()

    vmem = pl.BlockSpec(memory_space=pltpu.VMEM)
    return pl.pallas_call(
        kernel,
        in_specs=[vmem] * 9,
        out_specs=pl.BlockSpec(memory_space=pltpu.HBM),
        out_shape=jax.ShapeDtypeStruct(state.shape, BF16),
        scratch_shapes=edge_scratch(wide, rows, members)
        + [
            pltpu.VMEM((tile_lat + 2, tile_lon + 2, members, members), BF16),
            pltpu.VMEM((tile_lon * rows, members), BF16),
            pltpu.VMEM(state.shape, BF16),
            pltpu.SemaphoreType.DMA((tile_lat,)),
        ],
        compiler_params=PARAMS,
        cost_estimate=pl.CostEstimate(flops=10**10, bytes_accessed=3 * 10**6, transcendentals=0),
        name="finish",
    )(state, wide_q, wide_side, got_b, inner_w, lat_a_w, lat_b_w, near_w, columns)


def body(state, obs_row, obs_count, obs_value, obs_weight, quadrant, frac_lat, frac_lon, land):
    send_a, side_a = prepare(state, obs_row, obs_count, obs_value, obs_weight)
    got_a = swap(send_a, "lat", 0)
    send_b, q, side, columns, own_grams = complete(
        state, obs_row, obs_count, obs_value, obs_weight, send_a, side_a, quadrant, frac_lat, frac_lon, land
    )
    got_b = swap_inner_lat(send_b)
    inner_w = interior(side, own_grams)
    lat_a_w = lat_edge(0, side, own_grams, got_a)
    wide_q, wide_side, to_a, to_b = widen(q, side, got_a, got_b, lat_a_w)
    lon_b = swap(to_b, "lon", 1)
    lon_a = swap(to_a, "lon", 0)
    lat_b_w = lat_edge(1, side, own_grams, got_b)
    near_w = near_edge(wide_q, wide_side, lon_a)
    return finish(state, wide_q, wide_side, lon_b, inner_w, lat_a_w, lat_b_w, near_w, columns)


def solution(mesh):
    cell = P("lat", "lon", None)
    return jax.shard_map(
        body,
        mesh=mesh,
        in_specs=(
            P("lat", "lon", None, None), cell, P("lat", "lon"), cell, cell, cell, cell, cell, cell,
        ),
        out_specs=P("lat", "lon", None, None),
        check_vma=False,
    )
```

```python
import math

import jax
import jax.numpy as jnp
from jax import lax
from jax.experimental import pallas as pl
from jax.experimental.pallas import tpu as pltpu
from jax.sharding import PartitionSpec as P

F32 = jnp.float32
BF16 = jnp.bfloat16
ITERS = 6
NEAR = (0.5, 1.0, 0.5)
PARAMS = pltpu.CompilerParams(vmem_limit_bytes=40 * 2**20)


def swap(x, axis, phase):
    count = lax.axis_size(axis)
    pairs = []
    for k in range(phase, count, 2):
        a, b = k, (k + 1) % count
        pairs += [(a, b), (b, a)]
    return lax.ppermute(x, axis, pairs)


def swap_inner_lat(x):
    lats, lons = lax.axis_size("lat"), lax.axis_size("lon")
    pairs = []
    for j in range(lons):
        for k in range(1, lats - 1, 2):
            a, b = k * lons + j, (k + 1) * lons + j
            pairs += [(a, b), (b, a)]
        for k in (0, lats - 1):
            pairs.append((k * lons + j, k * lons + (j ^ 1)))
    return lax.ppermute(x, ("lat", "lon"), pairs)


def split(x):
    high = x.astype(BF16)
    return high, (x - high.astype(F32)).astype(BF16)


def stream(pair):
    return jnp.concatenate(pair, axis=1)


def held(pair):
    row = jnp.concatenate(pair, axis=1)
    return jnp.concatenate([row, row], axis=0)


def product(a, b):
    out = jnp.dot(stream(a), held(b), preferred_element_type=F32)
    half = out.shape[1] // 2
    return out[:, :half] + out[:, half:]


def weights_of(grams, sides):
    members = grams[0].shape[0]
    rows = lax.broadcasted_iota(jnp.int32, (members, members), 0)
    cols = lax.broadcasted_iota(jnp.int32, (members, members), 1)
    eye = jnp.where(rows == cols, F32(1.0), F32(0.0))
    inv_frob = []
    iterates = []
    for gram in grams:
        total = jnp.sum(jnp.sum(gram * gram, axis=0, keepdims=True), axis=1, keepdims=True)
        inverse = lax.rsqrt(total)
        inv_frob.append(inverse)
        iterates.append(gram * inverse)
    first = [split(a) for a in iterates]
    squares, square_parts = iterates, first
    for step in range(0, ITERS, 2):
        inner = [
            product(part, part) + (3.375 * eye - 4.5 * x)
            for part, x in zip(square_parts, squares)
        ]
        inner_parts = [split(x) for x in inner]
        factors = [
            0.0625 * product(part, part) + ((24.609375 / 16) * eye - (8.625 / 16) * x)
            for part, x in zip(inner_parts, squares)
        ]
        factor_parts = [split(x) for x in factors]
        if step == 0:
            roots, root_parts = factors, factor_parts
        else:
            roots = [product(z, x) for z, x in zip(root_parts, factor_parts)]
        if step < ITERS - 2:
            if step > 0:
                root_parts = [split(z) for z in roots]
            half = [split(product(a, z)) for a, z in zip(first, root_parts)]
            squares = [product(x, z) for x, z in zip(half, root_parts)]
            square_parts = [split(x) for x in squares]
    out = []
    for root, side, inverse in zip(roots, sides, inv_frob):
        inner = jnp.sum(root * side, axis=1, keepdims=True)
        mean_weight = jnp.sum(root * inner, axis=0, keepdims=True) * inverse
        out.append((mean_weight + (math.sqrt(members - 1) * jnp.sqrt(inverse)) * root).astype(BF16))
    return out


def row_grams(pairs):
    turned = [pair.T for pair in pairs]
    rows = pairs[0].shape[0] // 2
    half = BF16(0.5)
    out = []
    for p in range(len(pairs) - 1):
        first, second = pairs[p], pairs[p + 1]
        zero = jnp.zeros((rows, first.shape[1]), BF16)
        left = jnp.concatenate([first[:rows] * half, first[rows:], second[:rows] * half, zero], axis=0)
        right = jnp.concatenate([zero, first[rows:] * half, second[:rows], second[rows:] * half], axis=0)
        both = jnp.dot(
            jnp.concatenate(turned[p : p + 2], axis=1),
            jnp.concatenate([left, right], axis=1),
            preferred_element_type=F32,
        )
        members = both.shape[0]
        out += [both[:, :members], both[:, members:]]
    return out


def pair_of(ref, i, j):
    pair = ref[i, j : j + 2]
    return pair.reshape(2 * pair.shape[1], pair.shape[2])


def node_sum(base, gram_ref, i, j):
    return base + 0.5 * (gram_ref[i, j] + gram_ref[i + 2, j]) + gram_ref[i + 1, j]


def near_side(side_ref, i, j):
    total = 0.0
    for a in range(3):
        for b in range(3):
            total = total + NEAR[a] * NEAR[b] * side_ref[i + a, j + b : j + b + 1, :]
    return total


def identity(members):
    rows = lax.broadcasted_iota(jnp.int32, (members, members), 0)
    cols = lax.broadcasted_iota(jnp.int32, (members, members), 1)
    return jnp.where(rows == cols, F32(members - 1), F32(0.0))


def pack_side(ref, at, side):
    high = side.astype(BF16).astype(F32)
    ref[at : at + 2 * side.shape[0], :] = jnp.concatenate([high, side - high], axis=0).astype(BF16)


def unpack_side(ref, at, count):
    both = ref[at : at + 2 * count, :].astype(F32)
    return both[:count] + both[count:]


def cell_copies(first, hbm_refs, refs, sems):
    copies = [pltpu.make_async_copy(hbm_refs[0], refs[0], sems.at[0])]
    for k in range(1, 5):
        source = hbm_refs[k].at[pl.ds(first, 2)]
        copies.append(pltpu.make_async_copy(source, refs[k], sems.at[k]))
    return copies


def cell_scratch(count, state, *rest):
    shapes = [pltpu.SMEM(count.shape, count.dtype)]
    for x in (state, *rest):
        shapes.append(pltpu.VMEM((2, *x.shape[1:]), x.dtype))
    return shapes + [pltpu.SemaphoreType.DMA((5,))]


def cell_rows(first, refs, payload_ref, side_ref):
    count_ref, state_ref, row_ref, value_ref, weight_ref = refs
    _, tile_lon, rows, members = state_ref.shape
    slots = row_ref.shape[2]
    lane = lax.broadcasted_iota(jnp.int32, (1, slots), 1)
    row_ids = lax.broadcasted_iota(jnp.int32, (rows, slots), 0)
    for i in range(2):
        for j in range(tile_lon):
            x = state_ref[i, j].astype(F32)
            mean = jnp.sum(x, axis=1, keepdims=True) * (1.0 / members)
            centred = x - mean
            live = jnp.where(lane < count_ref[first + i, j], weight_ref[i, j : j + 1, :], 0.0)
            hit = row_ids == row_ref[i, j : j + 1, :]
            centre = jnp.sum(jnp.where(hit, mean, 0.0), axis=0, keepdims=True)
            innovation = ((value_ref[i, j : j + 1, :] - centre) * live).astype(BF16).astype(F32)
            square = jnp.sum(jnp.where(hit, live * live, 0.0), axis=1, keepdims=True)
            pull = jnp.sum(jnp.where(hit, live * innovation, 0.0), axis=1, keepdims=True)
            k = i * tile_lon + j
            payload_ref[k * rows : (k + 1) * rows, :] = (centred * jnp.sqrt(square)).astype(BF16)
            side_ref[k : k + 1, :] = jnp.sum(centred * pull, axis=0, keepdims=True)
    pack_side(payload_ref, 2 * tile_lon * rows, side_ref[...])


def in_hbm(arrays):
    return [pltpu.with_memory_space_constraint(x, pltpu.HBM) for x in arrays]


def prepare(state, obs_row, obs_count, obs_value, obs_weight):
    tile_lat, tile_lon, rows, members = state.shape
    half = 2 * tile_lon
    arrays = (obs_count, state, obs_row, obs_value, obs_weight)

    def kernel(*refs):
        hbm_refs, (payload_ref, side_ref), cells, sems = refs[:5], refs[5:7], refs[7:12], refs[12]
        first = (1 - lax.rem(lax.axis_index("lat"), 2)) * (tile_lat - 2)
        copies = cell_copies(first, hbm_refs, cells, sems)
        for copy in copies:
            copy.start()
        for copy in copies:
            copy.wait()
        cell_rows(first, cells, payload_ref, side_ref)

    vmem = pl.BlockSpec(memory_space=pltpu.VMEM)
    return pl.pallas_call(
        kernel,
        in_specs=[pl.BlockSpec(memory_space=pltpu.HBM)] * 5,
        out_specs=[vmem] * 2,
        out_shape=[
            jax.ShapeDtypeStruct((half * rows + 2 * half, members), BF16),
            jax.ShapeDtypeStruct((half, members), F32),
        ],
        scratch_shapes=cell_scratch(*arrays),
        compiler_params=PARAMS,
        cost_estimate=pl.CostEstimate(flops=10**8, bytes_accessed=10**6, transcendentals=0),
        name="prepare",
    )(*in_hbm(arrays))


def complete(state, obs_row, obs_count, obs_value, obs_weight, first_rows, first_side):
    tile_lat, tile_lon, rows, members = state.shape
    half = 2 * tile_lon
    arrays = (obs_count, state, obs_row, obs_value, obs_weight)

    def kernel(*refs):
        hbm_refs, (a_ref, a_side_ref) = refs[:5], refs[5:7]
        b_ref, q_ref, side_ref, gram_ref = refs[7:11]
        cells, sems, b_side_ref = refs[11:16], refs[16], refs[17]
        odd = lax.rem(lax.axis_index("lat"), 2)
        a_first, b_first = (1 - odd) * (tile_lat - 2), odd * (tile_lat - 2)
        copies = cell_copies(b_first, hbm_refs, cells, sems)
        for copy in copies:
            copy.start()

        def place(ref, part_ref, first):
            for i in range(2):
                side_ref[first + i] = part_ref[i * tile_lon : (i + 1) * tile_lon]
                pairs = []
                for j in range(0, tile_lon, 2):
                    k = (i * tile_lon + j) * rows
                    q_ref[first + i, j] = ref[k : k + rows, :]
                    q_ref[first + i, j + 1] = ref[k + rows : k + 2 * rows, :]
                    pairs.append(ref[k : k + 2 * rows, :])
                for j, gram in enumerate(row_grams(pairs)):
                    gram_ref[first + i, j] = gram

        place(a_ref, a_side_ref, a_first)
        for copy in copies:
            copy.wait()
        cell_rows(b_first, cells, b_ref, b_side_ref)
        place(b_ref, b_side_ref, b_first)

    vmem = pl.BlockSpec(memory_space=pltpu.VMEM)
    return pl.pallas_call(
        kernel,
        in_specs=[pl.BlockSpec(memory_space=pltpu.HBM)] * 5 + [vmem] * 2,
        out_specs=[vmem] * 4,
        out_shape=[
            jax.ShapeDtypeStruct(first_rows.shape, BF16),
            jax.ShapeDtypeStruct(state.shape, BF16),
            jax.ShapeDtypeStruct((tile_lat, tile_lon, members), F32),
            jax.ShapeDtypeStruct((tile_lat, tile_lon - 2, members, members), F32),
        ],
        scratch_shapes=cell_scratch(*arrays) + [pltpu.VMEM((half, members), F32)],
        compiler_params=PARAMS,
        cost_estimate=pl.CostEstimate(flops=10**9, bytes_accessed=10**6, transcendentals=0),
        name="complete",
    )(*in_hbm(arrays), first_rows, first_side)


def interior(side, own_grams, quadrant, frac_lat, frac_lon, land):
    tile_lat, tile_lon, members = side.shape
    rows = quadrant.shape[2]
    placing = (quadrant, frac_lat, frac_lon, land)

    def kernel(side_ref, gram_ref, *refs):
        placing_hbm, (out_ref, columns_ref, coef_ref) = refs[:4], refs[4:7]
        placing_refs, sems = refs[7:11], refs[11]
        quad_ref, flat_ref, flon_ref, land_ref = placing_refs
        copies = [
            pltpu.make_async_copy(source, target, sems.at[k])
            for k, (source, target) in enumerate(zip(placing_hbm, placing_refs))
        ]
        for copy in copies:
            copy.start()
        coef_ref[...] = jnp.zeros_like(coef_ref)
        base = identity(members)
        nodes = [(i, j) for i in range(tile_lat - 2) for j in range(tile_lon - 2)]
        sums = [node_sum(base, gram_ref, i, j) for i, j in nodes]
        sides = [near_side(side_ref, i, j) for i, j in nodes]
        for copy in copies:
            copy.wait()
        for i in range(tile_lat):
            quad = quad_ref[i]
            fa, fo = flat_ref[i], flon_ref[i]
            dry = jnp.where(land_ref[i] == 1, F32(1.0), F32(0.0))
            north, west = quad < 2, lax.rem(quad, 2) == 0
            zero = jnp.zeros_like(fa)
            coefs = (
                jnp.where(north, 1.0 - fa, zero) * dry,
                jnp.where(north, zero, fa) * dry,
                jnp.where(west, 1.0 - fo, zero),
                jnp.where(west, zero, fo),
                dry,
            )
            for k, coef in enumerate(coefs):
                coef_ref[i, k * tile_lon : (k + 1) * tile_lon, :rows] = coef
            turned = coef_ref[i].T
            for k in range(len(coefs)):
                for j in range(tile_lon):
                    at = k * tile_lon + j
                    columns_ref[i, k, j * rows : (j + 1) * rows, :] = jnp.broadcast_to(
                        turned[:rows, at : at + 1], (rows, members)
                    )
        for (i, j), w in zip(nodes, weights_of(sums, sides)):
            out_ref[i, j] = w

    vmem = pl.BlockSpec(memory_space=pltpu.VMEM)
    return pl.pallas_call(
        kernel,
        in_specs=[vmem] * 2 + [pl.BlockSpec(memory_space=pltpu.HBM)] * 4,
        out_specs=[vmem] * 2,
        out_shape=[
            jax.ShapeDtypeStruct((tile_lat - 2, tile_lon - 2, members, members), BF16),
            jax.ShapeDtypeStruct((tile_lat, 5, tile_lon * rows, members), F32),
        ],
        scratch_shapes=[pltpu.VMEM((tile_lat, 128, 128), F32)]
        + [pltpu.VMEM(x.shape, x.dtype) for x in placing]
        + [pltpu.SemaphoreType.DMA((4,))],
        compiler_params=PARAMS,
        cost_estimate=pl.CostEstimate(flops=5 * 10**9, bytes_accessed=2 * 10**6, transcendentals=0),
        name="interior",
    )(side, own_grams, *in_hbm(placing))


def lat_edge(phase, side, own_grams, got):
    tile_lat, tile_lon, members = side.shape
    inner = tile_lon - 2
    count = 2 * tile_lon
    rows = got.shape[0] // count - 2

    def kernel(side_ref, own_ref, got_ref, out_ref, near_ref):
        lat = lax.axis_index("lat")
        south = (lax.rem(lat, 2) + phase + 1) % 2
        valid = jnp.where(south == 1, lat < lax.axis_size("lat") - 1, lat > 0)
        got_side = jnp.where(valid, unpack_side(got_ref, count * rows, count), 0.0)
        north_side, south_side = got_side[:tile_lon], got_side[tile_lon:]
        own, behind = south * (tile_lat - 1), 1 + south * (tile_lat - 3)
        near_ref[0] = jnp.where(south == 1, south_side, north_side)
        near_ref[1] = jnp.where(south == 1, north_side, south_side)
        near_ref[2] = side_ref[own]
        near_ref[3] = side_ref[behind]
        grams = []
        for first in (south, 1 - south):
            pairs = []
            for j in range(0, tile_lon, 2):
                start = pl.multiple_of((first * tile_lon + j) * rows, 2 * rows)
                pair = got_ref[pl.ds(start, 2 * rows), :]
                pairs.append(jnp.where(valid, pair, jnp.zeros_like(pair)))
            grams.append(row_grams(pairs))
        far, near = grams
        base = identity(members)
        sums = [base + 0.5 * (far[j] + own_ref[own, j]) + near[j] for j in range(inner)]
        sums += [base + 0.5 * (near[j] + own_ref[behind, j]) + own_ref[own, j] for j in range(inner)]
        sides = [near_side(near_ref, k, j) for k in range(2) for j in range(inner)]
        for n, w in enumerate(weights_of(sums, sides)):
            if n < inner:
                w = jnp.where(valid, w, jnp.zeros_like(w))
            out_ref[n // inner, n % inner] = w

    vmem = pl.BlockSpec(memory_space=pltpu.VMEM)
    return pl.pallas_call(
        kernel,
        in_specs=[vmem] * 3,
        out_specs=vmem,
        out_shape=jax.ShapeDtypeStruct((2, inner, members, members), BF16),
        scratch_shapes=[pltpu.VMEM((4, tile_lon, members), F32)],
        compiler_params=PARAMS,
        cost_estimate=pl.CostEstimate(flops=5 * 10**9, bytes_accessed=2 * 10**6, transcendentals=0),
        name="lat_edge",
    )(side, own_grams, got)


def widen(q, side, got_a, got_b, after):
    tile_lat, tile_lon, rows, members = q.shape
    half = 2 * tile_lon
    wide = tile_lat + 4
    count = 2 * wide
    payload = count * rows + 2 * count

    def kernel(
        q_ref, side_ref, a_ref, b_ref, after_ref, wide_ref, wide_side_ref, to_a_ref, to_b_ref,
    ):
        lat = lax.axis_index("lat")
        lon = lax.axis_index("lon")
        lat_odd = lax.rem(lat, 2)
        lon_odd = lax.rem(lon, 2)
        wide_ref[2 : 2 + tile_lat] = q_ref[...]
        wide_side_ref[2 : 2 + tile_lat] = side_ref[...]
        last = lax.axis_size("lat") - 1
        a_valid = jnp.where(lat_odd == 0, lat < last, lat > 0)
        b_valid = jnp.where(lat_odd == 0, lat > 0, lat < last)
        for ref, first, valid in (
            (a_ref, (1 - lat_odd) * (tile_lat + 2), a_valid),
            (b_ref, lat_odd * (tile_lat + 2), b_valid),
        ):
            total = jnp.where(valid, unpack_side(ref, half * rows, half), 0.0)
            for i in range(2):
                wide_side_ref[first + i] = total[i * tile_lon : (i + 1) * tile_lon]
                for j in range(tile_lon):
                    k = (i * tile_lon + j) * rows
                    piece = ref[k : k + rows, :]
                    wide_ref[first + i, j] = jnp.where(valid, piece, jnp.zeros_like(piece))
        for ref, first in ((to_a_ref, (1 - lon_odd) * (tile_lon - 2)), (to_b_ref, lon_odd * (tile_lon - 2))):
            collected = []
            for i in range(wide):
                for j in range(2):
                    k = (i * 2 + j) * rows
                    ref[k : k + rows, :] = wide_ref[i, first + j]
                    collected.append(wide_side_ref[i, pl.ds(first + j, 1), :])
            pack_side(ref, count * rows, jnp.concatenate(collected, axis=0))

    vmem = pl.BlockSpec(memory_space=pltpu.VMEM)
    return pl.pallas_call(
        kernel,
        in_specs=[vmem] * 4 + [pl.BlockSpec(memory_space=pl.ANY)],
        out_specs=[vmem] * 4,
        out_shape=[
            jax.ShapeDtypeStruct((wide, tile_lon, rows, members), BF16),
            jax.ShapeDtypeStruct((wide, tile_lon, members), F32),
            jax.ShapeDtypeStruct((payload, members), BF16),
            jax.ShapeDtypeStruct((payload, members), BF16),
        ],
        compiler_params=PARAMS,
        cost_estimate=pl.CostEstimate(flops=10**6, bytes_accessed=3 * 10**6, transcendentals=0),
        name="widen",
    )(q, side, got_a, got_b, after)


def edge_weights(q_ref, side_ref, got_ref, edge, edge_ref, edge_side_ref, store):
    wide, tile_lon, rows, members = q_ref.shape
    tile_lat = wide - 4
    lat = lax.axis_index("lat")
    last = lax.axis_size("lat") - 1
    own, at = edge * (tile_lon - 2), edge * 2
    got_side = unpack_side(got_ref, 2 * wide * rows, 2 * wide)
    for i in range(wide):
        for j in range(2):
            k = (i * 2 + j) * rows
            edge_ref[i, at + j] = got_ref[k : k + rows, :]
            edge_ref[i, 2 - at + j] = q_ref[i, own + j]
        got_part = got_side[2 * i : 2 * i + 2]
        own_part = jnp.where(edge == 0, side_ref[i, :2, :], side_ref[i, tile_lon - 2 :, :])
        edge_side_ref[i, :2, :] = jnp.where(edge == 0, got_part, own_part)
        edge_side_ref[i, 2:, :] = jnp.where(edge == 0, own_part, got_part)
    grams = [row_grams([pair_of(edge_ref, i, 0), pair_of(edge_ref, i, 2)]) for i in range(wide)]
    base = identity(members)
    nodes = [(i, j) for i in range(tile_lat + 2) for j in range(2)]
    sums = [base + 0.5 * (grams[i][j] + grams[i + 2][j]) + grams[i + 1][j] for i, j in nodes]
    sides = [near_side(edge_side_ref, i, j) for i, j in nodes]
    for (i, j), w in zip(nodes, weights_of(sums, sides)):
        if i == 0:
            w = jnp.where(lat == 0, jnp.zeros_like(w), w)
        if i == tile_lat + 1:
            w = jnp.where(lat == last, jnp.zeros_like(w), w)
        store(i, j, w)


def edge_scratch(wide, rows, members):
    return [pltpu.VMEM((wide, 4, rows, members), BF16), pltpu.VMEM((wide, 4, members), F32)]


def near_edge(wide_q, wide_side, got_a):
    wide, tile_lon, rows, members = wide_q.shape

    def kernel(q_ref, side_ref, a_ref, out_ref, edge_ref, edge_side_ref):
        def store(i, j, w):
            out_ref[i, j] = w

        edge = 1 - lax.rem(lax.axis_index("lon"), 2)
        edge_weights(q_ref, side_ref, a_ref, edge, edge_ref, edge_side_ref, store)

    vmem = pl.BlockSpec(memory_space=pltpu.VMEM)
    return pl.pallas_call(
        kernel,
        in_specs=[vmem] * 3,
        out_specs=vmem,
        out_shape=jax.ShapeDtypeStruct((wide - 2, 2, members, members), BF16),
        scratch_shapes=edge_scratch(wide, rows, members),
        compiler_params=PARAMS,
        cost_estimate=pl.CostEstimate(flops=5 * 10**9, bytes_accessed=3 * 10**6, transcendentals=0),
        name="near_edge",
    )(wide_q, wide_side, got_a)


def finish(state, wide_q, wide_side, got_b, inner_w, lat_a_w, lat_b_w, near_w, columns):
    tile_lat, tile_lon, rows, members = state.shape
    wide = tile_lat + 4

    def kernel(
        state_ref, q_ref, side_ref, b_ref, inner_ref, lat_a_ref, lat_b_ref, near_ref, columns_ref,
        out_hbm, edge_ref, edge_side_ref, w_ref, perturb_ref, out_ref, sems,
    ):
        edge = lax.rem(lax.axis_index("lon"), 2)

        def store(i, j, w):
            w_ref[i, edge * tile_lon + j] = w

        edge_weights(q_ref, side_ref, b_ref, edge, edge_ref, edge_side_ref, store)
        for i in range(tile_lat - 2):
            w_ref[2 + i, 2:tile_lon] = inner_ref[i]
        odd = lax.rem(lax.axis_index("lat"), 2)
        for ref, south in ((lat_a_ref, 1 - odd), (lat_b_ref, odd)):
            w_ref[south * (tile_lat + 1), 2:tile_lon] = ref[0]
            w_ref[1 + south * (tile_lat - 1), 2:tile_lon] = ref[1]
        for i in range(tile_lat + 2):
            for j in range(2):
                w_ref[i, (1 - edge) * tile_lon + j] = near_ref[i, j]

        def analyse(i, carry):
            totals = []
            for j in range(tile_lon):
                x = state_ref[i, j].astype(F32)
                mean = jnp.sum(x, axis=1, keepdims=True) * (1.0 / members)
                centred = x - mean
                perturb_ref[j * rows : (j + 1) * rows, :] = centred.astype(BF16)
                totals.append(x - columns_ref[i, 4, j * rows : (j + 1) * rows, :] * centred)
            for n in range(tile_lon + 2):
                low, high = max(n - 2, 0), min(n, tile_lon - 1)
                near = jnp.concatenate([w_ref[i + a, n] for a in range(3)], axis=0)
                out = lax.dot_general(
                    perturb_ref[low * rows : (high + 1) * rows, :],
                    near,
                    (((1,), (1,)), ((), ())),
                    preferred_element_type=F32,
                )
                for j in range(low, high + 1):
                    here = out[(j - low) * rows : (j - low + 1) * rows]
                    span = slice(j * rows, (j + 1) * rows)
                    first, third = columns_ref[i, 0, span, :], columns_ref[i, 1, span, :]
                    along = (first, columns_ref[i, 4, span, :] - first - third, third)
                    mixed = 0.0
                    for a in range(3):
                        mixed = mixed + along[a] * here[:, a * members : (a + 1) * members]
                    if n - j == 1:
                        across = 1.0 - columns_ref[i, 2, span, :] - columns_ref[i, 3, span, :]
                    else:
                        across = columns_ref[i, 2 + (n - j) // 2, span, :]
                    totals[j] = totals[j] + across * mixed
                    if n == j + 2:
                        out_ref[i, j] = totals[j].astype(BF16)
            pltpu.make_async_copy(out_ref.at[i], out_hbm.at[i], sems.at[i]).start()
            return carry

        lax.fori_loop(0, tile_lat, analyse, 0)
        for i in range(tile_lat):
            pltpu.make_async_copy(out_ref.at[i], out_hbm.at[i], sems.at[i]).wait()

    vmem = pl.BlockSpec(memory_space=pltpu.VMEM)
    return pl.pallas_call(
        kernel,
        in_specs=[vmem] * 9,
        out_specs=pl.BlockSpec(memory_space=pltpu.HBM),
        out_shape=jax.ShapeDtypeStruct(state.shape, BF16),
        scratch_shapes=edge_scratch(wide, rows, members)
        + [
            pltpu.VMEM((tile_lat + 2, tile_lon + 2, members, members), BF16),
            pltpu.VMEM((tile_lon * rows, members), BF16),
            pltpu.VMEM(state.shape, BF16),
            pltpu.SemaphoreType.DMA((tile_lat,)),
        ],
        compiler_params=PARAMS,
        cost_estimate=pl.CostEstimate(flops=10**10, bytes_accessed=3 * 10**6, transcendentals=0),
        name="finish",
    )(state, wide_q, wide_side, got_b, inner_w, lat_a_w, lat_b_w, near_w, columns)


def body(state, obs_row, obs_count, obs_value, obs_weight, quadrant, frac_lat, frac_lon, land):
    send_a, side_a = prepare(state, obs_row, obs_count, obs_value, obs_weight)
    got_a = swap(send_a, "lat", 0)
    send_b, q, side, own_grams = complete(
        state, obs_row, obs_count, obs_value, obs_weight, send_a, side_a
    )
    got_b = swap_inner_lat(send_b)
    inner_w, columns = interior(side, own_grams, quadrant, frac_lat, frac_lon, land)
    lat_a_w = lat_edge(0, side, own_grams, got_a)
    wide_q, wide_side, to_a, to_b = widen(q, side, got_a, got_b, lat_a_w)
    lon_b = swap(to_b, "lon", 1)
    lon_a = swap(to_a, "lon", 0)
    lat_b_w = lat_edge(1, side, own_grams, got_b)
    near_w = near_edge(wide_q, wide_side, lon_a)
    return finish(state, wide_q, wide_side, lon_b, inner_w, lat_a_w, lat_b_w, near_w, columns)


def solution(mesh):
    cell = P("lat", "lon", None)
    return jax.shard_map(
        body,
        mesh=mesh,
        in_specs=(
            P("lat", "lon", None, None), cell, P("lat", "lon"), cell, cell, cell, cell, cell, cell,
        ),
        out_specs=P("lat", "lon", None, None),
        check_vma=False,
    )
```

```python
import math

import jax
import jax.numpy as jnp
from jax import lax
from jax.experimental import pallas as pl
from jax.experimental.pallas import tpu as pltpu
from jax.sharding import PartitionSpec as P

F32 = jnp.float32
BF16 = jnp.bfloat16
ITERS = 6
NEAR = (0.5, 1.0, 0.5)
PARAMS = pltpu.CompilerParams(vmem_limit_bytes=40 * 2**20)


def swap(x, axis, phase):
    count = lax.axis_size(axis)
    pairs = []
    for k in range(phase, count, 2):
        a, b = k, (k + 1) % count
        pairs += [(a, b), (b, a)]
    return lax.ppermute(x, axis, pairs)


def swap_inner_lat(x):
    lats, lons = lax.axis_size("lat"), lax.axis_size("lon")
    pairs = []
    for j in range(lons):
        for k in range(1, lats - 1, 2):
            a, b = k * lons + j, (k + 1) * lons + j
            pairs += [(a, b), (b, a)]
        for k in (0, lats - 1):
            pairs.append((k * lons + j, k * lons + (j ^ 1)))
    return lax.ppermute(x, ("lat", "lon"), pairs)


def split(x):
    high = x.astype(BF16)
    return high, (x - high.astype(F32)).astype(BF16)


def stream(pair):
    return jnp.concatenate(pair, axis=1)


def held(pair):
    row = jnp.concatenate(pair, axis=1)
    return jnp.concatenate([row, row], axis=0)


def product(a, b):
    out = jnp.dot(stream(a), held(b), preferred_element_type=F32)
    half = out.shape[1] // 2
    return out[:, :half] + out[:, half:]


def weights_of(grams, sides):
    members = grams[0].shape[0]
    rows = lax.broadcasted_iota(jnp.int32, (members, members), 0)
    cols = lax.broadcasted_iota(jnp.int32, (members, members), 1)
    eye = jnp.where(rows == cols, F32(1.0), F32(0.0))
    inv_frob = []
    iterates = []
    for gram in grams:
        total = jnp.sum(jnp.sum(gram * gram, axis=0, keepdims=True), axis=1, keepdims=True)
        inverse = lax.rsqrt(total)
        inv_frob.append(inverse)
        iterates.append(gram * inverse)
    first = [split(a) for a in iterates]
    squares, square_parts = iterates, first
    for step in range(0, ITERS, 2):
        inner = [
            product(part, part) + (3.375 * eye - 4.5 * x)
            for part, x in zip(square_parts, squares)
        ]
        inner_parts = [split(x) for x in inner]
        factors = [
            0.0625 * product(part, part) + ((24.609375 / 16) * eye - (8.625 / 16) * x)
            for part, x in zip(inner_parts, squares)
        ]
        factor_parts = [split(x) for x in factors]
        if step == 0:
            roots, root_parts = factors, factor_parts
        else:
            roots = [product(z, x) for z, x in zip(root_parts, factor_parts)]
        if step < ITERS - 2:
            if step > 0:
                root_parts = [split(z) for z in roots]
            half = [split(product(a, z)) for a, z in zip(first, root_parts)]
            squares = [product(x, z) for x, z in zip(half, root_parts)]
            square_parts = [split(x) for x in squares]
    out = []
    for root, side, inverse in zip(roots, sides, inv_frob):
        inner = jnp.sum(root * side, axis=1, keepdims=True)
        mean_weight = jnp.sum(root * inner, axis=0, keepdims=True) * inverse
        out.append((mean_weight + (math.sqrt(members - 1) * jnp.sqrt(inverse)) * root).astype(BF16))
    return out


def row_grams(pairs):
    turned = [pair.T for pair in pairs]
    rows = pairs[0].shape[0] // 2
    half = BF16(0.5)
    out = []
    for p in range(len(pairs) - 1):
        first, second = pairs[p], pairs[p + 1]
        zero = jnp.zeros((rows, first.shape[1]), BF16)
        left = jnp.concatenate([first[:rows] * half, first[rows:], second[:rows] * half, zero], axis=0)
        right = jnp.concatenate([zero, first[rows:] * half, second[:rows], second[rows:] * half], axis=0)
        both = jnp.dot(
            jnp.concatenate(turned[p : p + 2], axis=1),
            jnp.concatenate([left, right], axis=1),
            preferred_element_type=F32,
        )
        members = both.shape[0]
        out += [both[:, :members], both[:, members:]]
    return out


def pair_of(ref, i, j):
    pair = ref[i, j : j + 2]
    return pair.reshape(2 * pair.shape[1], pair.shape[2])


def node_sum(base, gram_ref, i, j):
    return base + 0.5 * (gram_ref[i, j] + gram_ref[i + 2, j]) + gram_ref[i + 1, j]


def near_side(side_ref, i, j):
    total = 0.0
    for a in range(3):
        for b in range(3):
            total = total + NEAR[a] * NEAR[b] * side_ref[i + a, j + b : j + b + 1, :]
    return total


def identity(members):
    rows = lax.broadcasted_iota(jnp.int32, (members, members), 0)
    cols = lax.broadcasted_iota(jnp.int32, (members, members), 1)
    return jnp.where(rows == cols, F32(members - 1), F32(0.0))


def pack_side(ref, at, side):
    high = side.astype(BF16).astype(F32)
    ref[at : at + 2 * side.shape[0], :] = jnp.concatenate([high, side - high], axis=0).astype(BF16)


def unpack_side(ref, at, count):
    both = ref[at : at + 2 * count, :].astype(F32)
    return both[:count] + both[count:]


def cell_copies(first, hbm_refs, refs, sems):
    copies = [pltpu.make_async_copy(hbm_refs[0], refs[0], sems.at[0])]
    for k in range(1, 5):
        source = hbm_refs[k].at[pl.ds(first, 2)]
        copies.append(pltpu.make_async_copy(source, refs[k], sems.at[k]))
    return copies


def cell_scratch(count, state, *rest):
    shapes = [pltpu.SMEM(count.shape, count.dtype)]
    for x in (state, *rest):
        shapes.append(pltpu.VMEM((2, *x.shape[1:]), x.dtype))
    return shapes + [pltpu.SemaphoreType.DMA((5,))]


def cell_rows(first, refs, payload_ref, side_ref):
    count_ref, state_ref, row_ref, value_ref, weight_ref = refs
    _, tile_lon, rows, members = state_ref.shape
    slots = row_ref.shape[2]
    lane = lax.broadcasted_iota(jnp.int32, (1, slots), 1)
    row_ids = lax.broadcasted_iota(jnp.int32, (rows, slots), 0)
    for i in range(2):
        for j in range(tile_lon):
            x = state_ref[i, j].astype(F32)
            mean = jnp.sum(x, axis=1, keepdims=True) * (1.0 / members)
            centred = x - mean
            live = jnp.where(lane < count_ref[first + i, j], weight_ref[i, j : j + 1, :], 0.0)
            hit = row_ids == row_ref[i, j : j + 1, :]
            centre = jnp.sum(jnp.where(hit, mean, 0.0), axis=0, keepdims=True)
            innovation = ((value_ref[i, j : j + 1, :] - centre) * live).astype(BF16).astype(F32)
            square = jnp.sum(jnp.where(hit, live * live, 0.0), axis=1, keepdims=True)
            pull = jnp.sum(jnp.where(hit, live * innovation, 0.0), axis=1, keepdims=True)
            k = i * tile_lon + j
            payload_ref[k * rows : (k + 1) * rows, :] = (centred * jnp.sqrt(square)).astype(BF16)
            side_ref[k : k + 1, :] = jnp.sum(centred * pull, axis=0, keepdims=True)
    pack_side(payload_ref, 2 * tile_lon * rows, side_ref[...])


def in_hbm(arrays):
    return [pltpu.with_memory_space_constraint(x, pltpu.HBM) for x in arrays]


def prepare(state, obs_row, obs_count, obs_value, obs_weight):
    tile_lat, tile_lon, rows, members = state.shape
    half = 2 * tile_lon
    arrays = (obs_count, state, obs_row, obs_value, obs_weight)

    def kernel(*refs):
        hbm_refs, (payload_ref, side_ref), cells, sems = refs[:5], refs[5:7], refs[7:12], refs[12]
        first = (1 - lax.rem(lax.axis_index("lat"), 2)) * (tile_lat - 2)
        copies = cell_copies(first, hbm_refs, cells, sems)
        for copy in copies:
            copy.start()
        for copy in copies:
            copy.wait()
        cell_rows(first, cells, payload_ref, side_ref)

    vmem = pl.BlockSpec(memory_space=pltpu.VMEM)
    return pl.pallas_call(
        kernel,
        in_specs=[pl.BlockSpec(memory_space=pltpu.HBM)] * 5,
        out_specs=[vmem] * 2,
        out_shape=[
            jax.ShapeDtypeStruct((half * rows + 2 * half, members), BF16),
            jax.ShapeDtypeStruct((half, members), F32),
        ],
        scratch_shapes=cell_scratch(*arrays),
        compiler_params=PARAMS,
        cost_estimate=pl.CostEstimate(flops=10**8, bytes_accessed=10**6, transcendentals=0),
        name="prepare",
    )(*in_hbm(arrays))


def complete(state, obs_row, obs_count, obs_value, obs_weight, first_rows, first_side, quadrant, frac_lat, frac_lon, land):
    tile_lat, tile_lon, rows, members = state.shape
    half = 2 * tile_lon
    arrays = (obs_count, state, obs_row, obs_value, obs_weight)
    placing = (quadrant, frac_lat, frac_lon, land)

    def kernel(*refs):
        hbm_refs, placing_hbm, (a_ref, a_side_ref) = refs[:5], refs[5:9], refs[9:11]
        b_ref, q_ref, side_ref, columns_ref, gram_ref = refs[11:16]
        cells, sems = refs[16:21], refs[21]
        b_side_ref, coef_ref = refs[22:24]
        placing_refs, placing_sems = refs[24:28], refs[28]
        quad_ref, flat_ref, flon_ref, land_ref = placing_refs
        odd = lax.rem(lax.axis_index("lat"), 2)
        a_first, b_first = (1 - odd) * (tile_lat - 2), odd * (tile_lat - 2)
        copies = cell_copies(b_first, hbm_refs, cells, sems)
        placing_copies = [
            pltpu.make_async_copy(source, target, placing_sems.at[k])
            for k, (source, target) in enumerate(zip(placing_hbm, placing_refs))
        ]
        for copy in copies + placing_copies:
            copy.start()

        def place(ref, part_ref, first):
            for i in range(2):
                side_ref[first + i] = part_ref[i * tile_lon : (i + 1) * tile_lon]
                pairs = []
                for j in range(0, tile_lon, 2):
                    k = (i * tile_lon + j) * rows
                    q_ref[first + i, j] = ref[k : k + rows, :]
                    q_ref[first + i, j + 1] = ref[k + rows : k + 2 * rows, :]
                    pairs.append(ref[k : k + 2 * rows, :])
                for j, gram in enumerate(row_grams(pairs)):
                    gram_ref[first + i, j] = gram

        place(a_ref, a_side_ref, a_first)
        coef_ref[...] = jnp.zeros_like(coef_ref)
        for copy in placing_copies:
            copy.wait()
        for i in range(tile_lat):
            quad = quad_ref[i]
            fa, fo = flat_ref[i], flon_ref[i]
            dry = jnp.where(land_ref[i] == 1, F32(1.0), F32(0.0))
            north, west = quad < 2, lax.rem(quad, 2) == 0
            zero = jnp.zeros_like(fa)
            coefs = (
                jnp.where(north, 1.0 - fa, zero) * dry,
                jnp.where(north, zero, fa) * dry,
                jnp.where(west, 1.0 - fo, zero),
                jnp.where(west, zero, fo),
                dry,
            )
            for k, coef in enumerate(coefs):
                coef_ref[i, k * tile_lon : (k + 1) * tile_lon, :rows] = coef
            turned = coef_ref[i].T
            for k in range(len(coefs)):
                for j in range(tile_lon):
                    at = k * tile_lon + j
                    columns_ref[i, k, j * rows : (j + 1) * rows, :] = jnp.broadcast_to(
                        turned[:rows, at : at + 1], (rows, members)
                    )
        for copy in copies:
            copy.wait()
        cell_rows(b_first, cells, b_ref, b_side_ref)
        place(b_ref, b_side_ref, b_first)

    vmem = pl.BlockSpec(memory_space=pltpu.VMEM)
    return pl.pallas_call(
        kernel,
        in_specs=[pl.BlockSpec(memory_space=pltpu.HBM)] * 9 + [vmem] * 2,
        out_specs=[vmem] * 5,
        out_shape=[
            jax.ShapeDtypeStruct(first_rows.shape, BF16),
            jax.ShapeDtypeStruct(state.shape, BF16),
            jax.ShapeDtypeStruct((tile_lat, tile_lon, members), F32),
            jax.ShapeDtypeStruct((tile_lat, 5, tile_lon * rows, members), F32),
            jax.ShapeDtypeStruct((tile_lat, tile_lon - 2, members, members), F32),
        ],
        scratch_shapes=cell_scratch(*arrays)
        + [pltpu.VMEM((half, members), F32), pltpu.VMEM((tile_lat, 128, 128), F32)]
        + [pltpu.VMEM(x.shape, x.dtype) for x in placing]
        + [pltpu.SemaphoreType.DMA((4,))],
        compiler_params=PARAMS,
        cost_estimate=pl.CostEstimate(flops=10**9, bytes_accessed=10**6, transcendentals=0),
        name="complete",
    )(*in_hbm(arrays), *in_hbm(placing), first_rows, first_side)


def interior(side, own_grams):
    tile_lat, tile_lon, members = side.shape

    def kernel(side_ref, gram_ref, out_ref):
        base = identity(members)
        nodes = [(i, j) for i in range(tile_lat - 2) for j in range(tile_lon - 2)]
        sums = [node_sum(base, gram_ref, i, j) for i, j in nodes]
        sides = [near_side(side_ref, i, j) for i, j in nodes]
        for (i, j), w in zip(nodes, weights_of(sums, sides)):
            out_ref[i, j] = w

    vmem = pl.BlockSpec(memory_space=pltpu.VMEM)
    return pl.pallas_call(
        kernel,
        in_specs=[vmem] * 2,
        out_specs=vmem,
        out_shape=jax.ShapeDtypeStruct((tile_lat - 2, tile_lon - 2, members, members), BF16),
        compiler_params=PARAMS,
        cost_estimate=pl.CostEstimate(flops=5 * 10**9, bytes_accessed=2 * 10**6, transcendentals=0),
        name="interior",
    )(side, own_grams)


def lat_edge(phase, side, own_grams, got):
    tile_lat, tile_lon, members = side.shape
    inner = tile_lon - 2
    count = 2 * tile_lon
    rows = got.shape[0] // count - 2

    def kernel(side_ref, own_ref, got_ref, out_ref, near_ref):
        lat = lax.axis_index("lat")
        south = (lax.rem(lat, 2) + phase + 1) % 2
        valid = jnp.where(south == 1, lat < lax.axis_size("lat") - 1, lat > 0)
        got_side = jnp.where(valid, unpack_side(got_ref, count * rows, count), 0.0)
        north_side, south_side = got_side[:tile_lon], got_side[tile_lon:]
        own, behind = south * (tile_lat - 1), 1 + south * (tile_lat - 3)
        near_ref[0] = jnp.where(south == 1, south_side, north_side)
        near_ref[1] = jnp.where(south == 1, north_side, south_side)
        near_ref[2] = side_ref[own]
        near_ref[3] = side_ref[behind]
        grams = []
        for first in (south, 1 - south):
            pairs = []
            for j in range(0, tile_lon, 2):
                start = pl.multiple_of((first * tile_lon + j) * rows, 2 * rows)
                pair = got_ref[pl.ds(start, 2 * rows), :]
                pairs.append(jnp.where(valid, pair, jnp.zeros_like(pair)))
            grams.append(row_grams(pairs))
        far, near = grams
        base = identity(members)
        sums = [base + 0.5 * (far[j] + own_ref[own, j]) + near[j] for j in range(inner)]
        sums += [base + 0.5 * (near[j] + own_ref[behind, j]) + own_ref[own, j] for j in range(inner)]
        sides = [near_side(near_ref, k, j) for k in range(2) for j in range(inner)]
        for n, w in enumerate(weights_of(sums, sides)):
            if n < inner:
                w = jnp.where(valid, w, jnp.zeros_like(w))
            out_ref[n // inner, n % inner] = w

    vmem = pl.BlockSpec(memory_space=pltpu.VMEM)
    return pl.pallas_call(
        kernel,
        in_specs=[vmem] * 3,
        out_specs=vmem,
        out_shape=jax.ShapeDtypeStruct((2, inner, members, members), BF16),
        scratch_shapes=[pltpu.VMEM((4, tile_lon, members), F32)],
        compiler_params=PARAMS,
        cost_estimate=pl.CostEstimate(flops=5 * 10**9, bytes_accessed=2 * 10**6, transcendentals=0),
        name="lat_edge",
    )(side, own_grams, got)


def widen(q, side, got_a, got_b, after):
    tile_lat, tile_lon, rows, members = q.shape
    half = 2 * tile_lon
    wide = tile_lat + 4
    count = 2 * wide
    payload = count * rows + 2 * count

    def kernel(
        q_ref, side_ref, a_ref, b_ref, after_ref, wide_ref, wide_side_ref, to_a_ref, to_b_ref,
    ):
        lat = lax.axis_index("lat")
        lon = lax.axis_index("lon")
        lat_odd = lax.rem(lat, 2)
        lon_odd = lax.rem(lon, 2)
        wide_ref[2 : 2 + tile_lat] = q_ref[...]
        wide_side_ref[2 : 2 + tile_lat] = side_ref[...]
        last = lax.axis_size("lat") - 1
        a_valid = jnp.where(lat_odd == 0, lat < last, lat > 0)
        b_valid = jnp.where(lat_odd == 0, lat > 0, lat < last)
        for ref, first, valid in (
            (a_ref, (1 - lat_odd) * (tile_lat + 2), a_valid),
            (b_ref, lat_odd * (tile_lat + 2), b_valid),
        ):
            total = jnp.where(valid, unpack_side(ref, half * rows, half), 0.0)
            for i in range(2):
                wide_side_ref[first + i] = total[i * tile_lon : (i + 1) * tile_lon]
                for j in range(tile_lon):
                    k = (i * tile_lon + j) * rows
                    piece = ref[k : k + rows, :]
                    wide_ref[first + i, j] = jnp.where(valid, piece, jnp.zeros_like(piece))
        for ref, first in ((to_a_ref, (1 - lon_odd) * (tile_lon - 2)), (to_b_ref, lon_odd * (tile_lon - 2))):
            collected = []
            for i in range(wide):
                for j in range(2):
                    k = (i * 2 + j) * rows
                    ref[k : k + rows, :] = wide_ref[i, first + j]
                    collected.append(wide_side_ref[i, pl.ds(first + j, 1), :])
            pack_side(ref, count * rows, jnp.concatenate(collected, axis=0))

    vmem = pl.BlockSpec(memory_space=pltpu.VMEM)
    return pl.pallas_call(
        kernel,
        in_specs=[vmem] * 4 + [pl.BlockSpec(memory_space=pl.ANY)],
        out_specs=[vmem] * 4,
        out_shape=[
            jax.ShapeDtypeStruct((wide, tile_lon, rows, members), BF16),
            jax.ShapeDtypeStruct((wide, tile_lon, members), F32),
            jax.ShapeDtypeStruct((payload, members), BF16),
            jax.ShapeDtypeStruct((payload, members), BF16),
        ],
        compiler_params=PARAMS,
        cost_estimate=pl.CostEstimate(flops=10**6, bytes_accessed=3 * 10**6, transcendentals=0),
        name="widen",
    )(q, side, got_a, got_b, after)


def edge_weights(q_ref, side_ref, got_ref, edge, edge_ref, edge_side_ref, store):
    wide, tile_lon, rows, members = q_ref.shape
    tile_lat = wide - 4
    lat = lax.axis_index("lat")
    last = lax.axis_size("lat") - 1
    own, at = edge * (tile_lon - 2), edge * 2
    got_side = unpack_side(got_ref, 2 * wide * rows, 2 * wide)
    for i in range(wide):
        for j in range(2):
            k = (i * 2 + j) * rows
            edge_ref[i, at + j] = got_ref[k : k + rows, :]
            edge_ref[i, 2 - at + j] = q_ref[i, own + j]
        got_part = got_side[2 * i : 2 * i + 2]
        own_part = jnp.where(edge == 0, side_ref[i, :2, :], side_ref[i, tile_lon - 2 :, :])
        edge_side_ref[i, :2, :] = jnp.where(edge == 0, got_part, own_part)
        edge_side_ref[i, 2:, :] = jnp.where(edge == 0, own_part, got_part)
    grams = [row_grams([pair_of(edge_ref, i, 0), pair_of(edge_ref, i, 2)]) for i in range(wide)]
    base = identity(members)
    nodes = [(i, j) for i in range(tile_lat + 2) for j in range(2)]
    sums = [base + 0.5 * (grams[i][j] + grams[i + 2][j]) + grams[i + 1][j] for i, j in nodes]
    sides = [near_side(edge_side_ref, i, j) for i, j in nodes]
    for (i, j), w in zip(nodes, weights_of(sums, sides)):
        if i == 0:
            w = jnp.where(lat == 0, jnp.zeros_like(w), w)
        if i == tile_lat + 1:
            w = jnp.where(lat == last, jnp.zeros_like(w), w)
        store(i, j, w)


def edge_scratch(wide, rows, members):
    return [pltpu.VMEM((wide, 4, rows, members), BF16), pltpu.VMEM((wide, 4, members), F32)]


def near_edge(wide_q, wide_side, got_a):
    wide, tile_lon, rows, members = wide_q.shape

    def kernel(q_ref, side_ref, a_ref, out_ref, edge_ref, edge_side_ref):
        def store(i, j, w):
            out_ref[i, j] = w

        edge = 1 - lax.rem(lax.axis_index("lon"), 2)
        edge_weights(q_ref, side_ref, a_ref, edge, edge_ref, edge_side_ref, store)

    vmem = pl.BlockSpec(memory_space=pltpu.VMEM)
    return pl.pallas_call(
        kernel,
        in_specs=[vmem] * 3,
        out_specs=vmem,
        out_shape=jax.ShapeDtypeStruct((wide - 2, 2, members, members), BF16),
        scratch_shapes=edge_scratch(wide, rows, members),
        compiler_params=PARAMS,
        cost_estimate=pl.CostEstimate(flops=5 * 10**9, bytes_accessed=3 * 10**6, transcendentals=0),
        name="near_edge",
    )(wide_q, wide_side, got_a)


def finish(state, wide_q, wide_side, got_b, inner_w, lat_a_w, lat_b_w, near_w, columns):
    tile_lat, tile_lon, rows, members = state.shape
    wide = tile_lat + 4

    def kernel(
        state_ref, q_ref, side_ref, b_ref, inner_ref, lat_a_ref, lat_b_ref, near_ref, columns_ref,
        out_hbm, edge_ref, edge_side_ref, w_ref, perturb_ref, out_ref, sems,
    ):
        edge = lax.rem(lax.axis_index("lon"), 2)

        def store(i, j, w):
            w_ref[i, edge * tile_lon + j] = w

        edge_weights(q_ref, side_ref, b_ref, edge, edge_ref, edge_side_ref, store)
        for i in range(tile_lat - 2):
            w_ref[2 + i, 2:tile_lon] = inner_ref[i]
        odd = lax.rem(lax.axis_index("lat"), 2)
        for ref, south in ((lat_a_ref, 1 - odd), (lat_b_ref, odd)):
            w_ref[south * (tile_lat + 1), 2:tile_lon] = ref[0]
            w_ref[1 + south * (tile_lat - 1), 2:tile_lon] = ref[1]
        for i in range(tile_lat + 2):
            for j in range(2):
                w_ref[i, (1 - edge) * tile_lon + j] = near_ref[i, j]

        def analyse(i, carry):
            totals = []
            for j in range(tile_lon):
                x = state_ref[i, j].astype(F32)
                mean = jnp.sum(x, axis=1, keepdims=True) * (1.0 / members)
                centred = x - mean
                perturb_ref[j * rows : (j + 1) * rows, :] = centred.astype(BF16)
                totals.append(x - columns_ref[i, 4, j * rows : (j + 1) * rows, :] * centred)
            for n in range(tile_lon + 2):
                low, high = max(n - 2, 0), min(n, tile_lon - 1)
                near = jnp.concatenate([w_ref[i + a, n] for a in range(3)], axis=0)
                out = lax.dot_general(
                    perturb_ref[low * rows : (high + 1) * rows, :],
                    near,
                    (((1,), (1,)), ((), ())),
                    preferred_element_type=F32,
                )
                for j in range(low, high + 1):
                    here = out[(j - low) * rows : (j - low + 1) * rows]
                    span = slice(j * rows, (j + 1) * rows)
                    first, third = columns_ref[i, 0, span, :], columns_ref[i, 1, span, :]
                    along = (first, columns_ref[i, 4, span, :] - first - third, third)
                    mixed = 0.0
                    for a in range(3):
                        mixed = mixed + along[a] * here[:, a * members : (a + 1) * members]
                    if n - j == 1:
                        across = 1.0 - columns_ref[i, 2, span, :] - columns_ref[i, 3, span, :]
                    else:
                        across = columns_ref[i, 2 + (n - j) // 2, span, :]
                    totals[j] = totals[j] + across * mixed
                    if n == j + 2:
                        out_ref[i, j] = totals[j].astype(BF16)
            pltpu.make_async_copy(out_ref.at[i], out_hbm.at[i], sems.at[i]).start()
            return carry

        lax.fori_loop(0, tile_lat, analyse, 0)
        for i in range(tile_lat):
            pltpu.make_async_copy(out_ref.at[i], out_hbm.at[i], sems.at[i]).wait()

    vmem = pl.BlockSpec(memory_space=pltpu.VMEM)
    return pl.pallas_call(
        kernel,
        in_specs=[vmem] * 9,
        out_specs=pl.BlockSpec(memory_space=pltpu.HBM),
        out_shape=jax.ShapeDtypeStruct(state.shape, BF16),
        scratch_shapes=edge_scratch(wide, rows, members)
        + [
            pltpu.VMEM((tile_lat + 2, tile_lon + 2, members, members), BF16),
            pltpu.VMEM((tile_lon * rows, members), BF16),
            pltpu.VMEM(state.shape, BF16),
            pltpu.SemaphoreType.DMA((tile_lat,)),
        ],
        compiler_params=PARAMS,
        cost_estimate=pl.CostEstimate(flops=10**10, bytes_accessed=3 * 10**6, transcendentals=0),
        name="finish",
    )(state, wide_q, wide_side, got_b, inner_w, lat_a_w, lat_b_w, near_w, columns)


def body(state, obs_row, obs_count, obs_value, obs_weight, quadrant, frac_lat, frac_lon, land):
    send_a, side_a = prepare(state, obs_row, obs_count, obs_value, obs_weight)
    got_a = swap(send_a, "lat", 0)
    send_b, q, side, columns, own_grams = complete(
        state, obs_row, obs_count, obs_value, obs_weight, send_a, side_a, quadrant, frac_lat, frac_lon, land
    )
    got_b = swap_inner_lat(send_b)
    inner_w = interior(side, own_grams)
    lat_a_w = lat_edge(0, side, own_grams, got_a)
    wide_q, wide_side, to_a, to_b = widen(q, side, got_a, got_b, lat_a_w)
    lon_b = swap(to_b, "lon", 1)
    lon_a = swap(to_a, "lon", 0)
    lat_b_w = lat_edge(1, side, own_grams, got_b)
    near_w = near_edge(wide_q, wide_side, lon_a)
    return finish(state, wide_q, wide_side, lon_b, inner_w, lat_a_w, lat_b_w, near_w, columns)


def solution(mesh):
    cell = P("lat", "lon", None)
    return jax.shard_map(
        body,
        mesh=mesh,
        in_specs=(
            P("lat", "lon", None, None), cell, P("lat", "lon"), cell, cell, cell, cell, cell, cell,
        ),
        out_specs=P("lat", "lon", None, None),
        check_vma=False,
    )
```

```python
import math

import jax
import jax.numpy as jnp
from jax import lax
from jax.experimental import pallas as pl
from jax.experimental.pallas import tpu as pltpu
from jax.sharding import PartitionSpec as P

F32 = jnp.float32
BF16 = jnp.bfloat16
ITERS = 6
NEAR = (0.5, 1.0, 0.5)
PARAMS = pltpu.CompilerParams(vmem_limit_bytes=40 * 2**20)


def swap(x, axis, phase):
    count = lax.axis_size(axis)
    pairs = []
    for k in range(phase, count, 2):
        a, b = k, (k + 1) % count
        pairs += [(a, b), (b, a)]
    return lax.ppermute(x, axis, pairs)


def swap_inner_lat(x):
    lats, lons = lax.axis_size("lat"), lax.axis_size("lon")
    pairs = []
    for j in range(lons):
        for k in range(1, lats - 1, 2):
            a, b = k * lons + j, (k + 1) * lons + j
            pairs += [(a, b), (b, a)]
        for k in (0, lats - 1):
            pairs.append((k * lons + j, k * lons + (j ^ 1)))
    return lax.ppermute(x, ("lat", "lon"), pairs)


def split(x):
    high = x.astype(BF16)
    return high, (x - high.astype(F32)).astype(BF16)


def stream(pair):
    return jnp.concatenate(pair, axis=1)


def held(pair):
    row = jnp.concatenate(pair, axis=1)
    return jnp.concatenate([row, row], axis=0)


def product(a, b):
    out = jnp.dot(stream(a), held(b), preferred_element_type=F32)
    half = out.shape[1] // 2
    return out[:, :half] + out[:, half:]


def weights_of(grams, sides):
    members = grams[0].shape[0]
    rows = lax.broadcasted_iota(jnp.int32, (members, members), 0)
    cols = lax.broadcasted_iota(jnp.int32, (members, members), 1)
    eye = jnp.where(rows == cols, F32(1.0), F32(0.0))
    inv_frob = []
    iterates = []
    for gram in grams:
        total = jnp.sum(jnp.sum(gram * gram, axis=0, keepdims=True), axis=1, keepdims=True)
        inverse = lax.rsqrt(total)
        inv_frob.append(inverse)
        iterates.append(gram * inverse)
    first = [split(a) for a in iterates]
    squares, square_parts = iterates, first
    for step in range(0, ITERS, 2):
        inner = [
            product(part, part) + (3.375 * eye - 4.5 * x)
            for part, x in zip(square_parts, squares)
        ]
        inner_parts = [split(x) for x in inner]
        factors = [
            0.0625 * product(part, part) + ((24.609375 / 16) * eye - (8.625 / 16) * x)
            for part, x in zip(inner_parts, squares)
        ]
        factor_parts = [split(x) for x in factors]
        if step == 0:
            roots, root_parts = factors, factor_parts
        else:
            roots = [product(z, x) for z, x in zip(root_parts, factor_parts)]
        if step < ITERS - 2:
            if step > 0:
                root_parts = [split(z) for z in roots]
            half = [split(product(a, z)) for a, z in zip(first, root_parts)]
            squares = [product(x, z) for x, z in zip(half, root_parts)]
            square_parts = [split(x) for x in squares]
    out = []
    for root, side, inverse in zip(roots, sides, inv_frob):
        inner = jnp.sum(root * side, axis=1, keepdims=True)
        mean_weight = jnp.sum(root * inner, axis=0, keepdims=True) * inverse
        out.append((mean_weight + (math.sqrt(members - 1) * jnp.sqrt(inverse)) * root).astype(BF16))
    return out


def row_grams(pairs):
    turned = [pair.T for pair in pairs]
    rows = pairs[0].shape[0] // 2
    half = BF16(0.5)
    out = []
    for p in range(len(pairs) - 1):
        first, second = pairs[p], pairs[p + 1]
        zero = jnp.zeros((rows, first.shape[1]), BF16)
        left = jnp.concatenate([first[:rows] * half, first[rows:], second[:rows] * half, zero], axis=0)
        right = jnp.concatenate([zero, first[rows:] * half, second[:rows], second[rows:] * half], axis=0)
        both = jnp.dot(
            jnp.concatenate(turned[p : p + 2], axis=1),
            jnp.concatenate([left, right], axis=1),
            preferred_element_type=F32,
        )
        members = both.shape[0]
        out += [both[:, :members], both[:, members:]]
    return out


def pair_of(ref, i, j):
    pair = ref[i, j : j + 2]
    return pair.reshape(2 * pair.shape[1], pair.shape[2])


def node_sum(base, gram_ref, i, j):
    return base + 0.5 * (gram_ref[i, j] + gram_ref[i + 2, j]) + gram_ref[i + 1, j]


def near_side(side_ref, i, j):
    total = 0.0
    for a in range(3):
        for b in range(3):
            total = total + NEAR[a] * NEAR[b] * side_ref[i + a, j + b : j + b + 1, :]
    return total


def identity(members):
    rows = lax.broadcasted_iota(jnp.int32, (members, members), 0)
    cols = lax.broadcasted_iota(jnp.int32, (members, members), 1)
    return jnp.where(rows == cols, F32(members - 1), F32(0.0))


def pack_side(ref, at, side):
    high = side.astype(BF16).astype(F32)
    ref[at : at + 2 * side.shape[0], :] = jnp.concatenate([high, side - high], axis=0).astype(BF16)


def unpack_side(ref, at, count):
    both = ref[at : at + 2 * count, :].astype(F32)
    return both[:count] + both[count:]


def cell_copies(first, hbm_refs, refs, sems):
    copies = [pltpu.make_async_copy(hbm_refs[0], refs[0], sems.at[0])]
    for k in range(1, 5):
        source = hbm_refs[k].at[pl.ds(first, 2)]
        copies.append(pltpu.make_async_copy(source, refs[k], sems.at[k]))
    return copies


def cell_scratch(count, state, *rest):
    shapes = [pltpu.SMEM(count.shape, count.dtype)]
    for x in (state, *rest):
        shapes.append(pltpu.VMEM((2, *x.shape[1:]), x.dtype))
    return shapes + [pltpu.SemaphoreType.DMA((5,))]


def cell_rows(first, refs, payload_ref, side_ref):
    count_ref, state_ref, row_ref, value_ref, weight_ref = refs
    _, tile_lon, rows, members = state_ref.shape
    slots = row_ref.shape[2]
    lane = lax.broadcasted_iota(jnp.int32, (1, slots), 1)
    row_ids = lax.broadcasted_iota(jnp.int32, (rows, slots), 0)
    for i in range(2):
        for j in range(tile_lon):
            x = state_ref[i, j].astype(F32)
            mean = jnp.sum(x, axis=1, keepdims=True) * (1.0 / members)
            centred = x - mean
            live = jnp.where(lane < count_ref[first + i, j], weight_ref[i, j : j + 1, :], 0.0)
            hit = row_ids == row_ref[i, j : j + 1, :]
            centre = jnp.sum(jnp.where(hit, mean, 0.0), axis=0, keepdims=True)
            innovation = ((value_ref[i, j : j + 1, :] - centre) * live).astype(BF16).astype(F32)
            square = jnp.sum(jnp.where(hit, live * live, 0.0), axis=1, keepdims=True)
            pull = jnp.sum(jnp.where(hit, live * innovation, 0.0), axis=1, keepdims=True)
            k = i * tile_lon + j
            payload_ref[k * rows : (k + 1) * rows, :] = (centred * jnp.sqrt(square)).astype(BF16)
            side_ref[k : k + 1, :] = jnp.sum(centred * pull, axis=0, keepdims=True)
    pack_side(payload_ref, 2 * tile_lon * rows, side_ref[...])


def in_hbm(arrays):
    return [pltpu.with_memory_space_constraint(x, pltpu.HBM) for x in arrays]


def prepare(state, obs_row, obs_count, obs_value, obs_weight):
    tile_lat, tile_lon, rows, members = state.shape
    half = 2 * tile_lon
    arrays = (obs_count, state, obs_row, obs_value, obs_weight)

    def kernel(*refs):
        hbm_refs, (payload_ref, side_ref), cells, sems = refs[:5], refs[5:7], refs[7:12], refs[12]
        first = (1 - lax.rem(lax.axis_index("lat"), 2)) * (tile_lat - 2)
        copies = cell_copies(first, hbm_refs, cells, sems)
        for copy in copies:
            copy.start()
        for copy in copies:
            copy.wait()
        cell_rows(first, cells, payload_ref, side_ref)

    vmem = pl.BlockSpec(memory_space=pltpu.VMEM)
    return pl.pallas_call(
        kernel,
        in_specs=[pl.BlockSpec(memory_space=pltpu.HBM)] * 5,
        out_specs=[vmem] * 2,
        out_shape=[
            jax.ShapeDtypeStruct((half * rows + 2 * half, members), BF16),
            jax.ShapeDtypeStruct((half, members), F32),
        ],
        scratch_shapes=cell_scratch(*arrays),
        compiler_params=PARAMS,
        cost_estimate=pl.CostEstimate(flops=10**8, bytes_accessed=10**6, transcendentals=0),
        name="prepare",
    )(*in_hbm(arrays))


def complete(state, obs_row, obs_count, obs_value, obs_weight, first_rows, first_side, quadrant, frac_lat, frac_lon, land):
    tile_lat, tile_lon, rows, members = state.shape
    half = 2 * tile_lon
    arrays = (obs_count, state, obs_row, obs_value, obs_weight)
    placing = (quadrant, frac_lat, frac_lon, land)

    def kernel(*refs):
        hbm_refs, placing_hbm, (a_ref, a_side_ref) = refs[:5], refs[5:9], refs[9:11]
        b_ref, q_ref, side_ref, columns_ref, gram_ref = refs[11:16]
        cells, sems = refs[16:21], refs[21]
        b_side_ref, coef_ref = refs[22:24]
        placing_refs, placing_sems = refs[24:28], refs[28]
        quad_ref, flat_ref, flon_ref, land_ref = placing_refs
        odd = lax.rem(lax.axis_index("lat"), 2)
        a_first, b_first = (1 - odd) * (tile_lat - 2), odd * (tile_lat - 2)
        copies = cell_copies(b_first, hbm_refs, cells, sems)
        placing_copies = [
            pltpu.make_async_copy(source, target, placing_sems.at[k])
            for k, (source, target) in enumerate(zip(placing_hbm, placing_refs))
        ]
        for copy in copies + placing_copies:
            copy.start()

        def place(ref, part_ref, first):
            for i in range(2):
                side_ref[first + i] = part_ref[i * tile_lon : (i + 1) * tile_lon]
                pairs = []
                for j in range(0, tile_lon, 2):
                    k = (i * tile_lon + j) * rows
                    q_ref[first + i, j] = ref[k : k + rows, :]
                    q_ref[first + i, j + 1] = ref[k + rows : k + 2 * rows, :]
                    pairs.append(ref[k : k + 2 * rows, :])
                for j, gram in enumerate(row_grams(pairs)):
                    gram_ref[first + i, j] = gram

        place(a_ref, a_side_ref, a_first)
        coef_ref[...] = jnp.zeros_like(coef_ref)
        for copy in placing_copies:
            copy.wait()
        for i in range(tile_lat):
            quad = quad_ref[i]
            fa, fo = flat_ref[i], flon_ref[i]
            dry = jnp.where(land_ref[i] == 1, F32(1.0), F32(0.0))
            north, west = quad < 2, lax.rem(quad, 2) == 0
            zero = jnp.zeros_like(fa)
            coefs = (
                jnp.where(north, 1.0 - fa, zero) * dry,
                jnp.where(north, zero, fa) * dry,
                jnp.where(west, 1.0 - fo, zero),
                jnp.where(west, zero, fo),
                dry,
            )
            for k, coef in enumerate(coefs):
                coef_ref[i, k * tile_lon : (k + 1) * tile_lon, :rows] = coef
            turned = coef_ref[i].T
            for k in range(len(coefs)):
                for j in range(tile_lon):
                    at = k * tile_lon + j
                    columns_ref[i, k, j * rows : (j + 1) * rows, :] = jnp.broadcast_to(
                        turned[:rows, at : at + 1], (rows, members)
                    )
        for copy in copies:
            copy.wait()
        cell_rows(b_first, cells, b_ref, b_side_ref)
        place(b_ref, b_side_ref, b_first)

    vmem = pl.BlockSpec(memory_space=pltpu.VMEM)
    return pl.pallas_call(
        kernel,
        in_specs=[pl.BlockSpec(memory_space=pltpu.HBM)] * 9 + [vmem] * 2,
        out_specs=[vmem] * 5,
        out_shape=[
            jax.ShapeDtypeStruct(first_rows.shape, BF16),
            jax.ShapeDtypeStruct(state.shape, BF16),
            jax.ShapeDtypeStruct((tile_lat, tile_lon, members), F32),
            jax.ShapeDtypeStruct((tile_lat, 5, tile_lon * rows, members), F32),
            jax.ShapeDtypeStruct((tile_lat, tile_lon - 2, members, members), F32),
        ],
        scratch_shapes=cell_scratch(*arrays)
        + [pltpu.VMEM((half, members), F32), pltpu.VMEM((tile_lat, 128, 128), F32)]
        + [pltpu.VMEM(x.shape, x.dtype) for x in placing]
        + [pltpu.SemaphoreType.DMA((4,))],
        compiler_params=PARAMS,
        cost_estimate=pl.CostEstimate(flops=10**9, bytes_accessed=10**6, transcendentals=0),
        name="complete",
    )(*in_hbm(arrays), *in_hbm(placing), first_rows, first_side)


def interior(side, own_grams):
    tile_lat, tile_lon, members = side.shape

    def kernel(side_ref, gram_ref, out_ref):
        base = identity(members)
        nodes = [(i, j) for i in range(tile_lat - 2) for j in range(tile_lon - 2)]
        sums = [node_sum(base, gram_ref, i, j) for i, j in nodes]
        sides = [near_side(side_ref, i, j) for i, j in nodes]
        for (i, j), w in zip(nodes, weights_of(sums, sides)):
            out_ref[i, j] = w

    vmem = pl.BlockSpec(memory_space=pltpu.VMEM)
    return pl.pallas_call(
        kernel,
        in_specs=[vmem] * 2,
        out_specs=vmem,
        out_shape=jax.ShapeDtypeStruct((tile_lat - 2, tile_lon - 2, members, members), BF16),
        compiler_params=PARAMS,
        cost_estimate=pl.CostEstimate(flops=5 * 10**9, bytes_accessed=2 * 10**6, transcendentals=0),
        name="interior",
    )(side, own_grams)


def lat_edge(phase, side, own_grams, got):
    tile_lat, tile_lon, members = side.shape
    inner = tile_lon - 2
    count = 2 * tile_lon
    rows = got.shape[0] // count - 2

    def kernel(side_ref, own_ref, got_ref, out_ref, near_ref):
        lat = lax.axis_index("lat")
        south = (lax.rem(lat, 2) + phase + 1) % 2
        valid = jnp.where(south == 1, lat < lax.axis_size("lat") - 1, lat > 0)
        got_side = jnp.where(valid, unpack_side(got_ref, count * rows, count), 0.0)
        north_side, south_side = got_side[:tile_lon], got_side[tile_lon:]
        own, behind = south * (tile_lat - 1), 1 + south * (tile_lat - 3)
        near_ref[0] = jnp.where(south == 1, south_side, north_side)
        near_ref[1] = jnp.where(south == 1, north_side, south_side)
        near_ref[2] = side_ref[own]
        near_ref[3] = side_ref[behind]
        grams = []
        for first in (south, 1 - south):
            pairs = []
            for j in range(0, tile_lon, 2):
                start = pl.multiple_of((first * tile_lon + j) * rows, 2 * rows)
                pair = got_ref[pl.ds(start, 2 * rows), :]
                pairs.append(jnp.where(valid, pair, jnp.zeros_like(pair)))
            grams.append(row_grams(pairs))
        far, near = grams
        base = identity(members)
        sums = [base + 0.5 * (far[j] + own_ref[own, j]) + near[j] for j in range(inner)]
        sums += [base + 0.5 * (near[j] + own_ref[behind, j]) + own_ref[own, j] for j in range(inner)]
        sides = [near_side(near_ref, k, j) for k in range(2) for j in range(inner)]
        for n, w in enumerate(weights_of(sums, sides)):
            if n < inner:
                w = jnp.where(valid, w, jnp.zeros_like(w))
            out_ref[n // inner, n % inner] = w

    vmem = pl.BlockSpec(memory_space=pltpu.VMEM)
    return pl.pallas_call(
        kernel,
        in_specs=[vmem] * 3,
        out_specs=vmem,
        out_shape=jax.ShapeDtypeStruct((2, inner, members, members), BF16),
        scratch_shapes=[pltpu.VMEM((4, tile_lon, members), F32)],
        compiler_params=PARAMS,
        cost_estimate=pl.CostEstimate(flops=5 * 10**9, bytes_accessed=2 * 10**6, transcendentals=0),
        name="lat_edge",
    )(side, own_grams, got)


def widen(q, side, got_a, got_b, after):
    tile_lat, tile_lon, rows, members = q.shape
    half = 2 * tile_lon
    wide = tile_lat + 4
    count = 2 * wide
    payload = count * rows + 2 * count

    def kernel(
        q_ref, side_ref, a_ref, b_ref, after_ref, wide_ref, wide_side_ref, to_a_ref, to_b_ref,
    ):
        lat = lax.axis_index("lat")
        lon = lax.axis_index("lon")
        lat_odd = lax.rem(lat, 2)
        lon_odd = lax.rem(lon, 2)
        wide_ref[2 : 2 + tile_lat] = q_ref[...]
        wide_side_ref[2 : 2 + tile_lat] = side_ref[...]
        last = lax.axis_size("lat") - 1
        a_valid = jnp.where(lat_odd == 0, lat < last, lat > 0)
        b_valid = jnp.where(lat_odd == 0, lat > 0, lat < last)
        for ref, first, valid in (
            (a_ref, (1 - lat_odd) * (tile_lat + 2), a_valid),
            (b_ref, lat_odd * (tile_lat + 2), b_valid),
        ):
            total = jnp.where(valid, unpack_side(ref, half * rows, half), 0.0)
            for i in range(2):
                wide_side_ref[first + i] = total[i * tile_lon : (i + 1) * tile_lon]
                for j in range(tile_lon):
                    k = (i * tile_lon + j) * rows
                    piece = ref[k : k + rows, :]
                    wide_ref[first + i, j] = jnp.where(valid, piece, jnp.zeros_like(piece))
        for ref, first in ((to_a_ref, (1 - lon_odd) * (tile_lon - 2)), (to_b_ref, lon_odd * (tile_lon - 2))):
            collected = []
            for i in range(wide):
                for j in range(2):
                    k = (i * 2 + j) * rows
                    ref[k : k + rows, :] = wide_ref[i, first + j]
                    collected.append(wide_side_ref[i, pl.ds(first + j, 1), :])
            pack_side(ref, count * rows, jnp.concatenate(collected, axis=0))

    vmem = pl.BlockSpec(memory_space=pltpu.VMEM)
    return pl.pallas_call(
        kernel,
        in_specs=[vmem] * 4 + [pl.BlockSpec(memory_space=pl.ANY)],
        out_specs=[vmem] * 4,
        out_shape=[
            jax.ShapeDtypeStruct((wide, tile_lon, rows, members), BF16),
            jax.ShapeDtypeStruct((wide, tile_lon, members), F32),
            jax.ShapeDtypeStruct((payload, members), BF16),
            jax.ShapeDtypeStruct((payload, members), BF16),
        ],
        compiler_params=PARAMS,
        cost_estimate=pl.CostEstimate(flops=10**6, bytes_accessed=3 * 10**6, transcendentals=0),
        name="widen",
    )(q, side, got_a, got_b, after)


def edge_weights(q_ref, side_ref, got_ref, edge, edge_ref, edge_side_ref, store):
    wide, tile_lon, rows, members = q_ref.shape
    tile_lat = wide - 4
    lat = lax.axis_index("lat")
    last = lax.axis_size("lat") - 1
    own, at = edge * (tile_lon - 2), edge * 2
    got_side = unpack_side(got_ref, 2 * wide * rows, 2 * wide)
    for i in range(wide):
        for j in range(2):
            k = (i * 2 + j) * rows
            edge_ref[i, at + j] = got_ref[k : k + rows, :]
            edge_ref[i, 2 - at + j] = q_ref[i, own + j]
        got_part = got_side[2 * i : 2 * i + 2]
        own_part = jnp.where(edge == 0, side_ref[i, :2, :], side_ref[i, tile_lon - 2 :, :])
        edge_side_ref[i, :2, :] = jnp.where(edge == 0, got_part, own_part)
        edge_side_ref[i, 2:, :] = jnp.where(edge == 0, own_part, got_part)
    grams = [row_grams([pair_of(edge_ref, i, 0), pair_of(edge_ref, i, 2)]) for i in range(wide)]
    base = identity(members)
    nodes = [(i, j) for i in range(tile_lat + 2) for j in range(2)]
    sums = [base + 0.5 * (grams[i][j] + grams[i + 2][j]) + grams[i + 1][j] for i, j in nodes]
    sides = [near_side(edge_side_ref, i, j) for i, j in nodes]
    for (i, j), w in zip(nodes, weights_of(sums, sides)):
        if i == 0:
            w = jnp.where(lat == 0, jnp.zeros_like(w), w)
        if i == tile_lat + 1:
            w = jnp.where(lat == last, jnp.zeros_like(w), w)
        store(i, j, w)


def edge_scratch(wide, rows, members):
    return [pltpu.VMEM((wide, 4, rows, members), BF16), pltpu.VMEM((wide, 4, members), F32)]


def near_edge(wide_q, wide_side, got_a):
    wide, tile_lon, rows, members = wide_q.shape

    def kernel(q_ref, side_ref, a_ref, out_ref, edge_ref, edge_side_ref):
        def store(i, j, w):
            out_ref[i, j] = w

        edge = 1 - lax.rem(lax.axis_index("lon"), 2)
        edge_weights(q_ref, side_ref, a_ref, edge, edge_ref, edge_side_ref, store)

    vmem = pl.BlockSpec(memory_space=pltpu.VMEM)
    return pl.pallas_call(
        kernel,
        in_specs=[vmem] * 3,
        out_specs=vmem,
        out_shape=jax.ShapeDtypeStruct((wide - 2, 2, members, members), BF16),
        scratch_shapes=edge_scratch(wide, rows, members),
        compiler_params=PARAMS,
        cost_estimate=pl.CostEstimate(flops=5 * 10**9, bytes_accessed=3 * 10**6, transcendentals=0),
        name="near_edge",
    )(wide_q, wide_side, got_a)


def finish(state, wide_q, wide_side, got_b, inner_w, lat_a_w, lat_b_w, near_w, columns):
    tile_lat, tile_lon, rows, members = state.shape
    wide = tile_lat + 4

    def kernel(
        state_ref, q_ref, side_ref, b_ref, inner_ref, lat_a_ref, lat_b_ref, near_ref, columns_ref,
        out_hbm, edge_ref, edge_side_ref, w_ref, perturb_ref, out_ref, sems,
    ):
        edge = lax.rem(lax.axis_index("lon"), 2)

        def store(i, j, w):
            w_ref[i, edge * tile_lon + j] = w

        edge_weights(q_ref, side_ref, b_ref, edge, edge_ref, edge_side_ref, store)
        for i in range(tile_lat - 2):
            w_ref[2 + i, 2:tile_lon] = inner_ref[i]
        odd = lax.rem(lax.axis_index("lat"), 2)
        for ref, south in ((lat_a_ref, 1 - odd), (lat_b_ref, odd)):
            w_ref[south * (tile_lat + 1), 2:tile_lon] = ref[0]
            w_ref[1 + south * (tile_lat - 1), 2:tile_lon] = ref[1]
        for i in range(tile_lat + 2):
            for j in range(2):
                w_ref[i, (1 - edge) * tile_lon + j] = near_ref[i, j]

        def analyse(i, carry):
            totals = []
            for j in range(tile_lon):
                x = state_ref[i, j].astype(F32)
                mean = jnp.sum(x, axis=1, keepdims=True) * (1.0 / members)
                centred = x - mean
                perturb_ref[j * rows : (j + 1) * rows, :] = centred.astype(BF16)
                totals.append(x - columns_ref[i, 4, j * rows : (j + 1) * rows, :] * centred)
            for n in range(tile_lon + 2):
                low, high = max(n - 2, 0), min(n, tile_lon - 1)
                near = jnp.concatenate([w_ref[i + a, n] for a in range(3)], axis=0)
                out = lax.dot_general(
                    perturb_ref[low * rows : (high + 1) * rows, :],
                    near,
                    (((1,), (1,)), ((), ())),
                    preferred_element_type=F32,
                )
                for j in range(low, high + 1):
                    here = out[(j - low) * rows : (j - low + 1) * rows]
                    span = slice(j * rows, (j + 1) * rows)
                    first, third = columns_ref[i, 0, span, :], columns_ref[i, 1, span, :]
                    along = (first, columns_ref[i, 4, span, :] - first - third, third)
                    mixed = 0.0
                    for a in range(3):
                        mixed = mixed + along[a] * here[:, a * members : (a + 1) * members]
                    if n - j == 1:
                        across = 1.0 - columns_ref[i, 2, span, :] - columns_ref[i, 3, span, :]
                    else:
                        across = columns_ref[i, 2 + (n - j) // 2, span, :]
                    totals[j] = totals[j] + across * mixed
                    if n == j + 2:
                        out_ref[i, j] = totals[j].astype(BF16)
            pltpu.make_async_copy(out_ref.at[i], out_hbm.at[i], sems.at[i]).start()
            return carry

        lax.fori_loop(0, tile_lat, analyse, 0, unroll=True)
        for i in range(tile_lat):
            pltpu.make_async_copy(out_ref.at[i], out_hbm.at[i], sems.at[i]).wait()

    vmem = pl.BlockSpec(memory_space=pltpu.VMEM)
    return pl.pallas_call(
        kernel,
        in_specs=[vmem] * 9,
        out_specs=pl.BlockSpec(memory_space=pltpu.HBM),
        out_shape=jax.ShapeDtypeStruct(state.shape, BF16),
        scratch_shapes=edge_scratch(wide, rows, members)
        + [
            pltpu.VMEM((tile_lat + 2, tile_lon + 2, members, members), BF16),
            pltpu.VMEM((tile_lon * rows, members), BF16),
            pltpu.VMEM(state.shape, BF16),
            pltpu.SemaphoreType.DMA((tile_lat,)),
        ],
        compiler_params=PARAMS,
        cost_estimate=pl.CostEstimate(flops=10**10, bytes_accessed=3 * 10**6, transcendentals=0),
        name="finish",
    )(state, wide_q, wide_side, got_b, inner_w, lat_a_w, lat_b_w, near_w, columns)


def body(state, obs_row, obs_count, obs_value, obs_weight, quadrant, frac_lat, frac_lon, land):
    send_a, side_a = prepare(state, obs_row, obs_count, obs_value, obs_weight)
    got_a = swap(send_a, "lat", 0)
    send_b, q, side, columns, own_grams = complete(
        state, obs_row, obs_count, obs_value, obs_weight, send_a, side_a, quadrant, frac_lat, frac_lon, land
    )
    got_b = swap_inner_lat(send_b)
    inner_w = interior(side, own_grams)
    lat_a_w = lat_edge(0, side, own_grams, got_a)
    wide_q, wide_side, to_a, to_b = widen(q, side, got_a, got_b, lat_a_w)
    lon_b = swap(to_b, "lon", 1)
    lon_a = swap(to_a, "lon", 0)
    lat_b_w = lat_edge(1, side, own_grams, got_b)
    near_w = near_edge(wide_q, wide_side, lon_a)
    return finish(state, wide_q, wide_side, lon_b, inner_w, lat_a_w, lat_b_w, near_w, columns)


def solution(mesh):
    cell = P("lat", "lon", None)
    return jax.shard_map(
        body,
        mesh=mesh,
        in_specs=(
            P("lat", "lon", None, None), cell, P("lat", "lon"), cell, cell, cell, cell, cell, cell,
        ),
        out_specs=P("lat", "lon", None, None),
        check_vma=False,
    )
```
